32 devices in a mesh: groups: 2 (over x), seq: 16 (over z, y, core).
Axes of the slice: x: 2, y: 2, z: 4, core: 2. Of those that a mesh axis runs over, the one named last changes fastest.
Arguments:
- patches: bfloat16 [4096, 1176], P(('groups', 'seq')), parts along dimension 0, may hold values from -6 to 6
- row_owner: int32 [4096, 1], P(('groups', 'seq')), parts along dimension 0, may hold values from 0 to 15; in each aligned block of 128 rows (0 to 127, 128 to 255, ...) at most 16 rows name the same one
- window_slot: int32 [4096], P(('groups', 'seq')), parts along dimension 0, may hold values from 0 to 3
- w_patch: bfloat16 [1176, 1280], replicated, may hold values from -1 to 1
- vit_gain: float32 [1280], replicated, may hold values from 0.1 to 1.9
- w_qkv: bfloat16 [1280, 1920], replicated, may hold values from -1 to 1
- queries: bfloat16 [4096, 4096], P(('groups', 'seq')), parts along dimension 0, may hold values from -36 to 36
- new_kv: bfloat16 [4096, 1024], P(('groups', 'seq')), parts along dimension 0, may hold values from -6 to 6
- kv_cache: bfloat16 [2048, 16, 1024], P(('groups', 'seq')), parts along dimension 0, may hold values from -6 to 6
- block_table: int32 [32, 64], P(('groups', 'seq')), parts along dimension 0, may hold values from -1 to 1023, as said below
Outputs:
- vision_out: bfloat16 [4096, 640], P(('groups', 'seq')), parts along dimension 0
- attention_out: bfloat16 [4096, 4096], P(('groups', 'seq')), parts along dimension 0
The draws below stay inside these ranges and needn't reach their ends.
There are 2 independent parts, one for each index of `groups`. The reference program is written for one: setup_inputs(seed, part) draws one part's arguments, and reference() takes and returns one part's arrays. A program takes and returns all parts, laid end to end along the dimension named above; an argument that names none is the same for every part. Nothing has to cross between parts.
Inputs may be any that keep to these rules, and one draw needn't show every extreme that they name: `row_owner`: in the rows of one device, each owner is named by at most 16 rows. `block_table`: block b is stored on device b // 64. Each row lists 8 or more distinct blocks, then -1 entries; at most 8 of a row's blocks lie on one device.
All inputs are finite; a program needn't handle non-finite values.
Results may differ from the reference program's by a relative error of at most 0.0093.
Values may be sent and summed in bfloat16 or wider, within the bound.
No kernel may reach another device: no remote copies, remote signals or barrier semaphores. Data moves between devices by JAX's collectives and lax.ppermute only.
A program may use at most 64 MiB of HBM per device.

```python
import math
import jax
import jax.numpy as jnp
import numpy as np
from jax import lax

SRC_ROWS = 128
ROWS = 2048
CAP = 16
PATCH = 1176
VIT = 1280
VHEADS = 8
VHD = 80
VQKV = 640
WSLOTS = 4
TOK_DEV = 128
TOKENS = 2048
QHEADS = 32
KVH = 4
HD = 128
BT = 16
BLK_DEV = 64
TMAX = 64
N_SEQ = 16


def table_law(key):
    table_key = jax.random.fold_in(key, 101)
    star_key, perm_key, offset_key, length_key, longest_key = jax.random.split(table_key, 5)
    per_owner = 2 * TMAX // N_SEQ
    star_owner = jax.random.randint(star_key, (), 0, N_SEQ)
    reader_keys = jax.random.split(perm_key, N_SEQ)
    rest_owner = jax.vmap(lambda sub_key: jax.random.permutation(sub_key, N_SEQ - 1))(reader_keys) + 1
    owner_order = jnp.concatenate([jnp.zeros((N_SEQ, 1), jnp.int32), rest_owner.astype(jnp.int32)], axis=1)
    owners_all = (star_owner + owner_order) % N_SEQ
    slot_index = jnp.arange(TMAX)
    owner_entry = owners_all[:, slot_index // per_owner]
    offsets = jax.random.randint(offset_key, (N_SEQ, N_SEQ), 0, BLK_DEV)
    local_index = (jnp.take_along_axis(offsets, owner_entry, axis=1) + slot_index[None, :] % per_owner) % BLK_DEV
    lengths = jax.random.randint(length_key, (N_SEQ,), per_owner, TMAX + 1)
    longest = jax.random.randint(longest_key, (), 0, N_SEQ)
    lengths = jnp.where(jnp.arange(N_SEQ) == longest, TMAX, lengths)
    entries = owner_entry * BLK_DEV + local_index
    return jnp.where(slot_index[None, :] < lengths[:, None], entries, -1).astype(jnp.int32)


def cache_law(key):
    cache_key = jax.random.fold_in(key, 202)
    array_shape = (N_SEQ * BLK_DEV, BT, 2 * KVH * HD)
    values = jnp.clip(jax.random.normal(cache_key, array_shape, jnp.float32), -6.0, 6.0)
    return values


def draw_block_table(key, part):
    return table_law(key)


def draw_kv_cache(key, part):
    return cache_law(key).astype(jnp.bfloat16)


def draw_queries(key, part):
    query_key = jax.random.fold_in(key, 303)
    array_shape = (N_SEQ * TOK_DEV, QHEADS * HD)
    values = jnp.clip(jax.random.normal(query_key, array_shape, jnp.float32), -6.0, 6.0)
    return values.astype(jnp.bfloat16)


def draw_patches(key, part):
    patch_key = jax.random.fold_in(key, 707)
    row_count = N_SEQ * SRC_ROWS
    array_shape = (row_count, PATCH)
    values = jnp.clip(jax.random.normal(patch_key, array_shape, jnp.float32), -6.0, 6.0)
    return values.astype(jnp.bfloat16)


def draw_w_patch(key, part):
    weight_key = jax.random.fold_in(key, 505)
    array_shape = (PATCH, VIT)
    values = jnp.clip(jax.random.normal(weight_key, array_shape, jnp.float32), -6.0, 6.0) * PATCH ** (-0.5)
    return values.astype(jnp.bfloat16)


def draw_w_qkv(key, part):
    weight_key = jax.random.fold_in(key, 606)
    inner_width = VHEADS * VHD
    array_shape = (VIT, 3 * inner_width)
    values = jnp.clip(jax.random.normal(weight_key, array_shape, jnp.float32), -6.0, 6.0) * VIT ** (-0.5)
    return values.astype(jnp.bfloat16)


def place_ends(values, stream_key, low, top_value):
    longest = values.shape.index(max(values.shape))
    spots = []
    for shift in (0, 1):
        where = [jax.random.randint(jax.random.fold_in(stream_key, axis), (), 0, length) for axis, length in enumerate(values.shape)]
        where[longest] = (where[longest] + shift) % values.shape[longest]
        spots.append(tuple(where))
    return values.at[spots[0]].set(low).at[spots[1]].set(top_value)


def steps_of(rng, dims, shards, low, top_value):
    def one(position, parts):
        draws = jax.random.uniform(jax.random.fold_in(jax.random.fold_in(rng, 6), position), (parts,), jnp.float32, low / len(shards), top_value / len(shards))
        return jnp.repeat(jnp.exp(draws), dims[position] // parts).reshape((-1,) + (1,) * (len(dims) - position - 1))

    loudness = one(*shards[0])
    for cut in shards[1:]:
        loudness = loudness * one(*cut)
    return loudness


def assign_block(rng, own, number, rows, amount, top, limit, slope):
    ranking = jax.random.permutation(rng, amount)
    crowded, usual = portions_of(amount, rows * top, limit, slope, True), portions_of(amount, rows * top, limit, slope, False)
    places = jnp.arange(amount)

    def named(sizes, rotation):
        used = int((sizes > 0).sum())
        fixed = max(1, used // 4)
        passed = fixed + (places - fixed + rotation * (used - fixed)) % max(1, amount - fixed)
        return jnp.zeros((amount,), jnp.int32).at[ranking[jnp.where(places < fixed, places, passed)]].set(jnp.asarray(sizes, jnp.int32))

    sizes = jnp.where(number % 4 == 0, named(crowded, number // 4), named(usual, number - number // 4 - 1))
    mixed = jax.random.permutation(jax.random.fold_in(own, 3), amount)
    giver, receiver = mixed[0:amount // 2 * 2:2], mixed[1:amount // 2 * 2:2]
    room = jnp.minimum(sizes[giver] - 1, limit - sizes[receiver]) // 2
    room = jnp.where((giver == ranking[0]) | (receiver == ranking[0]) | (sizes[receiver] == 0), 0, jnp.maximum(room, 0))
    passed = jax.random.randint(jax.random.fold_in(own, 4), (amount // 2,), 0, 1 << 20) % (room + 1)
    sizes = sizes.at[giver].add(-passed).at[receiver].add(passed)
    labels = jnp.searchsorted(jnp.cumsum(sizes), jnp.arange(rows * top), side="right").astype(jnp.int32)
    table = labels.reshape(top, rows).T
    table = table[jax.random.permutation(jax.random.fold_in(own, 1), rows)]
    rotation = jax.random.randint(jax.random.fold_in(own, 2), (rows, 1), 0, top)
    return jnp.take_along_axis(table, (jnp.arange(top)[None, :] + rotation) % top, axis=1)


def portions_of(count, total, reach, skew, full):
    portions = [(1 << 20) // math.isqrt(standing ** skew) + 1 for standing in range(1, count + 1)]
    largest = reach if full else min(reach, max(-(-total // count), total * portions[0] // sum(portions)))
    least = 1 if total - largest >= count - 1 else 0
    counts, surplus = [largest] + [least] * (count - 1), total - largest - least * (count - 1)
    while surplus > 0:
        movable = [i for i in range(1, count) if counts[i] < largest] or [i for i in range(1, count) if counts[i] < reach]
        whole, remaining = sum([portions[i] for i in movable]), surplus
        for i in movable:
            extra = min(reach - counts[i], max(1, remaining * portions[i] // whole), surplus)
            counts[i] = counts[i] + extra
            surplus = surplus - extra
    return np.array(counts)


def bell_draw(stream_key, shape, deviation, reach, cuts=(), kind=jnp.bfloat16):
    values = deviation * jax.random.normal(stream_key, shape, jnp.float32)
    if cuts:
        values = values * steps_of(stream_key, shape, cuts, -0.22, 0.18)
    return jnp.clip(values, -reach, reach).astype(kind)


def setup_inputs(seed: int = 0, part: int = 0) -> dict:
    keys = jax.random.split(jax.random.key(seed), 11)
    own_keys = jax.random.split(jax.random.fold_in(keys[10], part), 11)
    patches = draw_patches(jax.random.fold_in(jax.random.fold_in(keys[10], part), 71), part)
    row_owner_keys = jax.random.split(jax.random.fold_in(own_keys[1], 1), ROWS // SRC_ROWS)
    row_owner_turns = jax.random.permutation(jax.random.fold_in(own_keys[1], 3), ROWS // SRC_ROWS)
    row_owner = jax.vmap(lambda own, number: assign_block(jax.random.fold_in(own_keys[1], 2), own, number, SRC_ROWS, N_SEQ, 1, CAP, 2))(row_owner_keys, row_owner_turns).reshape((ROWS, 1))
    window_slot = place_ends(jax.random.randint(own_keys[2], (ROWS,), 0, WSLOTS), jax.random.fold_in(own_keys[2], 1), 0, WSLOTS - 1).astype(jnp.int32)
    w_patch = draw_w_patch(jax.random.fold_in(keys[10], 71), part)
    vit_gain = jnp.clip(1.0 + 0.18 * jax.random.normal(keys[4], (VIT,), jnp.float32), 0.1, 1.9)
    w_qkv = draw_w_qkv(jax.random.fold_in(keys[10], 71), part)
    queries = draw_queries(jax.random.fold_in(jax.random.fold_in(keys[10], part), 71), part)
    new_kv = bell_draw(own_keys[7], (TOKENS, 2 * KVH * HD), 1.0, 6.0, ((0, 16),))
    kv_cache = draw_kv_cache(jax.random.fold_in(jax.random.fold_in(keys[10], part), 71), part)
    block_table = draw_block_table(jax.random.fold_in(jax.random.fold_in(keys[10], part), 71), part)
    return dict(patches=patches, row_owner=row_owner, window_slot=window_slot, w_patch=w_patch, vit_gain=vit_gain, w_qkv=w_qkv, queries=queries, new_kv=new_kv, kv_cache=kv_cache, block_table=block_table)


def embed_rows(patch_rows, w_patch, vit_gain):
    embedded = jnp.dot(patch_rows, w_patch, preferred_element_type=jnp.float32).astype(jnp.bfloat16)
    widened = lax.optimization_barrier(embedded).astype(jnp.float32)
    factor = lax.rsqrt(lax.optimization_barrier(jnp.mean(widened * widened, axis=1, keepdims=True)) + 1e-06)
    return (widened * factor * vit_gain).astype(jnp.bfloat16)

def window_attention(qkv_rows, windows):
    total_rows = qkv_rows.shape[0]
    inner_width = VHEADS * VHD
    query_heads = qkv_rows[:, :inner_width].reshape(total_rows, VHEADS, VHD).astype(jnp.float32)
    key_heads = qkv_rows[:, inner_width:2 * inner_width].reshape(total_rows, VHEADS, VHD).astype(jnp.float32)
    value_heads = qkv_rows[:, 2 * inner_width:].reshape(total_rows, VHEADS, VHD).astype(jnp.float32)
    is_live = windows >= 0
    scores = jnp.einsum('qhd,khd->hqk', query_heads, key_heads) * VHD ** (-0.5)
    row_index = jnp.arange(total_rows)
    allowed = (windows[:, None] == windows[None, :]) & is_live[None, :] | (row_index[:, None] == row_index[None, :])
    scores = jnp.where(allowed[None], scores, -jnp.inf)
    highest = lax.optimization_barrier(jnp.max(scores, axis=2, keepdims=True))
    weights = jnp.exp(scores - highest)
    totals = lax.optimization_barrier(jnp.sum(weights, axis=2))
    rounded = lax.optimization_barrier(weights.astype(jnp.bfloat16)).astype(jnp.float32)
    blended = jnp.einsum('hqk,khd->qhd', rounded, value_heads)
    return (blended / totals.T[:, :, None]).reshape(total_rows, inner_width).astype(jnp.bfloat16)

def prompt_attention(query_rows, fresh_kv, cached_kv, cached_live):
    token_count = query_rows.shape[0]
    kv_width = KVH * HD
    group_size = QHEADS // KVH
    every_kv = jnp.concatenate([cached_kv, fresh_kv], axis=0).astype(jnp.float32)
    causal = jnp.arange(token_count)[None, :] <= jnp.arange(token_count)[:, None]
    allowed = jnp.concatenate([jnp.broadcast_to(cached_live[None, :], (token_count, cached_live.shape[0])), causal], axis=1)
    outputs = []
    for head_group in range(KVH):
        query_heads = query_rows[:, head_group * group_size * HD:(head_group + 1) * group_size * HD]
        query_heads = query_heads.reshape(token_count, group_size, HD).astype(jnp.float32)
        key_head = every_kv[:, head_group * HD:(head_group + 1) * HD]
        value_head = every_kv[:, kv_width + head_group * HD:kv_width + (head_group + 1) * HD]
        scores = jnp.einsum('cpd,kd->cpk', query_heads, key_head) * HD ** (-0.5)
        scores = jnp.where(allowed[:, None, :], scores, -jnp.inf)
        highest = lax.optimization_barrier(jnp.max(scores, axis=2, keepdims=True))
        weights = jnp.exp(scores - highest)
        totals = lax.optimization_barrier(jnp.sum(weights, axis=2))
        rounded = lax.optimization_barrier(weights.astype(jnp.bfloat16)).astype(jnp.float32)
        blended = jnp.einsum('cpk,kd->cpd', rounded, value_head)
        outputs.append((blended / totals[:, :, None]).reshape(token_count, group_size * HD))
    return jnp.concatenate(outputs, axis=1).astype(jnp.bfloat16)

def reference(patches, row_owner, window_slot, w_patch, vit_gain, w_qkv, queries, new_kv, kv_cache, block_table):
    normed = embed_rows(patches, w_patch, vit_gain)
    qkv_all = jnp.dot(normed, w_qkv, preferred_element_type=jnp.float32).astype(jnp.bfloat16)
    owner_ids = row_owner[:, 0]
    slot_count = 2 * SRC_ROWS

    def per_owner(owner):
        picked = jnp.nonzero(owner_ids == owner, size=slot_count, fill_value=ROWS)[0].astype(jnp.int32)
        is_live = picked < ROWS
        safe_rows = jnp.minimum(picked, ROWS - 1)
        windows = jnp.where(is_live, window_slot[safe_rows], -1)
        return (window_attention(qkv_all[safe_rows], windows), picked)
    attended, picked_rows = lax.map(per_owner, jnp.arange(N_SEQ, dtype=jnp.int32))
    vision_out = jnp.zeros((ROWS, VQKV), jnp.bfloat16).at[picked_rows.reshape(-1)].set(attended.reshape(-1, VQKV), mode='drop')

    def per_reader(reader):
        table_row = block_table[reader]
        is_live = table_row >= 0
        blocks = kv_cache[jnp.maximum(table_row, 0)]
        cached_kv = blocks.reshape(TMAX * BT, 2 * KVH * HD)
        cached_live = jnp.repeat(is_live, BT)
        first_row = (reader * TOK_DEV).astype(jnp.int32)
        query_rows = lax.dynamic_slice_in_dim(queries, first_row, TOK_DEV, 0)
        fresh_kv = lax.dynamic_slice_in_dim(new_kv, first_row, TOK_DEV, 0)
        return prompt_attention(query_rows, fresh_kv, cached_kv, cached_live)
    attention_out = lax.map(per_reader, jnp.arange(N_SEQ, dtype=jnp.int32)).reshape(TOKENS, QHEADS * HD)
    return (vision_out, attention_out)
```

```python
import functools

import jax
import jax.numpy as jnp
from jax import lax
from jax.experimental import pallas as pl
from jax.experimental.pallas import tpu as pltpu
from jax.sharding import PartitionSpec as P

VHEADS = 8
VHD = 80
QHEADS = 32
KVH = 4
HD = 128
LANES = 128
CHUNK_BLOCKS = 16
HEADS_TILE = 4
LOG2E = 1.4426950408889634
HIDDEN = -1e30
VMEM_BYTES = 48 * 1024 * 1024


def iota(shape, axis):
    return lax.broadcasted_iota(jnp.int32, shape, axis)


def count(hits, axis):
    return jnp.sum(hits.astype(jnp.float32), axis=axis, keepdims=True).astype(jnp.int32)


def as_row(column):
    size = column.shape[0]
    diagonal = iota((size, size), 0) == iota((size, size), 1)
    return jnp.sum(jnp.where(diagonal, column, 0).astype(jnp.float32), axis=0, keepdims=True).astype(jnp.int32)


def as_column(row):
    size = row.shape[1]
    diagonal = iota((size, size), 0) == iota((size, size), 1)
    return jnp.sum(jnp.where(diagonal, row, 0).astype(jnp.float32), axis=1, keepdims=True).astype(jnp.int32)


def embed_kernel(
    capacity,
    per_owner,
    blocks_dev,
    patches_ref,
    w_ref,
    gain_ref,
    owner_ref,
    window_ref,
    table_ref,
    payload_ref,
    target_ref,
    request_ref,
    live_ref,
    embedded_ref,
):
    step = pl.program_id(0)
    width = w_ref.shape[1]
    piece = jnp.dot(patches_ref[...], w_ref[...], preferred_element_type=jnp.float32)
    embedded_ref[:, pl.ds(pl.multiple_of(step * width, width), width)] = piece.astype(jnp.bfloat16)

    @pl.when(step == pl.num_programs(0) - 1)
    def _():
        slots = payload_ref.shape[0]
        vit = embedded_ref.shape[1]
        rows = owner_ref.shape[0]
        owner_column = owner_ref[...]
        owner_row = as_row(owner_column)
        same = owner_column == owner_row
        first, second = iota((rows, rows), 0), iota((rows, rows), 1)
        rank_row = count(same & (first < second), 0)
        rank_column = count(same & (second < first), 1)
        target_ref[...] = owner_column * capacity + rank_column
        placed = (owner_row * capacity + rank_row) == iota((slots, rows), 0)
        windows = jnp.sum(
            jnp.where(placed, window_ref[...] + 1, 0).astype(jnp.float32), axis=1, keepdims=True
        )

        table_row = table_ref[...]
        entries = table_row.shape[1]
        live_row = table_row >= 0
        holder_row = jnp.where(live_row, table_row // blocks_dev, -1)
        local_row = jnp.where(live_row, table_row % blocks_dev, 0)
        holder_column = as_column(holder_row)
        before = iota((entries, entries), 0) < iota((entries, entries), 1)
        holder_rank = count((holder_column == holder_row) & before, 0)
        request_row = jnp.where(live_row, holder_row * per_owner + holder_rank, -1)
        first_request = jnp.sum(
            jnp.where(iota((1, entries), 1) == 0, request_row, 0).astype(jnp.float32),
            axis=1,
            keepdims=True,
        ).astype(jnp.int32)
        request_ref[...] = jnp.where(live_row, request_row, first_request)
        live_ref[...] = count(live_row, 1)
        placed_row = jnp.where(
            live_row, holder_row * capacity + holder_rank, -1
        )
        asked = jnp.sum(
            jnp.where(placed_row == iota((slots, entries), 0), local_row + 1, 0).astype(jnp.float32),
            axis=1,
            keepdims=True,
        )
        lane = iota((slots, LANES), 1)
        notes = jnp.where(lane == 0, windows - 1.0, jnp.where(lane == 1, asked - 1.0, 0.0))
        payload_ref[:, vit:] = notes.astype(jnp.bfloat16)

        widened = embedded_ref[...].astype(jnp.float32)
        factor = lax.rsqrt(jnp.mean(widened * widened, axis=1, keepdims=True) + 1e-06)
        normed = (widened * factor * gain_ref[...]).astype(jnp.bfloat16)
        payload_ref[:, :vit] = jnp.dot(
            placed.astype(jnp.bfloat16), normed, preferred_element_type=jnp.float32
        ).astype(jnp.bfloat16)


def embed_and_route(patches, w_patch, vit_gain, row_owner, window_slot, block_table, capacity, slots, per_owner, blocks_dev):
    rows, patch = patches.shape
    vit = w_patch.shape[1]
    entries = block_table.shape[1]
    width = 2 * LANES
    whole = lambda *shape: pl.BlockSpec(shape, lambda step: (0,) * len(shape))
    return pl.pallas_call(
        functools.partial(embed_kernel, capacity, per_owner, blocks_dev),
        grid=(vit // width,),
        out_shape=(
            jax.ShapeDtypeStruct((slots, vit + LANES), jnp.bfloat16),
            jax.ShapeDtypeStruct((rows, 1), jnp.int32),
            jax.ShapeDtypeStruct((1, entries), jnp.int32),
            jax.ShapeDtypeStruct((1, 1), jnp.int32),
        ),
        in_specs=[
            whole(rows, patch),
            pl.BlockSpec((patch, width), lambda step: (0, step)),
            whole(1, vit),
            whole(rows, 1),
            whole(1, rows),
            whole(1, entries),
        ],
        out_specs=(whole(slots, vit + LANES), whole(rows, 1), whole(1, entries), whole(1, 1)),
        scratch_shapes=[pltpu.VMEM((rows, vit), jnp.bfloat16)],
        compiler_params=pltpu.CompilerParams(vmem_limit_bytes=VMEM_BYTES),
        cost_estimate=pl.CostEstimate(
            flops=2 * rows * patch * vit + 2 * slots * rows * vit,
            bytes_accessed=2 * patch * vit + 2 * rows * patch + 2 * slots * vit,
            transcendentals=rows,
        ),
        name="embed_and_route",
    )(patches, w_patch, vit_gain.reshape(1, vit), row_owner, window_slot.reshape(1, rows), block_table)


def prompt_kernel(
    request_ref, live_ref, query_ref, fresh_ref, blocks_ref, out_ref, kv_ref, top_ref, sum_ref, sems
):
    tokens = query_ref.shape[0]
    block_tokens = kv_ref.shape[1]
    kv_width = KVH * HD
    group_size = QHEADS // KVH
    chunk_keys = CHUNK_BLOCKS * block_tokens
    tile_rows = HEADS_TILE * tokens
    live_blocks = live_ref[0, 0]
    chunks = (live_blocks + (CHUNK_BLOCKS - 1)) // CHUNK_BLOCKS

    def fetch(chunk, carry):
        def one(place, inner):
            entry = chunk * CHUNK_BLOCKS + place
            pltpu.make_async_copy(
                blocks_ref.at[request_ref[0, entry]], kv_ref.at[entry], sems.at[chunk]
            ).start()
            return inner

        return lax.fori_loop(0, CHUNK_BLOCKS, one, carry)

    lax.fori_loop(0, chunks, fetch, 0)

    def tiles():
        for group in range(KVH):
            for part in range(group_size // HEADS_TILE):
                yield group, part, group * group_size + part * HEADS_TILE

    def tile_queries(head):
        return jnp.concatenate(
            [query_ref[:, (head + i) * HD : (head + i + 1) * HD] for i in range(HEADS_TILE)], axis=0
        )

    def scores_of(head, keys):
        return lax.dot_general(
            tile_queries(head), keys, (((1,), (1,)), ((), ())), preferred_element_type=jnp.float32
        ) * (HD ** (-0.5) * LOG2E)

    def with_ones(values):
        return jnp.concatenate([values, jnp.ones_like(values)], axis=1)

    causal = iota((tokens, tokens), 1) <= iota((tokens, tokens), 0)
    causal = jnp.concatenate([causal.astype(jnp.int32)] * HEADS_TILE, axis=0) > 0
    for group, part, head in tiles():
        row = head * tokens
        keys = fresh_ref[:, group * HD : (group + 1) * HD]
        values = fresh_ref[:, kv_width + group * HD : kv_width + (group + 1) * HD]
        scores = jnp.where(causal, scores_of(head, keys), HIDDEN)
        top = jnp.max(scores, axis=1, keepdims=True)
        weights = jnp.exp2(scores - top).astype(jnp.bfloat16)
        top_ref[row : row + tile_rows, :] = jnp.broadcast_to(top, (tile_rows, HD))
        sum_ref[row : row + tile_rows, :] = jnp.dot(
            weights, with_ones(values), preferred_element_type=jnp.float32
        )

    def visit(chunk, carry):
        first = chunk * CHUNK_BLOCKS
        pltpu.make_async_copy(
            blocks_ref.at[pl.ds(0, CHUNK_BLOCKS)], kv_ref.at[pl.ds(first, CHUNK_BLOCKS)], sems.at[chunk]
        ).wait()
        shown = iota((1, chunk_keys), 1) < (live_blocks - first) * block_tokens
        for group, part, head in tiles():
            row = head * tokens
            keys = kv_ref[pl.ds(first, CHUNK_BLOCKS), :, group * HD : (group + 1) * HD]
            values = kv_ref[
                pl.ds(first, CHUNK_BLOCKS), :, kv_width + group * HD : kv_width + (group + 1) * HD
            ]
            keys = keys.reshape(chunk_keys, HD)
            values = values.reshape(chunk_keys, HD)
            scores = jnp.where(shown, scores_of(head, keys), HIDDEN)
            old_top = top_ref[row : row + tile_rows, :]
            top = jnp.maximum(old_top, jnp.max(scores, axis=1, keepdims=True))
            shrink = jnp.exp2(old_top - top)
            weights = jnp.exp2(scores - jnp.concatenate([top] * (chunk_keys // HD), axis=1))
            top_ref[row : row + tile_rows, :] = top
            sum_ref[row : row + tile_rows, :] = sum_ref[row : row + tile_rows, :] * jnp.concatenate(
                [shrink, shrink], axis=1
            ) + jnp.dot(
                weights.astype(jnp.bfloat16), with_ones(values), preferred_element_type=jnp.float32
            )
        return carry

    lax.fori_loop(0, chunks, visit, 0)

    for head in range(QHEADS):
        blended = sum_ref[head * tokens : (head + 1) * tokens, :]
        out_ref[:, head * HD : (head + 1) * HD] = (blended[:, :HD] / blended[:, HD:]).astype(jnp.bfloat16)


def prompt_attention(request, live, queries, new_kv, blocks):
    tokens, width = queries.shape
    entries = request.shape[1]
    block_tokens = blocks.shape[1]
    chunks = -(-entries // CHUNK_BLOCKS)
    keys = entries * block_tokens + tokens
    whole = lambda *shape: pl.BlockSpec(shape, lambda *_: (0,) * len(shape))
    return pl.pallas_call(
        prompt_kernel,
        out_shape=jax.ShapeDtypeStruct((tokens, width), jnp.bfloat16),
        grid_spec=pltpu.PrefetchScalarGridSpec(
            num_scalar_prefetch=2,
            grid=(1,),
            in_specs=[
                whole(tokens, width),
                whole(tokens, new_kv.shape[1]),
                pl.BlockSpec(memory_space=pl.ANY),
            ],
            out_specs=whole(tokens, width),
            scratch_shapes=[
                pltpu.VMEM((chunks * CHUNK_BLOCKS, block_tokens, new_kv.shape[1]), jnp.bfloat16),
                pltpu.VMEM((QHEADS * tokens, HD), jnp.float32),
                pltpu.VMEM((QHEADS * tokens, 2 * HD), jnp.float32),
                pltpu.SemaphoreType.DMA((chunks,)),
            ],
        ),
        compiler_params=pltpu.CompilerParams(vmem_limit_bytes=VMEM_BYTES),
        cost_estimate=pl.CostEstimate(
            flops=4 * tokens * keys * width,
            bytes_accessed=4 * tokens * width + 2 * keys * new_kv.shape[1],
            transcendentals=tokens * QHEADS * keys,
        ),
        name="prompt_attention",
    )(request, live, queries, new_kv, blocks)


def pick_kernel(target_ref, returned_ref, out_ref):
    rows, slots = target_ref.shape[0], returned_ref.shape[0]
    picked = (target_ref[...] == iota((rows, slots), 1)).astype(jnp.bfloat16)
    out_ref[...] = jnp.dot(
        picked, returned_ref[...], preferred_element_type=jnp.float32
    ).astype(jnp.bfloat16)


def pick_rows(target, returned):
    return pl.pallas_call(
        pick_kernel,
        out_shape=jax.ShapeDtypeStruct((target.shape[0], returned.shape[1]), jnp.bfloat16),
        compiler_params=pltpu.CompilerParams(vmem_limit_bytes=VMEM_BYTES),
        name="pick_rows",
    )(target, returned)


def window_attention(qkv_rows, windows):
    total_rows = qkv_rows.shape[0]
    inner_width = VHEADS * VHD
    query_heads = qkv_rows[:, :inner_width].reshape(total_rows, VHEADS, VHD)
    key_heads = qkv_rows[:, inner_width : 2 * inner_width].reshape(total_rows, VHEADS, VHD)
    value_heads = qkv_rows[:, 2 * inner_width :].reshape(total_rows, VHEADS, VHD)
    is_live = windows >= 0
    every_row = jnp.arange(total_rows)
    scores = jnp.einsum(
        "qhd,khd->hqk", query_heads, key_heads, preferred_element_type=jnp.float32
    ) * VHD ** (-0.5)
    allowed = (windows[:, None] == windows[None, :]) & is_live[None, :] | (
        every_row[:, None] == every_row[None, :]
    )
    scores = jnp.where(allowed[None], scores, -jnp.inf)
    highest = jnp.max(scores, axis=2, keepdims=True)
    weights = jnp.exp(scores - highest)
    totals = jnp.sum(weights, axis=2)
    blended = jnp.einsum(
        "hqk,khd->qhd",
        weights.astype(jnp.bfloat16),
        value_heads,
        preferred_element_type=jnp.float32,
    )
    pieces = (blended / totals.T[:, :, None]).reshape(total_rows, inner_width)
    return pieces.astype(jnp.bfloat16)


def exchange(rows, devices):
    parts = rows.reshape((devices, rows.shape[0] // devices) + rows.shape[1:])
    return lax.all_to_all(parts, "seq", split_axis=0, concat_axis=0, tiled=True).reshape(rows.shape)


def shards(
    patches,
    row_owner,
    window_slot,
    w_patch,
    vit_gain,
    w_qkv,
    queries,
    new_kv,
    kv_cache,
    block_table,
):
    devices = lax.axis_size("seq")
    vit = w_patch.shape[1]
    capacity = 2 * patches.shape[0] // devices
    slots = devices * capacity
    per_owner = 2 * block_table.shape[1] // devices
    payload, target, request, live = embed_and_route(
        patches, w_patch, vit_gain, row_owner, window_slot, block_table,
        capacity, slots, per_owner, kv_cache.shape[0],
    )
    arrived = exchange(payload, devices)
    notes = arrived[:, vit : vit + 2].astype(jnp.int32)
    asked = notes[:, 1].reshape(devices, capacity)[:, :per_owner].reshape(devices * per_owner)
    fetched = kv_cache[jnp.maximum(asked, 0)]
    delivered = exchange(fetched, devices)
    qkv_rows = jnp.dot(arrived[:, :vit], w_qkv, preferred_element_type=jnp.float32).astype(jnp.bfloat16)
    attended = window_attention(qkv_rows, notes[:, 0])
    delivered, attended = lax.optimization_barrier((delivered, attended))
    returned = exchange(attended, devices)
    attention_out = prompt_attention(request, live, queries, new_kv, delivered)
    vision_out = pick_rows(target, returned)
    return (vision_out, attention_out)


def solution(mesh):
    in_specs = (
        P(("groups", "seq"), None),
        P(("groups", "seq"), None),
        P(("groups", "seq")),
        P(),
        P(),
        P(),
        P(("groups", "seq"), None),
        P(("groups", "seq"), None),
        P(("groups", "seq"), None, None),
        P(("groups", "seq"), None),
    )
    out_specs = (P(("groups", "seq"), None), P(("groups", "seq"), None))
    return jax.shard_map(shards, mesh=mesh, in_specs=in_specs, out_specs=out_specs, check_vma=False)
```

```python
import functools

import jax
import jax.numpy as jnp
from jax import lax
from jax.experimental import pallas as pl
from jax.experimental.pallas import tpu as pltpu
from jax.sharding import PartitionSpec as P

VHEADS = 8
VHD = 80
QHEADS = 32
KVH = 4
HD = 128
LANES = 128
CHUNK_BLOCKS = 16
HEADS_TILE = 4
LOG2E = 1.4426950408889634
HIDDEN = -1e30
VMEM_BYTES = 56 * 1024 * 1024
ROOM_STEP = 8


def iota(shape, axis):
    return lax.broadcasted_iota(jnp.int32, shape, axis)


def count(hits, axis):
    return jnp.sum(hits.astype(jnp.float32), axis=axis, keepdims=True).astype(jnp.int32)


def as_row(column):
    size = column.shape[0]
    diagonal = iota((size, size), 0) == iota((size, size), 1)
    return jnp.sum(jnp.where(diagonal, column, 0).astype(jnp.float32), axis=0, keepdims=True).astype(jnp.int32)


def as_column(row):
    size = row.shape[1]
    diagonal = iota((size, size), 0) == iota((size, size), 1)
    return jnp.sum(jnp.where(diagonal, row, 0).astype(jnp.float32), axis=1, keepdims=True).astype(jnp.int32)


def embed_kernel(
    capacity,
    per_owner,
    blocks_dev,
    lanes,
    patches_ref,
    w_ref,
    gain_ref,
    owner_ref,
    window_ref,
    table_ref,
    payload_ref,
    target_ref,
    request_ref,
    live_ref,
    embedded_ref,
):
    step = pl.program_id(0)
    width = w_ref.shape[1]
    piece = lax.dot_general(
        patches_ref[...], w_ref[...], (((0,), (0,)), ((), ())), preferred_element_type=jnp.float32
    )
    embedded_ref[:, pl.ds(pl.multiple_of(step * width, width), width)] = piece.astype(jnp.bfloat16)

    @pl.when(step == pl.num_programs(0) - 1)
    def _():
        slots = payload_ref.shape[0]
        vit = embedded_ref.shape[1]
        rows = owner_ref.shape[1]
        owner_row = owner_ref[...]
        owner_column = as_column(owner_row)
        same = owner_column == owner_row
        first, second = iota((rows, rows), 0), iota((rows, rows), 1)
        rank_row = count(same & (first < second), 0)
        rank_column = count(same & (second < first), 1)
        target_ref[...] = owner_column * capacity + rank_column
        placed = (owner_row * capacity + rank_row) == iota((slots, rows), 0)
        windows = (
            jnp.sum(jnp.where(placed, window_ref[...] + 1, 0).astype(jnp.float32), axis=1, keepdims=True)
            - 1.0
        )
        note_list(capacity, per_owner, blocks_dev, lanes, windows, table_ref, payload_ref.at[:, vit:], request_ref, live_ref)

        widened = embedded_ref[...].astype(jnp.float32)
        factor = lax.rsqrt(jnp.mean(widened * widened, axis=1, keepdims=True) + 1e-06)
        normed = (widened * factor * gain_ref[...]).astype(jnp.bfloat16)
        payload_ref[:, :vit] = jnp.dot(
            placed.astype(jnp.bfloat16), normed, preferred_element_type=jnp.float32
        ).astype(jnp.bfloat16)


def note_list(capacity, per_owner, blocks_dev, lanes, windows, table_ref, notes_ref, request_ref, live_ref):
    slots = notes_ref.shape[0]
    table_row = table_ref[...]
    entries = table_row.shape[1]
    live_row = table_row >= 0
    holder_row = jnp.where(live_row, table_row // blocks_dev, -1)
    local_row = jnp.where(live_row, table_row % blocks_dev, 0)
    lane = iota((slots, LANES), 1)
    before = iota((entries, entries), 0) < iota((entries, entries), 1)
    if lanes is None:
        holder_rank = count((as_column(holder_row) == holder_row) & before, 0)
        request_row = jnp.where(live_row, holder_row * per_owner + holder_rank, -1)
        first_request = jnp.sum(
            jnp.where(iota((1, entries), 1) == 0, request_row, 0).astype(jnp.float32), axis=1, keepdims=True
        ).astype(jnp.int32)
        request_ref[...] = jnp.where(live_row, request_row, first_request)
        live_ref[...] = jnp.broadcast_to(count(live_row, 1), live_ref.shape)
        placed_row = jnp.where(live_row, holder_row * capacity + holder_rank, -1)
        asked = jnp.sum(
            jnp.where(placed_row == iota((slots, entries), 0), local_row + 1, 0).astype(jnp.float32),
            axis=1,
            keepdims=True,
        )
        notes = jnp.where(lane == 0, windows, jnp.where(lane == 1, asked - 1.0, 0.0))
        notes_ref[...] = notes.astype(jnp.bfloat16)
        return
    regions = slots // capacity // lanes
    after = iota((entries, entries), 1) < iota((entries, entries), 0)
    region_row = jnp.where(live_row, holder_row // lanes, -1)
    region_column = as_column(region_row)
    region_rank = count((region_column == region_row) & after, 1)
    local_column, member_column = as_column(local_row), as_column(holder_row % lanes)
    place = iota((slots, LANES), 0)
    slot_row, slot_region = place % capacity, place // (capacity * lanes)
    pad = jnp.zeros((1, LANES - entries), jnp.float32)
    notes = jnp.where(lane == entries, windows, 0.0)
    most = jnp.zeros((1, 1), jnp.int32)
    live_ref[...] = jnp.zeros(live_ref.shape, jnp.int32)
    for region in range(regions):
        listed = (region_column == region) & (region_rank == iota((entries, entries), 1))
        pick = lambda column: jnp.sum(
            jnp.where(listed, column, 0).astype(jnp.float32), axis=0, keepdims=True
        )
        amount = count(region_row == region, 1)
        most = jnp.maximum(most, amount)
        live_ref[:, region : region + 1] = amount
        locals_row = jnp.concatenate([pick(local_column + 1) - 1.0, pad], axis=1)
        members_row = jnp.concatenate([pick(member_column), pad], axis=1)
        here = (slot_region == region) & (lane < entries)
        notes = jnp.where(here & (slot_row == 0), locals_row, notes)
        notes = jnp.where(here & (slot_row == 1), members_row, notes)
    notes = jnp.where((slot_row == 2) & (lane < entries), most.astype(jnp.float32), notes)
    notes_ref[...] = notes.astype(jnp.bfloat16)
    request_ref[...] = jnp.zeros(request_ref.shape, jnp.int32)


def embed_and_route(
    patches, w_patch, vit_gain, row_owner, window_slot, block_table, capacity, slots, per_owner, blocks_dev, lanes
):
    rows, patch = patches.shape
    vit = w_patch.shape[1]
    entries = block_table.shape[1]
    width = 2 * LANES
    whole = lambda *shape: pl.BlockSpec(shape, lambda step: (0,) * len(shape))
    return pl.pallas_call(
        functools.partial(embed_kernel, capacity, per_owner, blocks_dev, lanes),
        grid=(vit // width,),
        out_shape=(
            jax.ShapeDtypeStruct((slots, vit + LANES), jnp.bfloat16),
            jax.ShapeDtypeStruct((rows, 1), jnp.int32),
            jax.ShapeDtypeStruct((1, entries), jnp.int32),
            jax.ShapeDtypeStruct((1, LANES), jnp.int32),
        ),
        in_specs=[
            whole(patch, rows),
            pl.BlockSpec((patch, width), lambda step: (0, step)),
            whole(1, vit),
            whole(1, rows),
            whole(1, rows),
            whole(1, entries),
        ],
        out_specs=(whole(slots, vit + LANES), whole(rows, 1), whole(1, entries), whole(1, LANES)),
        scratch_shapes=[pltpu.VMEM((rows, vit), jnp.bfloat16)],
        compiler_params=pltpu.CompilerParams(vmem_limit_bytes=VMEM_BYTES),
        cost_estimate=pl.CostEstimate(
            flops=2 * rows * patch * vit + 2 * slots * rows * vit,
            bytes_accessed=2 * patch * vit + 2 * rows * patch + 2 * slots * vit,
            transcendentals=rows,
        ),
        name="embed_and_route",
    )(
        patches.T, w_patch, vit_gain.reshape(1, vit), row_owner.reshape(1, rows),
        window_slot.reshape(1, rows), block_table,
    )


def prompt_tiles():
    group_size = QHEADS // KVH
    for group in range(KVH):
        for part in range(group_size // HEADS_TILE):
            yield group, group * group_size + part * HEADS_TILE


def prompt_scores(query_ref, head, keys):
    rows = jnp.concatenate(
        [query_ref[:, (head + i) * HD : (head + i + 1) * HD] for i in range(HEADS_TILE)], axis=0
    )
    return lax.dot_general(
        rows, keys, (((1,), (1,)), ((), ())), preferred_element_type=jnp.float32
    ) * (HD ** (-0.5) * LOG2E)


def with_ones(values):
    return jnp.concatenate([values, jnp.ones_like(values)], axis=1)


def prompt_begin(query_ref, fresh_ref, top_ref, sum_ref):
    tokens = query_ref.shape[0]
    tile_rows = HEADS_TILE * tokens
    kv_width = KVH * HD
    causal = iota((tokens, tokens), 1) <= iota((tokens, tokens), 0)
    causal = jnp.concatenate([causal.astype(jnp.int32)] * HEADS_TILE, axis=0) > 0
    for group, head in prompt_tiles():
        row = head * tokens
        keys = fresh_ref[:, group * HD : (group + 1) * HD]
        values = fresh_ref[:, kv_width + group * HD : kv_width + (group + 1) * HD]
        scores = jnp.where(causal, prompt_scores(query_ref, head, keys), HIDDEN)
        top = jnp.max(scores, axis=1, keepdims=True)
        weights = jnp.exp2(scores - top).astype(jnp.bfloat16)
        top_ref[row : row + tile_rows, :] = jnp.broadcast_to(top, (tile_rows, HD))
        sum_ref[row : row + tile_rows, :] = jnp.dot(
            weights, with_ones(values), preferred_element_type=jnp.float32
        )


def prompt_add(query_ref, top_ref, sum_ref, keys_of, values_of, shown):
    tokens = query_ref.shape[0]
    tile_rows = HEADS_TILE * tokens
    chunk_keys = shown.shape[1]
    for group, head in prompt_tiles():
        row = head * tokens
        scores = jnp.where(shown, prompt_scores(query_ref, head, keys_of(group)), HIDDEN)
        old_top = top_ref[row : row + tile_rows, :]
        top = jnp.maximum(old_top, jnp.max(scores, axis=1, keepdims=True))
        shrink = jnp.exp2(old_top - top)
        weights = jnp.exp2(scores - jnp.concatenate([top] * (chunk_keys // HD), axis=1))
        top_ref[row : row + tile_rows, :] = top
        sum_ref[row : row + tile_rows, :] = sum_ref[row : row + tile_rows, :] * jnp.concatenate(
            [shrink, shrink], axis=1
        ) + jnp.dot(
            weights.astype(jnp.bfloat16), with_ones(values_of(group)), preferred_element_type=jnp.float32
        )


def prompt_end(out_ref, sum_ref):
    tokens = out_ref.shape[0]
    for head in range(QHEADS):
        blended = sum_ref[head * tokens : (head + 1) * tokens, :]
        out_ref[:, head * HD : (head + 1) * HD] = (blended[:, :HD] / blended[:, HD:]).astype(jnp.bfloat16)


def listed_prompt_kernel(
    request_ref, live_ref, query_ref, fresh_ref, blocks_ref, out_ref, kv_ref, top_ref, sum_ref, sems
):
    block_tokens = kv_ref.shape[1]
    kv_width = KVH * HD
    chunk_keys = CHUNK_BLOCKS * block_tokens
    live_blocks = live_ref[0, 0]
    chunks = (live_blocks + (CHUNK_BLOCKS - 1)) // CHUNK_BLOCKS

    def fetch(chunk, carry):
        def one(place, inner):
            entry = chunk * CHUNK_BLOCKS + place
            pltpu.make_async_copy(
                blocks_ref.at[request_ref[0, entry]], kv_ref.at[entry], sems.at[chunk]
            ).start()
            return inner

        return lax.fori_loop(0, CHUNK_BLOCKS, one, carry)

    lax.fori_loop(0, chunks, fetch, 0)
    prompt_begin(query_ref, fresh_ref, top_ref, sum_ref)

    def visit(chunk, carry):
        first = chunk * CHUNK_BLOCKS
        pltpu.make_async_copy(
            blocks_ref.at[pl.ds(0, CHUNK_BLOCKS)], kv_ref.at[pl.ds(first, CHUNK_BLOCKS)], sems.at[chunk]
        ).wait()
        shown = iota((1, chunk_keys), 1) < (live_blocks - first) * block_tokens
        take = lambda column: kv_ref[pl.ds(first, CHUNK_BLOCKS), :, column : column + HD].reshape(chunk_keys, HD)
        prompt_add(
            query_ref, top_ref, sum_ref,
            lambda group: take(group * HD), lambda group: take(kv_width + group * HD), shown,
        )
        return carry

    lax.fori_loop(0, chunks, visit, 0)
    prompt_end(out_ref, sum_ref)


def striped_prompt_kernel(
    lanes, live_ref, query_ref, fresh_ref, striped_ref, out_ref, top_ref, sum_ref
):
    regions, room, block_tokens = striped_ref.shape[0] // lanes, striped_ref.shape[1], striped_ref.shape[2]
    chunk_keys = CHUNK_BLOCKS * block_tokens
    prompt_begin(query_ref, fresh_ref, top_ref, sum_ref)
    for region in range(regions):
        live_blocks = live_ref[0, region]

        def visit(chunk, carry):
            first = jnp.minimum(chunk * CHUNK_BLOCKS, room - CHUNK_BLOCKS)
            key = iota((1, chunk_keys), 1)
            shown = (key < (live_blocks - first) * block_tokens) & (
                key >= (chunk * CHUNK_BLOCKS - first) * block_tokens
            )
            take = lambda lane: striped_ref[region * lanes + lane, pl.ds(first, CHUNK_BLOCKS)].reshape(
                chunk_keys, HD
            )
            prompt_add(
                query_ref, top_ref, sum_ref, lambda group: take(group), lambda group: take(KVH + group), shown
            )
            return carry

        lax.fori_loop(0, (live_blocks + (CHUNK_BLOCKS - 1)) // CHUNK_BLOCKS, visit, 0)
    prompt_end(out_ref, sum_ref)


def prompt_attention(kernel, scalars, queries, new_kv, cached, cached_spec, scratch, keys, name):
    tokens, width = queries.shape
    whole = lambda *shape: pl.BlockSpec(shape, lambda *_: (0,) * len(shape))
    return pl.pallas_call(
        kernel,
        out_shape=jax.ShapeDtypeStruct((tokens, width), jnp.bfloat16),
        grid_spec=pltpu.PrefetchScalarGridSpec(
            num_scalar_prefetch=len(scalars),
            grid=(1,),
            in_specs=[whole(tokens, width), whole(tokens, new_kv.shape[1]), cached_spec],
            out_specs=whole(tokens, width),
            scratch_shapes=scratch[:1] * (len(scratch) > 1)
            + [
                pltpu.VMEM((QHEADS * tokens, HD), jnp.float32),
                pltpu.VMEM((QHEADS * tokens, 2 * HD), jnp.float32),
            ]
            + scratch[1:],
        ),
        compiler_params=pltpu.CompilerParams(vmem_limit_bytes=VMEM_BYTES),
        cost_estimate=pl.CostEstimate(
            flops=4 * tokens * keys * width,
            bytes_accessed=4 * tokens * width + 2 * keys * new_kv.shape[1],
            transcendentals=tokens * QHEADS * keys,
        ),
        name=name,
    )(*scalars, queries, new_kv, cached)


def listed_prompt(request, live, queries, new_kv, blocks):
    entries, block_tokens = request.shape[1], blocks.shape[1]
    chunks = -(-entries // CHUNK_BLOCKS)
    scratch = [
        pltpu.VMEM((chunks * CHUNK_BLOCKS, block_tokens, new_kv.shape[1]), jnp.bfloat16),
        pltpu.SemaphoreType.DMA((chunks,)),
    ]
    return prompt_attention(
        listed_prompt_kernel, (request, live), queries, new_kv, blocks,
        pl.BlockSpec(memory_space=pl.ANY), scratch, entries * block_tokens + queries.shape[0], "listed_prompt",
    )


def striped_prompt(lanes, live, queries, new_kv, striped):
    keys = striped.shape[1] * striped.shape[2] + queries.shape[0]
    return prompt_attention(
        functools.partial(striped_prompt_kernel, lanes), (live,), queries, new_kv, striped,
        pl.BlockSpec(striped.shape, lambda *_: (0,) * 4), [], keys, "striped_prompt",
    )


def stripe_kernel(lanes, cache_ref, *refs):
    out_refs, sems = refs[:-1], refs[-1]
    member = lax.axis_index("seq") % lanes
    copies = []
    for step, out_ref in enumerate(out_refs, 1):
        column = pl.multiple_of((member ^ step) * LANES, LANES)
        copies.append(pltpu.make_async_copy(cache_ref.at[:, :, pl.ds(column, LANES)], out_ref, sems.at[step - 1]))
        copies[-1].start()
    for copy in copies:
        copy.wait()


def stripe(lanes, kv_cache):
    blocks, block_tokens, _ = kv_cache.shape
    piece = jax.ShapeDtypeStruct((blocks, block_tokens, LANES), jnp.bfloat16)
    return pl.pallas_call(
        functools.partial(stripe_kernel, lanes),
        out_shape=(piece,) * (lanes - 1),
        in_specs=[pl.BlockSpec(memory_space=pl.ANY)],
        out_specs=(pl.BlockSpec(memory_space=pl.ANY),) * (lanes - 1),
        scratch_shapes=[pltpu.SemaphoreType.DMA((lanes - 1,))],
        compiler_params=pltpu.CompilerParams(vmem_limit_bytes=VMEM_BYTES),
        name="stripe",
    )(kv_cache)


def gather_kernel(lanes, index_ref, amount_ref, cache_ref, *refs):
    piece_refs, out_ref, held_ref, sems = refs[: lanes - 1], refs[-3], refs[-2], refs[-1]
    blocks = cache_ref.shape[0]
    room = out_ref.shape[1]
    column = pl.multiple_of((lax.axis_index("seq") % lanes) * LANES, LANES)
    copies = [pltpu.make_async_copy(cache_ref.at[:, :, pl.ds(column, LANES)], held_ref.at[pl.ds(0, blocks)], sems.at[0])]
    for step, piece_ref in enumerate(piece_refs, 1):
        copies.append(
            pltpu.make_async_copy(piece_ref, held_ref.at[pl.ds(step * blocks, blocks)], sems.at[step])
        )
    for copy in copies:
        copy.start()
    for copy in copies:
        copy.wait()

    def reader(number, carry):
        chunks = (amount_ref[number] + (CHUNK_BLOCKS - 1)) // CHUNK_BLOCKS
        groups = jnp.minimum(chunks * (CHUNK_BLOCKS // ROOM_STEP), room // ROOM_STEP)

        def some(group, inner):
            for i in range(ROOM_STEP):
                entry = group * ROOM_STEP + i
                out_ref[number, entry] = held_ref[index_ref[number, entry]]
            return inner

        return lax.fori_loop(0, groups, some, carry)

    lax.fori_loop(0, out_ref.shape[0], reader, 0)


def gather_stripes(lanes, room, index, amount, kv_cache, pieces):
    blocks, block_tokens, _ = kv_cache.shape
    readers = index.shape[0]
    shape = (readers, room, block_tokens, LANES)
    return pl.pallas_call(
        functools.partial(gather_kernel, lanes),
        out_shape=jax.ShapeDtypeStruct(shape, jnp.bfloat16),
        grid_spec=pltpu.PrefetchScalarGridSpec(
            num_scalar_prefetch=2,
            grid=(1,),
            in_specs=[pl.BlockSpec(memory_space=pl.ANY)] * lanes,
            out_specs=pl.BlockSpec(shape, lambda *_: (0,) * 4),
            scratch_shapes=[
                pltpu.VMEM((lanes * blocks, block_tokens, LANES), jnp.bfloat16),
                pltpu.SemaphoreType.DMA((lanes,)),
            ],
        ),
        compiler_params=pltpu.CompilerParams(vmem_limit_bytes=VMEM_BYTES),
        cost_estimate=pl.CostEstimate(
            flops=0, bytes_accessed=4 * readers * room * block_tokens * LANES, transcendentals=0
        ),
        name="gather_stripes",
    )(index, amount, kv_cache, *pieces)


def pick_kernel(target_ref, returned_ref, out_ref):
    rows, slots = target_ref.shape[0], returned_ref.shape[0]
    picked = (target_ref[...] == iota((rows, slots), 1)).astype(jnp.bfloat16)
    out_ref[...] = jnp.dot(
        picked, returned_ref[...], preferred_element_type=jnp.float32
    ).astype(jnp.bfloat16)


def pick_rows(target, returned):
    return pl.pallas_call(
        pick_kernel,
        out_shape=jax.ShapeDtypeStruct((target.shape[0], returned.shape[1]), jnp.bfloat16),
        compiler_params=pltpu.CompilerParams(vmem_limit_bytes=VMEM_BYTES),
        name="pick_rows",
    )(target, returned)


def window_attention(qkv_rows, windows):
    total_rows = qkv_rows.shape[0]
    inner_width = VHEADS * VHD
    query_heads = qkv_rows[:, :inner_width].reshape(total_rows, VHEADS, VHD)
    key_heads = qkv_rows[:, inner_width : 2 * inner_width].reshape(total_rows, VHEADS, VHD)
    value_heads = qkv_rows[:, 2 * inner_width :].reshape(total_rows, VHEADS, VHD)
    is_live = windows >= 0
    every_row = jnp.arange(total_rows)
    scores = jnp.einsum(
        "qhd,khd->hqk", query_heads, key_heads, preferred_element_type=jnp.float32
    ) * VHD ** (-0.5)
    allowed = (windows[:, None] == windows[None, :]) & is_live[None, :] | (
        every_row[:, None] == every_row[None, :]
    )
    scores = jnp.where(allowed[None], scores, -jnp.inf)
    highest = jnp.max(scores, axis=2, keepdims=True)
    weights = jnp.exp(scores - highest)
    totals = jnp.sum(weights, axis=2)
    blended = jnp.einsum(
        "hqk,khd->qhd",
        weights.astype(jnp.bfloat16),
        value_heads,
        preferred_element_type=jnp.float32,
    )
    pieces = (blended / totals.T[:, :, None]).reshape(total_rows, inner_width)
    return pieces.astype(jnp.bfloat16)


def exchange(rows, devices):
    parts = rows.reshape((devices, rows.shape[0] // devices) + rows.shape[1:])
    return lax.all_to_all(parts, "seq", split_axis=0, concat_axis=0, tiled=True).reshape(rows.shape)


def vision_rows(arrived, windows, w_qkv):
    vit = w_qkv.shape[0]
    qkv_rows = jnp.dot(arrived[:, :vit], w_qkv, preferred_element_type=jnp.float32).astype(jnp.bfloat16)
    return window_attention(qkv_rows, windows)


def shards(
    patches,
    row_owner,
    window_slot,
    w_patch,
    vit_gain,
    w_qkv,
    queries,
    new_kv,
    kv_cache,
    block_table,
):
    devices = lax.axis_size("seq")
    vit = w_patch.shape[1]
    capacity = 2 * patches.shape[0] // devices
    slots = devices * capacity
    entries = block_table.shape[1]
    per_owner = 2 * entries // devices
    blocks_dev = kv_cache.shape[0]
    lanes = kv_cache.shape[2] // LANES
    striped = devices == 2 * lanes and capacity >= 3 and entries < LANES
    pieces = stripe(lanes, kv_cache) if striped else ()
    pieces = [
        lax.ppermute(piece, "seq", [(i, i ^ step) for i in range(devices)])
        for step, piece in enumerate(pieces, 1)
    ]
    payload, target, request, live = embed_and_route(
        patches, w_patch, vit_gain, row_owner, window_slot, block_table,
        capacity, slots, per_owner, blocks_dev, lanes if striped else None,
    )
    arrived = exchange(payload, devices)

    if not striped:
        notes = arrived[:, vit : vit + 2].astype(jnp.int32)
        asked = notes[:, 1].reshape(devices, capacity)[:, :per_owner].reshape(devices * per_owner)
        delivered = exchange(kv_cache[jnp.maximum(asked, 0)], devices)
        attended = vision_rows(arrived, notes[:, 0], w_qkv)
        delivered, attended = lax.optimization_barrier((delivered, attended))
        returned = exchange(attended, devices)
        attention_out = listed_prompt(request, live, queries, new_kv, delivered)
        return (pick_rows(target, returned), attention_out)

    notes = arrived[:, vit:].astype(jnp.int32).reshape(devices, capacity, LANES)
    windows = notes[:, :, entries].reshape(slots)
    member = lax.axis_index("seq") % lanes
    local, holder, most = notes[:, 0, :entries], notes[:, 1, :entries], notes[:, 2, 0]
    index = jnp.where(local >= 0, (holder ^ member) * blocks_dev + local, 0)
    amount = jnp.sum((local >= 0).astype(jnp.int32), axis=1)

    def finish(room):
        def run(arrived, windows, index, amount, target, live, kv_cache, w_qkv, queries, new_kv, *pieces):
            outgoing = gather_stripes(lanes, room, index, amount, kv_cache, pieces)
            delivered = exchange(outgoing.reshape((devices * room,) + outgoing.shape[2:]), devices)
            delivered = delivered.reshape(outgoing.shape)
            attended = vision_rows(arrived, windows, w_qkv)
            delivered, attended = lax.optimization_barrier((delivered, attended))
            returned = exchange(attended, devices)
            attention_out = striped_prompt(lanes, live, queries, new_kv, delivered)
            return (pick_rows(target, returned), attention_out)

        return run

    rooms = [room for room in (32, 40, 48, 56) if room < entries] + [entries]
    choice = sum((jnp.max(most) > room).astype(jnp.int32) for room in rooms[:-1])
    return lax.switch(
        choice, [finish(room) for room in rooms],
        arrived, windows, index, amount, target, live, kv_cache, w_qkv, queries, new_kv, *pieces,
    )


def solution(mesh):
    in_specs = (
        P(("groups", "seq"), None),
        P(("groups", "seq"), None),
        P(("groups", "seq")),
        P(),
        P(),
        P(),
        P(("groups", "seq"), None),
        P(("groups", "seq"), None),
        P(("groups", "seq"), None, None),
        P(("groups", "seq"), None),
    )
    out_specs = (P(("groups", "seq"), None), P(("groups", "seq"), None))
    return jax.shard_map(shards, mesh=mesh, in_specs=in_specs, out_specs=out_specs, check_vma=False)
```

```python
import functools

import jax
import jax.numpy as jnp
from jax import lax
from jax.experimental import pallas as pl
from jax.experimental.pallas import tpu as pltpu
from jax.sharding import PartitionSpec as P

VHEADS = 8
VHD = 80
QHEADS = 32
KVH = 4
HD = 128
LANES = 128
CHUNK_BLOCKS = 16
HEADS_TILE = 2
LOG2E = 1.4426950408889634
HIDDEN = -1e30
VMEM_BYTES = 56 * 1024 * 1024
ROOM_STEP = 8


def iota(shape, axis):
    return lax.broadcasted_iota(jnp.int32, shape, axis)


def count(hits, axis):
    return jnp.sum(hits.astype(jnp.float32), axis=axis, keepdims=True).astype(jnp.int32)


def as_row(column):
    size = column.shape[0]
    diagonal = iota((size, size), 0) == iota((size, size), 1)
    return jnp.sum(jnp.where(diagonal, column, 0).astype(jnp.float32), axis=0, keepdims=True).astype(jnp.int32)


def as_column(row):
    size = row.shape[1]
    diagonal = iota((size, size), 0) == iota((size, size), 1)
    return jnp.sum(jnp.where(diagonal, row, 0).astype(jnp.float32), axis=1, keepdims=True).astype(jnp.int32)


def embed_kernel(
    capacity,
    per_owner,
    blocks_dev,
    lanes,
    patches_ref,
    w_ref,
    gain_ref,
    owner_ref,
    window_ref,
    table_ref,
    payload_ref,
    target_ref,
    request_ref,
    live_ref,
    turned_ref,
    embedded_ref,
):
    step = pl.program_id(0)
    width = w_ref.shape[1]

    @pl.when(step == 0)
    def _():
        turned_ref[...] = patches_ref[...].T

    piece = jnp.dot(turned_ref[...], w_ref[...], preferred_element_type=jnp.float32)
    embedded_ref[:, pl.ds(pl.multiple_of(step * width, width), width)] = piece.astype(jnp.bfloat16)

    @pl.when(step == pl.num_programs(0) - 1)
    def _():
        slots = payload_ref.shape[0]
        vit = embedded_ref.shape[1]
        rows = owner_ref.shape[1]
        owner_row = owner_ref[...]
        owner_column = as_column(owner_row)
        same = owner_column == owner_row
        first, second = iota((rows, rows), 0), iota((rows, rows), 1)
        rank_row = count(same & (first < second), 0)
        rank_column = count(same & (second < first), 1)
        own = 0 if lanes is None else lax.axis_index("seq")
        target_ref[...] = (owner_column ^ own) * capacity + rank_column
        placed = (owner_row * capacity + rank_row) == iota((slots, rows), 0)
        windows = (
            jnp.sum(jnp.where(placed, window_ref[...] + 1, 0).astype(jnp.float32), axis=1, keepdims=True)
            - 1.0
        )
        note_list(capacity, per_owner, blocks_dev, lanes, windows, table_ref, payload_ref.at[:, vit:], request_ref, live_ref)

        widened = embedded_ref[...].astype(jnp.float32)
        factor = lax.rsqrt(jnp.mean(widened * widened, axis=1, keepdims=True) + 1e-06)
        normed = (widened * factor * gain_ref[...]).astype(jnp.bfloat16)
        payload_ref[:, :vit] = jnp.dot(
            placed.astype(jnp.bfloat16), normed, preferred_element_type=jnp.float32
        ).astype(jnp.bfloat16)


def note_list(capacity, per_owner, blocks_dev, lanes, windows, table_ref, notes_ref, request_ref, live_ref):
    slots = notes_ref.shape[0]
    table_row = table_ref[...]
    entries = table_row.shape[1]
    live_row = table_row >= 0
    holder_row = jnp.where(live_row, table_row // blocks_dev, -1)
    local_row = jnp.where(live_row, table_row % blocks_dev, 0)
    lane = iota((slots, LANES), 1)
    before = iota((entries, entries), 0) < iota((entries, entries), 1)
    if lanes is None:
        holder_rank = count((as_column(holder_row) == holder_row) & before, 0)
        request_row = jnp.where(live_row, holder_row * per_owner + holder_rank, -1)
        first_request = jnp.sum(
            jnp.where(iota((1, entries), 1) == 0, request_row, 0).astype(jnp.float32), axis=1, keepdims=True
        ).astype(jnp.int32)
        request_ref[...] = jnp.where(live_row, request_row, first_request)
        live_ref[...] = jnp.broadcast_to(count(live_row, 1), live_ref.shape)
        placed_row = jnp.where(live_row, holder_row * capacity + holder_rank, -1)
        asked = jnp.sum(
            jnp.where(placed_row == iota((slots, entries), 0), local_row + 1, 0).astype(jnp.float32),
            axis=1,
            keepdims=True,
        )
        notes = jnp.where(lane == 0, windows, jnp.where(lane == 1, asked - 1.0, 0.0))
        notes_ref[...] = notes.astype(jnp.bfloat16)
        return
    regions = slots // capacity // lanes
    after = iota((entries, entries), 1) < iota((entries, entries), 0)
    region_row = jnp.where(live_row, holder_row // lanes, -1)
    region_column = as_column(region_row)
    region_rank = count((region_column == region_row) & after, 1)
    local_column, member_column = as_column(local_row), as_column(jnp.where(live_row, holder_row % lanes, 0))
    place = iota((slots, LANES), 0)
    slot_row, slot_region = place % capacity, place // (capacity * lanes)
    pad = jnp.zeros((1, LANES - entries), jnp.float32)
    notes = jnp.where(lane == entries, windows, 0.0)
    most = jnp.zeros((1, 1), jnp.int32)
    live_ref[...] = jnp.zeros(live_ref.shape, jnp.int32)
    for region in range(regions):
        listed = (region_column == region) & (region_rank == iota((entries, entries), 1))
        pick = lambda column: jnp.sum(
            jnp.where(listed, column, 0).astype(jnp.float32), axis=0, keepdims=True
        )
        amount = count(region_row == region, 1)
        most = jnp.maximum(most, amount)
        live_ref[:, region : region + 1] = amount
        locals_row = jnp.concatenate([pick(local_column + 1) - 1.0, pad], axis=1)
        members_row = jnp.concatenate([pick(member_column), pad], axis=1)
        here = (slot_region == region) & (lane < entries)
        notes = jnp.where(here & (slot_row == 0), locals_row, notes)
        notes = jnp.where(here & (slot_row == 1), members_row, notes)
    notes = jnp.where(lane == entries + 1, most.astype(jnp.float32), notes)
    notes_ref[...] = notes.astype(jnp.bfloat16)
    request_ref[...] = jnp.zeros(request_ref.shape, jnp.int32)


def embed_and_route(
    patches, w_patch, vit_gain, row_owner, window_slot, block_table, capacity, slots, per_owner, blocks_dev, lanes
):
    rows, patch = patches.shape
    vit = w_patch.shape[1]
    entries = block_table.shape[1]
    width = 2 * LANES
    whole = lambda *shape: pl.BlockSpec(shape, lambda step: (0,) * len(shape))
    return pl.pallas_call(
        functools.partial(embed_kernel, capacity, per_owner, blocks_dev, lanes),
        grid=(vit // width,),
        out_shape=(
            jax.ShapeDtypeStruct((slots, vit + LANES), jnp.bfloat16),
            jax.ShapeDtypeStruct((rows, 1), jnp.int32),
            jax.ShapeDtypeStruct((1, entries), jnp.int32),
            jax.ShapeDtypeStruct((1, LANES), jnp.int32),
        ),
        in_specs=[
            whole(patch, rows),
            pl.BlockSpec((patch, width), lambda step: (0, step)),
            whole(1, vit),
            whole(1, rows),
            whole(1, rows),
            whole(1, entries),
        ],
        out_specs=(whole(slots, vit + LANES), whole(rows, 1), whole(1, entries), whole(1, LANES)),
        scratch_shapes=[pltpu.VMEM((rows, patch), jnp.bfloat16), pltpu.VMEM((rows, vit), jnp.bfloat16)],
        compiler_params=pltpu.CompilerParams(vmem_limit_bytes=VMEM_BYTES),
        cost_estimate=pl.CostEstimate(
            flops=2 * rows * patch * vit + 2 * slots * rows * vit,
            bytes_accessed=2 * patch * vit + 2 * rows * patch + 2 * slots * vit,
            transcendentals=rows,
        ),
        name="embed_and_route",
    )(
        patches.T, w_patch, vit_gain.reshape(1, vit), row_owner.reshape(1, rows),
        window_slot.reshape(1, rows), block_table,
    )


def prompt_groups(query_ref, tile):
    tokens = query_ref.shape[0]
    group_size = QHEADS // KVH
    tile_rows = HEADS_TILE * tokens

    def group_step(group, carry):
        for part in range(group_size // HEADS_TILE):
            head = group * group_size + part * HEADS_TILE
            queries = jnp.concatenate(
                [
                    query_ref[:, pl.ds(pl.multiple_of((head + i) * HD, HD), HD)]
                    for i in range(HEADS_TILE)
                ],
                axis=0,
            )
            tile(group, queries, pl.ds(pl.multiple_of(head * tokens, tile_rows), tile_rows))
        return carry

    lax.fori_loop(0, KVH, group_step, 0)


def prompt_scores(queries, keys):
    return lax.dot_general(
        queries, keys, (((1,), (1,)), ((), ())), preferred_element_type=jnp.float32
    ) * (HD ** (-0.5) * LOG2E)


def with_ones(values):
    return jnp.concatenate([values, jnp.ones_like(values)], axis=1)


def head_columns(head):
    return pl.ds(pl.multiple_of(head * HD, HD), HD)


def prompt_begin(query_ref, fresh_ref, top_ref, sum_ref):
    tokens = query_ref.shape[0]
    causal = iota((tokens, tokens), 1) <= iota((tokens, tokens), 0)
    causal = jnp.concatenate([causal.astype(jnp.int32)] * HEADS_TILE, axis=0) > 0

    def tile(group, queries, rows):
        keys, values = fresh_ref[:, head_columns(group)], fresh_ref[:, head_columns(KVH + group)]
        scores = jnp.where(causal, prompt_scores(queries, keys), HIDDEN)
        top = jnp.max(scores, axis=1, keepdims=True)
        weights = jnp.exp2(scores - top).astype(jnp.bfloat16)
        top_ref[rows, :] = jnp.broadcast_to(top, (scores.shape[0], HD))
        sum_ref[rows, :] = jnp.dot(weights, with_ones(values), preferred_element_type=jnp.float32)

    prompt_groups(query_ref, tile)


def prompt_add(query_ref, top_ref, sum_ref, take, shown):
    chunk_keys = shown.shape[1]

    def tile(group, queries, rows):
        scores = jnp.where(shown, prompt_scores(queries, take(group)), HIDDEN)
        old_top = top_ref[rows, :]
        top = jnp.maximum(old_top, jnp.max(scores, axis=1, keepdims=True))
        shrink = jnp.exp2(old_top - top)
        weights = jnp.exp2(scores - jnp.concatenate([top] * (chunk_keys // HD), axis=1))
        top_ref[rows, :] = top
        sum_ref[rows, :] = sum_ref[rows, :] * jnp.concatenate([shrink, shrink], axis=1) + jnp.dot(
            weights.astype(jnp.bfloat16), with_ones(take(KVH + group)), preferred_element_type=jnp.float32
        )

    prompt_groups(query_ref, tile)


def prompt_end(out_ref, sum_ref):
    tokens = out_ref.shape[0]

    def finish(head, carry):
        blended = sum_ref[pl.ds(pl.multiple_of(head * tokens, tokens), tokens), :]
        out_ref[:, head_columns(head)] = (blended[:, :HD] / blended[:, HD:]).astype(jnp.bfloat16)
        return carry

    lax.fori_loop(0, QHEADS, finish, 0)


def listed_prompt_kernel(
    request_ref, live_ref, query_ref, fresh_ref, blocks_ref, out_ref, kv_ref, top_ref, sum_ref, sems
):
    block_tokens = kv_ref.shape[1]
    chunk_keys = CHUNK_BLOCKS * block_tokens
    live_blocks = live_ref[0, 0]
    chunks = (live_blocks + (CHUNK_BLOCKS - 1)) // CHUNK_BLOCKS

    def fetch(chunk, carry):
        def one(place, inner):
            entry = chunk * CHUNK_BLOCKS + place
            pltpu.make_async_copy(
                blocks_ref.at[request_ref[0, entry]], kv_ref.at[entry], sems.at[chunk]
            ).start()
            return inner

        return lax.fori_loop(0, CHUNK_BLOCKS, one, carry)

    lax.fori_loop(0, chunks, fetch, 0)
    prompt_begin(query_ref, fresh_ref, top_ref, sum_ref)

    def visit(chunk, carry):
        first = chunk * CHUNK_BLOCKS
        pltpu.make_async_copy(
            blocks_ref.at[pl.ds(0, CHUNK_BLOCKS)], kv_ref.at[pl.ds(first, CHUNK_BLOCKS)], sems.at[chunk]
        ).wait()
        shown = iota((1, chunk_keys), 1) < (live_blocks - first) * block_tokens
        take = lambda head: kv_ref[pl.ds(first, CHUNK_BLOCKS), :, head_columns(head)].reshape(chunk_keys, HD)
        prompt_add(query_ref, top_ref, sum_ref, take, shown)
        return carry

    lax.fori_loop(0, chunks, visit, 0)
    prompt_end(out_ref, sum_ref)


def striped_prompt_kernel(
    lanes, live_ref, query_ref, fresh_ref, striped_ref, out_ref, top_ref, sum_ref
):
    regions, room, block_tokens = striped_ref.shape[0] // lanes, striped_ref.shape[1], striped_ref.shape[2]
    chunk_keys = CHUNK_BLOCKS * block_tokens
    prompt_begin(query_ref, fresh_ref, top_ref, sum_ref)
    chunks = [(live_ref[0, region] + (CHUNK_BLOCKS - 1)) // CHUNK_BLOCKS for region in range(regions)]

    def visit(turn, carry):
        region = (turn >= chunks[0]).astype(jnp.int32)
        chunk = turn - region * chunks[0]
        first = jnp.minimum(chunk * CHUNK_BLOCKS, room - CHUNK_BLOCKS)
        key = iota((1, chunk_keys), 1)
        shown = (key < (live_ref[0, region] - first) * block_tokens) & (
            key >= (chunk * CHUNK_BLOCKS - first) * block_tokens
        )
        take = lambda lane: striped_ref[region * lanes + lane, pl.ds(first, CHUNK_BLOCKS)].reshape(chunk_keys, HD)
        prompt_add(query_ref, top_ref, sum_ref, take, shown)
        return carry

    lax.fori_loop(0, chunks[0] + chunks[1], visit, 0)
    prompt_end(out_ref, sum_ref)


def prompt_attention(kernel, scalars, queries, new_kv, cached, cached_spec, scratch, keys, name):
    tokens, width = queries.shape
    whole = lambda *shape: pl.BlockSpec(shape, lambda *_: (0,) * len(shape))
    return pl.pallas_call(
        kernel,
        out_shape=jax.ShapeDtypeStruct((tokens, width), jnp.bfloat16),
        grid_spec=pltpu.PrefetchScalarGridSpec(
            num_scalar_prefetch=len(scalars),
            grid=(1,),
            in_specs=[whole(tokens, width), whole(tokens, new_kv.shape[1]), cached_spec],
            out_specs=whole(tokens, width),
            scratch_shapes=scratch[:1] * (len(scratch) > 1)
            + [
                pltpu.VMEM((QHEADS * tokens, HD), jnp.float32),
                pltpu.VMEM((QHEADS * tokens, 2 * HD), jnp.float32),
            ]
            + scratch[1:],
        ),
        compiler_params=pltpu.CompilerParams(vmem_limit_bytes=VMEM_BYTES),
        cost_estimate=pl.CostEstimate(
            flops=4 * tokens * keys * width,
            bytes_accessed=4 * tokens * width + 2 * keys * new_kv.shape[1],
            transcendentals=tokens * QHEADS * keys,
        ),
        name=name,
    )(*scalars, queries, new_kv, cached)


def listed_prompt(request, live, queries, new_kv, blocks):
    entries, block_tokens = request.shape[1], blocks.shape[1]
    chunks = -(-entries // CHUNK_BLOCKS)
    scratch = [
        pltpu.VMEM((chunks * CHUNK_BLOCKS, block_tokens, new_kv.shape[1]), jnp.bfloat16),
        pltpu.SemaphoreType.DMA((chunks,)),
    ]
    return prompt_attention(
        listed_prompt_kernel, (request, live), queries, new_kv, blocks,
        pl.BlockSpec(memory_space=pl.ANY), scratch, entries * block_tokens + queries.shape[0], "listed_prompt",
    )


def striped_prompt(lanes, live, queries, new_kv, striped):
    keys = striped.shape[1] * striped.shape[2] + queries.shape[0]
    return prompt_attention(
        functools.partial(striped_prompt_kernel, lanes), (live,), queries, new_kv, striped,
        pl.BlockSpec(striped.shape, lambda *_: (0,) * 4), [], keys, "striped_prompt",
    )


def stripe_kernel(lanes, cache_ref, *refs):
    out_refs, sems = refs[:-1], refs[-1]
    member = lax.axis_index("seq") % lanes
    copies = []
    for step, out_ref in enumerate(out_refs, 1):
        column = pl.multiple_of((member ^ step) * LANES, LANES)
        copies.append(pltpu.make_async_copy(cache_ref.at[:, :, pl.ds(column, LANES)], out_ref, sems.at[step - 1]))
        copies[-1].start()
    for copy in copies:
        copy.wait()


def stripe(lanes, kv_cache):
    blocks, block_tokens, _ = kv_cache.shape
    piece = jax.ShapeDtypeStruct((blocks, block_tokens, LANES), jnp.bfloat16)
    return pl.pallas_call(
        functools.partial(stripe_kernel, lanes),
        out_shape=(piece,) * (lanes - 1),
        in_specs=[pl.BlockSpec(memory_space=pl.ANY)],
        out_specs=(pl.BlockSpec(memory_space=pl.ANY),) * (lanes - 1),
        scratch_shapes=[pltpu.SemaphoreType.DMA((lanes - 1,))],
        compiler_params=pltpu.CompilerParams(vmem_limit_bytes=VMEM_BYTES),
        name="stripe",
    )(kv_cache)


def gather_kernel(lanes, entries, notes_ref, cache_ref, *refs):
    piece_refs = refs[: lanes - 1]
    out_ref, held_ref, wide_ref, index_ref, scalar_ref, sems = refs[lanes - 1 :]
    blocks = cache_ref.shape[0]
    readers, room = out_ref.shape[0], out_ref.shape[1]
    capacity = notes_ref.shape[0] // readers
    column = pl.multiple_of((lax.axis_index("seq") % lanes) * LANES, LANES)
    copies = [pltpu.make_async_copy(cache_ref.at[:, :, pl.ds(column, LANES)], held_ref.at[pl.ds(0, blocks)], sems.at[0])]
    for step, piece_ref in enumerate(piece_refs, 1):
        copies.append(
            pltpu.make_async_copy(piece_ref, held_ref.at[pl.ds(step * blocks, blocks)], sems.at[step])
        )
    for copy in copies:
        copy.start()

    wide_ref[...] = notes_ref[...].astype(jnp.float32)
    local = wide_ref[pl.ds(0, readers, capacity), :]
    member = wide_ref[pl.ds(1, readers, capacity), :]
    lane = iota((readers, LANES), 1)
    listed = (local >= 0.0) & (lane < entries)
    step = member.astype(jnp.int32) ^ (lax.axis_index("seq") % lanes)
    amount = jnp.sum(listed.astype(jnp.float32), axis=1, keepdims=True).astype(jnp.int32)
    index = jnp.where(listed, step * blocks + local.astype(jnp.int32), 0)
    index_ref[...] = jnp.where(lane == entries, amount, index)
    to_scalars = pltpu.make_async_copy(index_ref, scalar_ref, sems.at[lanes])
    to_scalars.start()
    to_scalars.wait()
    for copy in copies:
        copy.wait()

    def reader(number, carry):
        chunks = (scalar_ref[number, entries] + (CHUNK_BLOCKS - 1)) // CHUNK_BLOCKS
        groups = jnp.minimum(chunks * (CHUNK_BLOCKS // ROOM_STEP), room // ROOM_STEP)

        def some(group, inner):
            first = group * ROOM_STEP
            tiles = [held_ref[scalar_ref[number, first + i]] for i in range(ROOM_STEP)]
            for i, tile in enumerate(tiles):
                out_ref[number, first + i] = tile
            return inner

        return lax.fori_loop(0, groups, some, carry)

    lax.fori_loop(0, readers, reader, 0)


def gather_stripes(lanes, room, entries, readers, arrived, kv_cache, pieces):
    blocks, block_tokens, _ = kv_cache.shape
    slots = arrived.shape[0]
    last = arrived.shape[1] // LANES - 1
    shape = (readers, room, block_tokens, LANES)
    return pl.pallas_call(
        functools.partial(gather_kernel, lanes, entries),
        out_shape=jax.ShapeDtypeStruct(shape, jnp.bfloat16),
        grid=(1,),
        in_specs=[pl.BlockSpec((slots, LANES), lambda _: (0, last))]
        + [pl.BlockSpec(memory_space=pl.ANY)] * lanes,
        out_specs=pl.BlockSpec(shape, lambda _: (0,) * 4),
        scratch_shapes=[
            pltpu.VMEM((lanes * blocks, block_tokens, LANES), jnp.bfloat16),
            pltpu.VMEM((slots, LANES), jnp.float32),
            pltpu.VMEM((readers, LANES), jnp.int32),
            pltpu.SMEM((readers, LANES), jnp.int32),
            pltpu.SemaphoreType.DMA((lanes + 1,)),
        ],
        compiler_params=pltpu.CompilerParams(vmem_limit_bytes=VMEM_BYTES),
        cost_estimate=pl.CostEstimate(
            flops=0, bytes_accessed=4 * readers * room * block_tokens * LANES, transcendentals=0
        ),
        name="gather_stripes",
    )(arrived, kv_cache, *pieces)


def vision_kernel(entries, rows_ref, w_ref, *refs):
    out_refs, qkv_ref, blend_ref = refs[:-2], refs[-2], refs[-1]
    slots, vit = rows_ref.shape[0], w_ref.shape[0]
    inner = VHEADS * VHD
    qkv_ref[...] = jnp.dot(
        rows_ref[:, :vit], w_ref[...], preferred_element_type=jnp.float32
    ).astype(jnp.bfloat16)
    notes = rows_ref[:, vit:].astype(jnp.float32)
    window_column = jnp.sum(
        jnp.where(iota((slots, LANES), 1) == entries, notes, 0.0), axis=1, keepdims=True
    ).astype(jnp.int32)
    window_row = as_row(window_column)
    itself = iota((slots, slots), 0) == iota((slots, slots), 1)
    allowed = ((window_column == window_row) & (window_row >= 0)) | itself
    blend_ref[...] = jnp.zeros_like(blend_ref)
    for head in range(VHEADS):
        first, last = head * VHD, (head + 1) * VHD
        low, high = first // LANES * LANES, -(-last // LANES) * LANES
        column = low + iota((slots, high - low), 1)
        mine = (column >= first) & (column < last)
        part = lambda offset: qkv_ref[:, offset + low : offset + high]
        keys = jnp.where(mine, part(inner).astype(jnp.float32), 0.0).astype(jnp.bfloat16)
        values = jnp.where(mine, part(2 * inner).astype(jnp.float32), 0.0).astype(jnp.bfloat16)
        scores = lax.dot_general(
            part(0), keys, (((1,), (1,)), ((), ())), preferred_element_type=jnp.float32
        ) * VHD ** (-0.5)
        scores = jnp.where(allowed, scores, HIDDEN)
        weights = jnp.exp(scores - jnp.max(scores, axis=1, keepdims=True))
        total = jnp.sum(weights, axis=1, keepdims=True)
        blended = jnp.dot(weights.astype(jnp.bfloat16), values, preferred_element_type=jnp.float32)
        blend_ref[:, low:high] += blended / total
    device = lax.axis_index("seq")
    rows = out_refs[0].shape[0]
    for step, out_ref in enumerate(out_refs):
        place = pl.multiple_of((device ^ step) * rows, rows)
        out_ref[...] = blend_ref[pl.ds(place, rows), :].astype(jnp.bfloat16)


def vision_pieces(devices, entries, arrived, w_qkv):
    slots = arrived.shape[0]
    vit, width = w_qkv.shape
    inner = VHEADS * VHD
    return pl.pallas_call(
        functools.partial(vision_kernel, entries),
        out_shape=(jax.ShapeDtypeStruct((slots // devices, inner), jnp.bfloat16),) * devices,
        scratch_shapes=[pltpu.VMEM((slots, width), jnp.bfloat16), pltpu.VMEM((slots, inner), jnp.float32)],
        compiler_params=pltpu.CompilerParams(vmem_limit_bytes=VMEM_BYTES),
        cost_estimate=pl.CostEstimate(
            flops=2 * slots * vit * width + 4 * slots * slots * inner,
            bytes_accessed=2 * vit * width,
            transcendentals=VHEADS * slots * slots,
        ),
        name="vision_pieces",
    )(arrived, w_qkv)


def pick_kernel(target_ref, *refs):
    out_ref = refs[-1]
    returned = jnp.concatenate([ref[...] for ref in refs[:-1]], axis=0)
    rows, slots = target_ref.shape[0], returned.shape[0]
    picked = (target_ref[...] == iota((rows, slots), 1)).astype(jnp.bfloat16)
    out_ref[...] = jnp.dot(picked, returned, preferred_element_type=jnp.float32).astype(jnp.bfloat16)


def pick_rows(target, *returned):
    return pl.pallas_call(
        pick_kernel,
        out_shape=jax.ShapeDtypeStruct((target.shape[0], returned[0].shape[1]), jnp.bfloat16),
        compiler_params=pltpu.CompilerParams(vmem_limit_bytes=VMEM_BYTES),
        name="pick_rows",
    )(target, *returned)


def window_attention(qkv_rows, windows):
    total_rows = qkv_rows.shape[0]
    inner_width = VHEADS * VHD
    query_heads = qkv_rows[:, :inner_width].reshape(total_rows, VHEADS, VHD)
    key_heads = qkv_rows[:, inner_width : 2 * inner_width].reshape(total_rows, VHEADS, VHD)
    value_heads = qkv_rows[:, 2 * inner_width :].reshape(total_rows, VHEADS, VHD)
    is_live = windows >= 0
    every_row = jnp.arange(total_rows)
    scores = jnp.einsum(
        "qhd,khd->hqk", query_heads, key_heads, preferred_element_type=jnp.float32
    ) * VHD ** (-0.5)
    allowed = (windows[:, None] == windows[None, :]) & is_live[None, :] | (
        every_row[:, None] == every_row[None, :]
    )
    scores = jnp.where(allowed[None], scores, -jnp.inf)
    highest = jnp.max(scores, axis=2, keepdims=True)
    weights = jnp.exp(scores - highest)
    totals = jnp.sum(weights, axis=2)
    blended = jnp.einsum(
        "hqk,khd->qhd",
        weights.astype(jnp.bfloat16),
        value_heads,
        preferred_element_type=jnp.float32,
    )
    pieces = (blended / totals.T[:, :, None]).reshape(total_rows, inner_width)
    return pieces.astype(jnp.bfloat16)


def exchange(rows, devices):
    parts = rows.reshape((devices, rows.shape[0] // devices) + rows.shape[1:])
    return lax.all_to_all(parts, "seq", split_axis=0, concat_axis=0, tiled=True).reshape(rows.shape)


def swap(piece, step, devices):
    return lax.ppermute(piece, "seq", [(i, i ^ step) for i in range(devices)])


def vision_rows(arrived, windows, w_qkv):
    vit = w_qkv.shape[0]
    qkv_rows = jnp.dot(arrived[:, :vit], w_qkv, preferred_element_type=jnp.float32).astype(jnp.bfloat16)
    return window_attention(qkv_rows, windows)


def shards(
    patches,
    row_owner,
    window_slot,
    w_patch,
    vit_gain,
    w_qkv,
    queries,
    new_kv,
    kv_cache,
    block_table,
):
    devices = lax.axis_size("seq")
    vit = w_patch.shape[1]
    capacity = 2 * patches.shape[0] // devices
    slots = devices * capacity
    entries = block_table.shape[1]
    per_owner = 2 * entries // devices
    blocks_dev = kv_cache.shape[0]
    lanes = kv_cache.shape[2] // LANES
    striped = devices == 2 * lanes and capacity >= 3 and entries + 2 <= LANES
    if striped:
        pieces, block_table = lax.optimization_barrier((stripe(lanes, kv_cache), block_table))
        pieces = [swap(piece, step, devices) for step, piece in enumerate(pieces, 1)]
    payload, target, request, live = embed_and_route(
        patches, w_patch, vit_gain, row_owner, window_slot, block_table,
        capacity, slots, per_owner, blocks_dev, lanes if striped else None,
    )
    arrived = exchange(payload, devices)

    if not striped:
        notes = arrived[:, vit : vit + 2].astype(jnp.int32)
        asked = notes[:, 1].reshape(devices, capacity)[:, :per_owner].reshape(devices * per_owner)
        delivered = exchange(kv_cache[jnp.maximum(asked, 0)], devices)
        attended = vision_rows(arrived, notes[:, 0], w_qkv)
        delivered, attended = lax.optimization_barrier((delivered, attended))
        returned = exchange(attended, devices)
        attention_out = listed_prompt(request, live, queries, new_kv, delivered)
        return (pick_rows(target, returned), attention_out)

    most = jnp.max(arrived[:, vit + entries + 1].astype(jnp.float32))

    def finish(room):
        def run(arrived, target, live, kv_cache, w_qkv, queries, new_kv, *pieces):
            outgoing = gather_stripes(lanes, room, entries, devices, arrived, kv_cache, pieces)
            delivered = exchange(outgoing.reshape((devices * room,) + outgoing.shape[2:]), devices)
            delivered = delivered.reshape(outgoing.shape)
            attended = vision_pieces(devices, entries, arrived, w_qkv)
            returned = [attended[0]] + [
                swap(piece, step, devices) for step, piece in enumerate(attended[1:], 1)
            ]
            vision_out = pick_rows(target, *returned)
            return (vision_out, striped_prompt(lanes, live, queries, new_kv, delivered))

        return run

    rooms = [room for room in (32, 40, 48, 56) if room < entries] + [entries]
    choice = sum((most > room).astype(jnp.int32) for room in rooms[:-1])
    return lax.switch(
        choice, [finish(room) for room in rooms],
        arrived, target, live, kv_cache, w_qkv, queries, new_kv, *pieces,
    )


def solution(mesh):
    in_specs = (
        P(("groups", "seq"), None),
        P(("groups", "seq"), None),
        P(("groups", "seq")),
        P(),
        P(),
        P(),
        P(("groups", "seq"), None),
        P(("groups", "seq"), None),
        P(("groups", "seq"), None, None),
        P(("groups", "seq"), None),
    )
    out_specs = (P(("groups", "seq"), None), P(("groups", "seq"), None))
    return jax.shard_map(shards, mesh=mesh, in_specs=in_specs, out_specs=out_specs, check_vma=False)
```

```python
import functools

import jax
import jax.numpy as jnp
from jax import lax
from jax.experimental import pallas as pl
from jax.experimental.pallas import tpu as pltpu
from jax.sharding import PartitionSpec as P

VHEADS = 8
VHD = 80
QHEADS = 32
KVH = 4
HD = 128
LANES = 128
CHUNK_BLOCKS = 16
HEADS_TILE = 2
LOG2E = 1.4426950408889634
HIDDEN = -1e30
VMEM_BYTES = 56 * 1024 * 1024
ROOM_STEP = 8


def iota(shape, axis):
    return lax.broadcasted_iota(jnp.int32, shape, axis)


def count(hits, axis):
    return jnp.sum(hits.astype(jnp.float32), axis=axis, keepdims=True).astype(jnp.int32)


def as_row(column):
    size = column.shape[0]
    diagonal = iota((size, size), 0) == iota((size, size), 1)
    return jnp.sum(jnp.where(diagonal, column, 0).astype(jnp.float32), axis=0, keepdims=True).astype(jnp.int32)


def as_column(row):
    size = row.shape[1]
    diagonal = iota((size, size), 0) == iota((size, size), 1)
    return jnp.sum(jnp.where(diagonal, row, 0).astype(jnp.float32), axis=1, keepdims=True).astype(jnp.int32)


def embed_kernel(
    capacity,
    per_owner,
    blocks_dev,
    lanes,
    patches_ref,
    w_ref,
    gain_ref,
    owner_ref,
    window_ref,
    table_ref,
    payload_ref,
    target_ref,
    request_ref,
    live_ref,
    turned_ref,
    embedded_ref,
):
    step = pl.program_id(0)
    width = w_ref.shape[1]

    @pl.when(step == 0)
    def _():
        turned_ref[...] = patches_ref[...].T

    piece = jnp.dot(turned_ref[...], w_ref[...], preferred_element_type=jnp.float32)
    embedded_ref[:, pl.ds(pl.multiple_of(step * width, width), width)] = piece.astype(jnp.bfloat16)

    @pl.when(step == pl.num_programs(0) - 1)
    def _():
        slots = payload_ref.shape[0]
        vit = embedded_ref.shape[1]
        rows = owner_ref.shape[1]
        owner_row = owner_ref[...]
        owner_column = as_column(owner_row)
        same = owner_column == owner_row
        first, second = iota((rows, rows), 0), iota((rows, rows), 1)
        rank_row = count(same & (first < second), 0)
        rank_column = count(same & (second < first), 1)
        target_ref[...] = owner_column * capacity + rank_column
        placed = (owner_row * capacity + rank_row) == iota((slots, rows), 0)
        windows = (
            jnp.sum(jnp.where(placed, window_ref[...] + 1, 0).astype(jnp.float32), axis=1, keepdims=True)
            - 1.0
        )
        note_list(capacity, per_owner, blocks_dev, lanes, windows, table_ref, payload_ref.at[:, vit:], request_ref, live_ref)

        widened = embedded_ref[...].astype(jnp.float32)
        factor = lax.rsqrt(jnp.mean(widened * widened, axis=1, keepdims=True) + 1e-06)
        normed = (widened * factor * gain_ref[...]).astype(jnp.bfloat16)
        payload_ref[:, :vit] = jnp.dot(
            placed.astype(jnp.bfloat16), normed, preferred_element_type=jnp.float32
        ).astype(jnp.bfloat16)


def note_list(capacity, per_owner, blocks_dev, lanes, windows, table_ref, notes_ref, request_ref, live_ref):
    slots = notes_ref.shape[0]
    table_row = table_ref[...]
    entries = table_row.shape[1]
    live_row = table_row >= 0
    holder_row = jnp.where(live_row, table_row // blocks_dev, -1)
    local_row = jnp.where(live_row, table_row % blocks_dev, 0)
    lane = iota((slots, LANES), 1)
    before = iota((entries, entries), 0) < iota((entries, entries), 1)
    if lanes is None:
        holder_rank = count((as_column(holder_row) == holder_row) & before, 0)
        request_row = jnp.where(live_row, holder_row * per_owner + holder_rank, -1)
        first_request = jnp.sum(
            jnp.where(iota((1, entries), 1) == 0, request_row, 0).astype(jnp.float32), axis=1, keepdims=True
        ).astype(jnp.int32)
        request_ref[...] = jnp.where(live_row, request_row, first_request)
        live_ref[...] = jnp.broadcast_to(count(live_row, 1), live_ref.shape)
        placed_row = jnp.where(live_row, holder_row * capacity + holder_rank, -1)
        asked = jnp.sum(
            jnp.where(placed_row == iota((slots, entries), 0), local_row + 1, 0).astype(jnp.float32),
            axis=1,
            keepdims=True,
        )
        notes = jnp.where(lane == 0, windows, jnp.where(lane == 1, asked - 1.0, 0.0))
        notes_ref[...] = notes.astype(jnp.bfloat16)
        return
    regions = slots // capacity // lanes
    after = iota((entries, entries), 1) < iota((entries, entries), 0)
    region_row = jnp.where(live_row, holder_row // lanes, -1)
    region_column = as_column(region_row)
    region_rank = count((region_column == region_row) & after, 1)
    local_column, member_column = as_column(local_row), as_column(jnp.where(live_row, holder_row % lanes, 0))
    place = iota((slots, LANES), 0)
    slot_row, slot_region = place % capacity, place // (capacity * lanes)
    pad = jnp.zeros((1, LANES - entries), jnp.float32)
    notes = jnp.where(lane == entries, windows, 0.0)
    most = jnp.zeros((1, 1), jnp.int32)
    live_ref[...] = jnp.zeros(live_ref.shape, jnp.int32)
    for region in range(regions):
        listed = (region_column == region) & (region_rank == iota((entries, entries), 1))
        pick = lambda column: jnp.sum(
            jnp.where(listed, column, 0).astype(jnp.float32), axis=0, keepdims=True
        )
        amount = count(region_row == region, 1)
        most = jnp.maximum(most, amount)
        live_ref[:, region : region + 1] = amount
        locals_row = jnp.concatenate([pick(local_column + 1) - 1.0, pad], axis=1)
        members_row = jnp.concatenate([pick(member_column), pad], axis=1)
        here = (slot_region == region) & (lane < entries)
        notes = jnp.where(here & (slot_row == 0), locals_row, notes)
        notes = jnp.where(here & (slot_row == 1), members_row, notes)
    notes = jnp.where(lane == entries + 1, most.astype(jnp.float32), notes)
    notes_ref[...] = notes.astype(jnp.bfloat16)
    request_ref[...] = jnp.zeros(request_ref.shape, jnp.int32)


def embed_and_route(
    patches, w_patch, vit_gain, row_owner, window_slot, block_table, capacity, slots, per_owner, blocks_dev, lanes
):
    rows, patch = patches.shape
    vit = w_patch.shape[1]
    entries = block_table.shape[1]
    width = 2 * LANES
    whole = lambda *shape: pl.BlockSpec(shape, lambda step: (0,) * len(shape))
    return pl.pallas_call(
        functools.partial(embed_kernel, capacity, per_owner, blocks_dev, lanes),
        grid=(vit // width,),
        out_shape=(
            jax.ShapeDtypeStruct((slots, vit + LANES), jnp.bfloat16),
            jax.ShapeDtypeStruct((rows, 1), jnp.int32),
            jax.ShapeDtypeStruct((1, entries), jnp.int32),
            jax.ShapeDtypeStruct((1, LANES), jnp.int32),
        ),
        in_specs=[
            whole(patch, rows),
            pl.BlockSpec((patch, width), lambda step: (0, step)),
            whole(1, vit),
            whole(1, rows),
            whole(1, rows),
            whole(1, entries),
        ],
        out_specs=(whole(slots, vit + LANES), whole(rows, 1), whole(1, entries), whole(1, LANES)),
        scratch_shapes=[pltpu.VMEM((rows, patch), jnp.bfloat16), pltpu.VMEM((rows, vit), jnp.bfloat16)],
        compiler_params=pltpu.CompilerParams(vmem_limit_bytes=VMEM_BYTES),
        cost_estimate=pl.CostEstimate(
            flops=2 * rows * patch * vit + 2 * slots * rows * vit,
            bytes_accessed=2 * patch * vit + 2 * rows * patch + 2 * slots * vit,
            transcendentals=rows,
        ),
        name="embed_and_route",
    )(
        patches.T, w_patch, vit_gain.reshape(1, vit), row_owner.reshape(1, rows),
        window_slot.reshape(1, rows), block_table,
    )


def prompt_groups(query_ref, tile):
    tokens = query_ref.shape[0]
    group_size = QHEADS // KVH
    tile_rows = HEADS_TILE * tokens

    def group_step(group, carry):
        for part in range(group_size // HEADS_TILE):
            head = group * group_size + part * HEADS_TILE
            queries = jnp.concatenate(
                [
                    query_ref[:, pl.ds(pl.multiple_of((head + i) * HD, HD), HD)]
                    for i in range(HEADS_TILE)
                ],
                axis=0,
            )
            tile(group, queries, pl.ds(pl.multiple_of(head * tokens, tile_rows), tile_rows))
        return carry

    lax.fori_loop(0, KVH, group_step, 0)


def prompt_scores(queries, keys):
    return lax.dot_general(
        queries, keys, (((1,), (1,)), ((), ())), preferred_element_type=jnp.float32
    ) * (HD ** (-0.5) * LOG2E)


def with_ones(values):
    return jnp.concatenate([values, jnp.ones_like(values)], axis=1)


def head_columns(head):
    return pl.ds(pl.multiple_of(head * HD, HD), HD)


def prompt_begin(query_ref, fresh_ref, top_ref, sum_ref):
    tokens = query_ref.shape[0]
    causal = iota((tokens, tokens), 1) <= iota((tokens, tokens), 0)
    causal = jnp.concatenate([causal.astype(jnp.int32)] * HEADS_TILE, axis=0) > 0

    def tile(group, queries, rows):
        keys, values = fresh_ref[:, head_columns(group)], fresh_ref[:, head_columns(KVH + group)]
        scores = jnp.where(causal, prompt_scores(queries, keys), HIDDEN)
        top = jnp.max(scores, axis=1, keepdims=True)
        weights = jnp.exp2(scores - top).astype(jnp.bfloat16)
        top_ref[rows, :] = jnp.broadcast_to(top, (scores.shape[0], HD))
        sum_ref[rows, :] = jnp.dot(weights, with_ones(values), preferred_element_type=jnp.float32)

    prompt_groups(query_ref, tile)


def prompt_add(query_ref, top_ref, sum_ref, take, shown):
    chunk_keys = shown.shape[1]

    def tile(group, queries, rows):
        scores = jnp.where(shown, prompt_scores(queries, take(group)), HIDDEN)
        old_top = top_ref[rows, :]
        top = jnp.maximum(old_top, jnp.max(scores, axis=1, keepdims=True))
        shrink = jnp.exp2(old_top - top)
        weights = jnp.exp2(scores - jnp.concatenate([top] * (chunk_keys // HD), axis=1))
        top_ref[rows, :] = top
        sum_ref[rows, :] = sum_ref[rows, :] * jnp.concatenate([shrink, shrink], axis=1) + jnp.dot(
            weights.astype(jnp.bfloat16), with_ones(take(KVH + group)), preferred_element_type=jnp.float32
        )

    prompt_groups(query_ref, tile)


def prompt_end(out_ref, sum_ref):
    tokens = out_ref.shape[0]

    def finish(head, carry):
        blended = sum_ref[pl.ds(pl.multiple_of(head * tokens, tokens), tokens), :]
        out_ref[:, head_columns(head)] = (blended[:, :HD] / blended[:, HD:]).astype(jnp.bfloat16)
        return carry

    lax.fori_loop(0, QHEADS, finish, 0)


def listed_prompt_kernel(
    request_ref, live_ref, query_ref, fresh_ref, blocks_ref, out_ref, top_ref, sum_ref, kv_ref, sems
):
    block_tokens = kv_ref.shape[1]
    chunk_keys = CHUNK_BLOCKS * block_tokens
    live_blocks = live_ref[0, 0]
    chunks = (live_blocks + (CHUNK_BLOCKS - 1)) // CHUNK_BLOCKS

    def fetch(chunk, carry):
        def one(place, inner):
            entry = chunk * CHUNK_BLOCKS + place
            pltpu.make_async_copy(
                blocks_ref.at[request_ref[0, entry]], kv_ref.at[entry], sems.at[chunk]
            ).start()
            return inner

        return lax.fori_loop(0, CHUNK_BLOCKS, one, carry)

    lax.fori_loop(0, chunks, fetch, 0)
    prompt_begin(query_ref, fresh_ref, top_ref, sum_ref)

    def visit(chunk, carry):
        first = chunk * CHUNK_BLOCKS
        pltpu.make_async_copy(
            blocks_ref.at[pl.ds(0, CHUNK_BLOCKS)], kv_ref.at[pl.ds(first, CHUNK_BLOCKS)], sems.at[chunk]
        ).wait()
        shown = iota((1, chunk_keys), 1) < (live_blocks - first) * block_tokens
        take = lambda head: kv_ref[pl.ds(first, CHUNK_BLOCKS), :, head_columns(head)].reshape(chunk_keys, HD)
        prompt_add(query_ref, top_ref, sum_ref, take, shown)
        return carry

    lax.fori_loop(0, chunks, visit, 0)
    prompt_end(out_ref, sum_ref)


def striped_prompt_kernel(
    lanes, live_ref, query_ref, fresh_ref, target_ref, striped_ref, out_ref, vision_ref, top_ref, sum_ref
):
    extra = vision_ref.shape[1] // LANES
    regions, room, block_tokens = striped_ref.shape[0] // lanes, striped_ref.shape[1] - extra, striped_ref.shape[2]
    chunk_keys = CHUNK_BLOCKS * block_tokens
    prompt_begin(query_ref, fresh_ref, top_ref, sum_ref)
    chunks = [(live_ref[0, region] + (CHUNK_BLOCKS - 1)) // CHUNK_BLOCKS for region in range(regions)]

    def visit(turn, carry):
        region = (turn >= chunks[0]).astype(jnp.int32)
        chunk = turn - region * chunks[0]
        first = jnp.minimum(chunk * CHUNK_BLOCKS, room - CHUNK_BLOCKS)
        key = iota((1, chunk_keys), 1)
        shown = (key < (live_ref[0, region] - first) * block_tokens) & (
            key >= (chunk * CHUNK_BLOCKS - first) * block_tokens
        )
        take = lambda lane: striped_ref[region * lanes + lane, pl.ds(first, CHUNK_BLOCKS)].reshape(chunk_keys, HD)
        prompt_add(query_ref, top_ref, sum_ref, take, shown)
        return carry

    lax.fori_loop(0, chunks[0] + chunks[1], visit, 0)
    prompt_end(out_ref, sum_ref)
    rows, slots = target_ref.shape[0], striped_ref.shape[0] * block_tokens
    picked = (target_ref[...] == iota((rows, slots), 1)).astype(jnp.bfloat16)
    for tile in range(extra):
        vision_ref[:, tile * LANES : (tile + 1) * LANES] = jnp.dot(
            picked, striped_ref[:, room + tile].reshape(slots, LANES), preferred_element_type=jnp.float32
        ).astype(jnp.bfloat16)


def prompt_attention(kernel, scalars, operands, specs, outs, scratch, keys, name):
    tokens, width = operands[0].shape
    kv_width = operands[1].shape[1]
    whole = lambda shape: pl.BlockSpec(shape, lambda *_: (0,) * len(shape))
    outs = [(tokens, width)] + outs
    return pl.pallas_call(
        kernel,
        out_shape=tuple(jax.ShapeDtypeStruct(shape, jnp.bfloat16) for shape in outs),
        grid_spec=pltpu.PrefetchScalarGridSpec(
            num_scalar_prefetch=len(scalars),
            grid=(1,),
            in_specs=[spec or whole(operand.shape) for operand, spec in zip(operands, specs)],
            out_specs=tuple(whole(shape) for shape in outs),
            scratch_shapes=[
                pltpu.VMEM((QHEADS * tokens, HD), jnp.float32),
                pltpu.VMEM((QHEADS * tokens, 2 * HD), jnp.float32),
            ]
            + scratch,
        ),
        compiler_params=pltpu.CompilerParams(vmem_limit_bytes=VMEM_BYTES),
        cost_estimate=pl.CostEstimate(
            flops=4 * tokens * keys * width,
            bytes_accessed=4 * tokens * width + 2 * keys * kv_width,
            transcendentals=tokens * QHEADS * keys,
        ),
        name=name,
    )(*scalars, *operands)


def listed_prompt(request, live, queries, new_kv, blocks):
    entries, block_tokens = request.shape[1], blocks.shape[1]
    chunks = -(-entries // CHUNK_BLOCKS)
    scratch = [
        pltpu.VMEM((chunks * CHUNK_BLOCKS, block_tokens, new_kv.shape[1]), jnp.bfloat16),
        pltpu.SemaphoreType.DMA((chunks,)),
    ]
    return prompt_attention(
        listed_prompt_kernel, (request, live), (queries, new_kv, blocks),
        (None, None, pl.BlockSpec(memory_space=pl.ANY)), [], scratch,
        entries * block_tokens + queries.shape[0], "listed_prompt",
    )[0]


def striped_prompt(lanes, extra, live, queries, new_kv, target, striped):
    keys = striped.shape[1] * striped.shape[2] + queries.shape[0]
    return prompt_attention(
        functools.partial(striped_prompt_kernel, lanes), (live,), (queries, new_kv, target, striped),
        (None,) * 4, [(target.shape[0], extra * LANES)], [], keys, "striped_prompt",
    )


def stripe_kernel(lanes, steps, cache_ref, *refs):
    out_refs, sems = refs[:-1], refs[-1]
    member = lax.axis_index("seq") % lanes
    copies = []
    for place, step in enumerate(steps):
        column = pl.multiple_of((member ^ step) * LANES, LANES)
        copies.append(pltpu.make_async_copy(cache_ref.at[:, :, pl.ds(column, LANES)], out_refs[place], sems.at[place]))
        copies[-1].start()
    for copy in copies:
        copy.wait()


def stripe(lanes, steps, kv_cache):
    blocks, block_tokens, _ = kv_cache.shape
    piece = jax.ShapeDtypeStruct((blocks, block_tokens, LANES), jnp.bfloat16)
    return pl.pallas_call(
        functools.partial(stripe_kernel, lanes, steps),
        out_shape=(piece,) * len(steps),
        in_specs=[pl.BlockSpec(memory_space=pltpu.VMEM)],
        out_specs=(pl.BlockSpec(memory_space=pl.ANY),) * len(steps),
        scratch_shapes=[pltpu.SemaphoreType.DMA((len(steps),))],
        compiler_params=pltpu.CompilerParams(vmem_limit_bytes=VMEM_BYTES),
        name="stripe",
    )(kv_cache)


def gather_kernel(lanes, steps, entries, notes_ref, attended_ref, *refs):
    piece_refs = refs[:lanes]
    out_ref, held_ref, wide_ref, index_ref, scalar_ref, sems = refs[lanes:]
    blocks = piece_refs[0].shape[0]
    readers, extra = attended_ref.shape[0], attended_ref.shape[1]
    room = out_ref.shape[1] - extra
    capacity = notes_ref.shape[0] // readers
    copies = [
        pltpu.make_async_copy(piece_ref, held_ref.at[pl.ds(step * blocks, blocks)], sems.at[step])
        for step, piece_ref in zip(steps, piece_refs)
    ]
    for copy in copies:
        copy.start()

    wide_ref[...] = notes_ref[...].astype(jnp.float32)
    local = wide_ref[pl.ds(0, readers, capacity), :]
    member = wide_ref[pl.ds(1, readers, capacity), :]
    lane = iota((readers, LANES), 1)
    listed = (local >= 0.0) & (lane < entries)
    step = member.astype(jnp.int32) ^ (lax.axis_index("seq") % lanes)
    amount = jnp.sum(listed.astype(jnp.float32), axis=1, keepdims=True).astype(jnp.int32)
    index = jnp.where(listed, step * blocks + local.astype(jnp.int32), 0)
    index_ref[...] = jnp.where(lane == entries, amount, index)
    to_scalars = pltpu.make_async_copy(index_ref, scalar_ref, sems.at[lanes])
    to_scalars.start()
    out_ref[:, room:] = attended_ref[...]
    to_scalars.wait()
    for copy in copies:
        copy.wait()

    def reader(number, carry):
        chunks = (scalar_ref[number, entries] + (CHUNK_BLOCKS - 1)) // CHUNK_BLOCKS
        groups = jnp.minimum(chunks * (CHUNK_BLOCKS // ROOM_STEP), room // ROOM_STEP)

        def some(group, inner):
            first = group * ROOM_STEP
            tiles = [held_ref[scalar_ref[number, first + i]] for i in range(ROOM_STEP)]
            for i, tile in enumerate(tiles):
                out_ref[number, first + i] = tile
            return inner

        return lax.fori_loop(0, groups, some, carry)

    lax.fori_loop(0, readers, reader, 0)


def gather_stripes(lanes, steps, room, entries, arrived, attended, pieces):
    blocks, block_tokens, _ = pieces[0].shape
    slots = arrived.shape[0]
    last = arrived.shape[1] // LANES - 1
    readers, extra = attended.shape[:2]
    shape = (readers, room + extra, block_tokens, LANES)
    return pl.pallas_call(
        functools.partial(gather_kernel, lanes, steps, entries),
        out_shape=jax.ShapeDtypeStruct(shape, jnp.bfloat16),
        grid=(1,),
        in_specs=[
            pl.BlockSpec((slots, LANES), lambda _: (0, last)),
            pl.BlockSpec(attended.shape, lambda _: (0,) * 4),
        ]
        + [pl.BlockSpec(memory_space=pl.ANY)] * lanes,
        out_specs=pl.BlockSpec(shape, lambda _: (0,) * 4),
        scratch_shapes=[
            pltpu.VMEM((lanes * blocks, block_tokens, LANES), jnp.bfloat16),
            pltpu.VMEM((slots, LANES), jnp.float32),
            pltpu.VMEM((readers, LANES), jnp.int32),
            pltpu.SMEM((readers, LANES), jnp.int32),
            pltpu.SemaphoreType.DMA((lanes + 1,)),
        ],
        compiler_params=pltpu.CompilerParams(vmem_limit_bytes=VMEM_BYTES),
        cost_estimate=pl.CostEstimate(
            flops=0, bytes_accessed=4 * readers * room * block_tokens * LANES, transcendentals=0
        ),
        name="gather_stripes",
    )(arrived, attended, *pieces)


def vision_kernel(entries, rows_ref, w_ref, out_ref, qkv_ref, blend_ref):
    slots, vit = rows_ref.shape[0], w_ref.shape[0]
    inner = VHEADS * VHD
    qkv_ref[...] = jnp.dot(
        rows_ref[:, :vit], w_ref[...], preferred_element_type=jnp.float32
    ).astype(jnp.bfloat16)
    notes = rows_ref[:, vit:].astype(jnp.float32)
    window_column = jnp.sum(
        jnp.where(iota((slots, LANES), 1) == entries, notes, 0.0), axis=1, keepdims=True
    ).astype(jnp.int32)
    window_row = as_row(window_column)
    itself = iota((slots, slots), 0) == iota((slots, slots), 1)
    allowed = ((window_column == window_row) & (window_row >= 0)) | itself
    blend_ref[...] = jnp.zeros_like(blend_ref)
    for head in range(VHEADS):
        first, last = head * VHD, (head + 1) * VHD
        low, high = first // LANES * LANES, -(-last // LANES) * LANES
        column = low + iota((slots, high - low), 1)
        mine = (column >= first) & (column < last)
        part = lambda offset: qkv_ref[:, offset + low : offset + high]
        keys = jnp.where(mine, part(inner).astype(jnp.float32), 0.0).astype(jnp.bfloat16)
        values = jnp.where(mine, part(2 * inner).astype(jnp.float32), 0.0).astype(jnp.bfloat16)
        scores = lax.dot_general(
            part(0), keys, (((1,), (1,)), ((), ())), preferred_element_type=jnp.float32
        ) * VHD ** (-0.5)
        scores = jnp.where(allowed, scores, HIDDEN)
        weights = jnp.exp(scores - jnp.max(scores, axis=1, keepdims=True))
        total = jnp.sum(weights, axis=1, keepdims=True)
        blended = jnp.dot(weights.astype(jnp.bfloat16), values, preferred_element_type=jnp.float32)
        blend_ref[:, low:high] += blended / total
    devices, tiles, rows, _ = out_ref.shape
    for tile in range(tiles):
        part = blend_ref[:, tile * LANES : (tile + 1) * LANES].astype(jnp.bfloat16)
        out_ref[:, tile] = part.reshape(devices, rows, LANES)


def vision_tiles(devices, entries, arrived, w_qkv):
    slots = arrived.shape[0]
    vit, width = w_qkv.shape
    inner = VHEADS * VHD
    return pl.pallas_call(
        functools.partial(vision_kernel, entries),
        out_shape=jax.ShapeDtypeStruct((devices, inner // LANES, slots // devices, LANES), jnp.bfloat16),
        scratch_shapes=[pltpu.VMEM((slots, width), jnp.bfloat16), pltpu.VMEM((slots, inner), jnp.float32)],
        compiler_params=pltpu.CompilerParams(vmem_limit_bytes=VMEM_BYTES),
        cost_estimate=pl.CostEstimate(
            flops=2 * slots * vit * width + 4 * slots * slots * inner,
            bytes_accessed=2 * vit * width,
            transcendentals=VHEADS * slots * slots,
        ),
        name="vision_tiles",
    )(arrived, w_qkv)


def pick_kernel(target_ref, *refs):
    out_ref = refs[-1]
    returned = jnp.concatenate([ref[...] for ref in refs[:-1]], axis=0)
    rows, slots = target_ref.shape[0], returned.shape[0]
    picked = (target_ref[...] == iota((rows, slots), 1)).astype(jnp.bfloat16)
    out_ref[...] = jnp.dot(picked, returned, preferred_element_type=jnp.float32).astype(jnp.bfloat16)


def pick_rows(target, *returned):
    return pl.pallas_call(
        pick_kernel,
        out_shape=jax.ShapeDtypeStruct((target.shape[0], returned[0].shape[1]), jnp.bfloat16),
        compiler_params=pltpu.CompilerParams(vmem_limit_bytes=VMEM_BYTES),
        name="pick_rows",
    )(target, *returned)


def window_attention(qkv_rows, windows):
    total_rows = qkv_rows.shape[0]
    inner_width = VHEADS * VHD
    query_heads = qkv_rows[:, :inner_width].reshape(total_rows, VHEADS, VHD)
    key_heads = qkv_rows[:, inner_width : 2 * inner_width].reshape(total_rows, VHEADS, VHD)
    value_heads = qkv_rows[:, 2 * inner_width :].reshape(total_rows, VHEADS, VHD)
    is_live = windows >= 0
    every_row = jnp.arange(total_rows)
    scores = jnp.einsum(
        "qhd,khd->hqk", query_heads, key_heads, preferred_element_type=jnp.float32
    ) * VHD ** (-0.5)
    allowed = (windows[:, None] == windows[None, :]) & is_live[None, :] | (
        every_row[:, None] == every_row[None, :]
    )
    scores = jnp.where(allowed[None], scores, -jnp.inf)
    highest = jnp.max(scores, axis=2, keepdims=True)
    weights = jnp.exp(scores - highest)
    totals = jnp.sum(weights, axis=2)
    blended = jnp.einsum(
        "hqk,khd->qhd",
        weights.astype(jnp.bfloat16),
        value_heads,
        preferred_element_type=jnp.float32,
    )
    pieces = (blended / totals.T[:, :, None]).reshape(total_rows, inner_width)
    return pieces.astype(jnp.bfloat16)


def exchange(rows, devices):
    parts = rows.reshape((devices, rows.shape[0] // devices) + rows.shape[1:])
    return lax.all_to_all(parts, "seq", split_axis=0, concat_axis=0, tiled=True).reshape(rows.shape)


def swap(piece, step, devices):
    return lax.ppermute(piece, "seq", [(i, i ^ step) for i in range(devices)])


def vision_rows(arrived, windows, w_qkv):
    vit = w_qkv.shape[0]
    qkv_rows = jnp.dot(arrived[:, :vit], w_qkv, preferred_element_type=jnp.float32).astype(jnp.bfloat16)
    return window_attention(qkv_rows, windows)


def shards(
    patches,
    row_owner,
    window_slot,
    w_patch,
    vit_gain,
    w_qkv,
    queries,
    new_kv,
    kv_cache,
    block_table,
):
    devices = lax.axis_size("seq")
    vit = w_patch.shape[1]
    capacity = 2 * patches.shape[0] // devices
    slots = devices * capacity
    entries = block_table.shape[1]
    per_owner = 2 * entries // devices
    blocks_dev = kv_cache.shape[0]
    lanes = kv_cache.shape[2] // LANES
    striped = devices == 2 * lanes and capacity >= 3 and entries + 2 <= LANES
    if striped:
        steps = sorted(range(lanes), key=lambda step: (step < lanes // 2, step == 0))
        pieces, block_table = lax.optimization_barrier((stripe(lanes, steps, kv_cache), block_table))
        pieces = [swap(piece, step, devices) if step else piece for step, piece in zip(steps, pieces)]
    payload, target, request, live = embed_and_route(
        patches, w_patch, vit_gain, row_owner, window_slot, block_table,
        capacity, slots, per_owner, blocks_dev, lanes if striped else None,
    )
    arrived = exchange(payload, devices)

    if not striped:
        notes = arrived[:, vit : vit + 2].astype(jnp.int32)
        asked = notes[:, 1].reshape(devices, capacity)[:, :per_owner].reshape(devices * per_owner)
        delivered = exchange(kv_cache[jnp.maximum(asked, 0)], devices)
        attended = vision_rows(arrived, notes[:, 0], w_qkv)
        delivered, attended = lax.optimization_barrier((delivered, attended))
        returned = exchange(attended, devices)
        attention_out = listed_prompt(request, live, queries, new_kv, delivered)
        return (pick_rows(target, returned), attention_out)

    most = jnp.max(arrived[:, vit + entries + 1].astype(jnp.float32))
    attended = vision_tiles(devices, entries, arrived, w_qkv)

    def finish(room):
        def run(arrived, attended, target, live, queries, new_kv, *pieces):
            outgoing = gather_stripes(lanes, steps, room, entries, arrived, attended, pieces)
            delivered = exchange(outgoing.reshape((-1,) + outgoing.shape[2:]), devices).reshape(outgoing.shape)
            attention_out, vision_out = striped_prompt(
                lanes, attended.shape[1], live, queries, new_kv, target, delivered
            )
            return (vision_out, attention_out)

        return run

    rooms = [room for room in (32, 40, 48, 56) if room < entries] + [entries]
    choice = sum((most > room).astype(jnp.int32) for room in rooms[:-1])
    return lax.switch(
        choice, [finish(room) for room in rooms], arrived, attended, target, live, queries, new_kv, *pieces
    )


def solution(mesh):
    in_specs = (
        P(("groups", "seq"), None),
        P(("groups", "seq"), None),
        P(("groups", "seq")),
        P(),
        P(),
        P(),
        P(("groups", "seq"), None),
        P(("groups", "seq"), None),
        P(("groups", "seq"), None, None),
        P(("groups", "seq"), None),
    )
    out_specs = (P(("groups", "seq"), None), P(("groups", "seq"), None))
    return jax.shard_map(shards, mesh=mesh, in_specs=in_specs, out_specs=out_specs, check_vma=False)
```

```python
import functools

import jax
import jax.numpy as jnp
from jax import lax
from jax.experimental import pallas as pl
from jax.experimental.pallas import tpu as pltpu
from jax.sharding import PartitionSpec as P

VHEADS = 8
VHD = 80
QHEADS = 32
KVH = 4
HD = 128
LANES = 128
CHUNK_BLOCKS = 16
HEADS_TILE = 2
LOG2E = 1.4426950408889634
HIDDEN = -1e30
VMEM_BYTES = 56 * 1024 * 1024
ROOM_STEP = 8
EARLY_STEPS = (4, 5, 2, 3)


def iota(shape, axis):
    return lax.broadcasted_iota(jnp.int32, shape, axis)


def count(hits, axis):
    return jnp.sum(hits.astype(jnp.float32), axis=axis, keepdims=True).astype(jnp.int32)


def as_row(column):
    size = column.shape[0]
    diagonal = iota((size, size), 0) == iota((size, size), 1)
    return jnp.sum(jnp.where(diagonal, column, 0).astype(jnp.float32), axis=0, keepdims=True).astype(jnp.int32)


def as_column(row):
    size = row.shape[1]
    diagonal = iota((size, size), 0) == iota((size, size), 1)
    return jnp.sum(jnp.where(diagonal, row, 0).astype(jnp.float32), axis=1, keepdims=True).astype(jnp.int32)


def embed_kernel(
    capacity,
    per_owner,
    blocks_dev,
    lanes,
    patches_ref,
    w_ref,
    gain_ref,
    owner_ref,
    window_ref,
    table_ref,
    payload_ref,
    target_ref,
    request_ref,
    live_ref,
    turned_ref,
    embedded_ref,
):
    step = pl.program_id(0)
    width = w_ref.shape[1]

    @pl.when(step == 0)
    def _():
        turned_ref[...] = patches_ref[...].T

    piece = jnp.dot(turned_ref[...], w_ref[...], preferred_element_type=jnp.float32)
    embedded_ref[:, pl.ds(pl.multiple_of(step * width, width), width)] = piece.astype(jnp.bfloat16)

    @pl.when(step == pl.num_programs(0) - 1)
    def _():
        slots = payload_ref.shape[0]
        vit = embedded_ref.shape[1]
        rows = owner_ref.shape[1]
        owner_row = owner_ref[...]
        owner_column = as_column(owner_row)
        same = owner_column == owner_row
        first, second = iota((rows, rows), 0), iota((rows, rows), 1)
        rank_row = count(same & (first < second), 0)
        rank_column = count(same & (second < first), 1)
        target_ref[...] = owner_column * capacity + rank_column
        placed = (owner_row * capacity + rank_row) == iota((slots, rows), 0)
        windows = (
            jnp.sum(jnp.where(placed, window_ref[...] + 1, 0).astype(jnp.float32), axis=1, keepdims=True)
            - 1.0
        )
        note_list(capacity, per_owner, blocks_dev, lanes, windows, table_ref, payload_ref.at[:, vit:], request_ref, live_ref)

        widened = embedded_ref[...].astype(jnp.float32)
        factor = lax.rsqrt(jnp.mean(widened * widened, axis=1, keepdims=True) + 1e-06)
        normed = (widened * factor * gain_ref[...].reshape(1, -1)).astype(jnp.bfloat16)
        payload_ref[:, :vit] = jnp.dot(
            placed.astype(jnp.bfloat16), normed, preferred_element_type=jnp.float32
        ).astype(jnp.bfloat16)


def note_list(capacity, per_owner, blocks_dev, lanes, windows, table_ref, notes_ref, request_ref, live_ref):
    slots = notes_ref.shape[0]
    table_row = table_ref[...]
    entries = table_row.shape[1]
    live_row = table_row >= 0
    holder_row = jnp.where(live_row, table_row // blocks_dev, -1)
    local_row = jnp.where(live_row, table_row % blocks_dev, 0)
    lane = iota((slots, LANES), 1)
    before = iota((entries, entries), 0) < iota((entries, entries), 1)
    if lanes is None:
        holder_rank = count((as_column(holder_row) == holder_row) & before, 0)
        request_row = jnp.where(live_row, holder_row * per_owner + holder_rank, -1)
        first_request = jnp.sum(
            jnp.where(iota((1, entries), 1) == 0, request_row, 0).astype(jnp.float32), axis=1, keepdims=True
        ).astype(jnp.int32)
        request_ref[...] = jnp.where(live_row, request_row, first_request)
        live_ref[...] = jnp.broadcast_to(count(live_row, 1), live_ref.shape)
        placed_row = jnp.where(live_row, holder_row * capacity + holder_rank, -1)
        asked = jnp.sum(
            jnp.where(placed_row == iota((slots, entries), 0), local_row + 1, 0).astype(jnp.float32),
            axis=1,
            keepdims=True,
        )
        notes = jnp.where(lane == 0, windows, jnp.where(lane == 1, asked - 1.0, 0.0))
        notes_ref[...] = notes.astype(jnp.bfloat16)
        return
    regions = slots // capacity // lanes
    after = iota((entries, entries), 1) < iota((entries, entries), 0)
    region_row = jnp.where(live_row, holder_row // lanes, -1)
    region_column = as_column(region_row)
    region_rank = count((region_column == region_row) & after, 1)
    local_column, member_column = as_column(local_row), as_column(jnp.where(live_row, holder_row % lanes, 0))
    place = iota((slots, LANES), 0)
    slot_row, slot_region = place % capacity, place // (capacity * lanes)
    pad = jnp.zeros((1, LANES - entries), jnp.float32)
    notes = jnp.where(lane == entries, windows, 0.0)
    most = jnp.zeros((1, 1), jnp.int32)
    live_ref[...] = jnp.zeros(live_ref.shape, jnp.int32)
    for region in range(regions):
        listed = (region_column == region) & (region_rank == iota((entries, entries), 1))
        pick = lambda column: jnp.sum(
            jnp.where(listed, column, 0).astype(jnp.float32), axis=0, keepdims=True
        )
        amount = count(region_row == region, 1)
        most = jnp.maximum(most, amount)
        live_ref[:, region : region + 1] = amount
        locals_row = jnp.concatenate([pick(local_column + 1) - 1.0, pad], axis=1)
        members_row = jnp.concatenate([pick(member_column), pad], axis=1)
        here = (slot_region == region) & (lane < entries)
        notes = jnp.where(here & (slot_row == 0), locals_row, notes)
        notes = jnp.where(here & (slot_row == 1), members_row, notes)
    notes = jnp.where(lane == entries + 1, most.astype(jnp.float32), notes)
    notes_ref[...] = notes.astype(jnp.bfloat16)
    request_ref[...] = jnp.zeros(request_ref.shape, jnp.int32)


def embed_and_route(
    patches, w_patch, vit_gain, row_owner, window_slot, block_table, capacity, slots, per_owner, blocks_dev, lanes
):
    rows, patch = patches.shape
    vit = w_patch.shape[1]
    entries = block_table.shape[1]
    width = vit // 2
    whole = lambda *shape: pl.BlockSpec(shape, lambda step: (0,) * len(shape))
    return pl.pallas_call(
        functools.partial(embed_kernel, capacity, per_owner, blocks_dev, lanes),
        grid=(vit // width,),
        out_shape=(
            jax.ShapeDtypeStruct((slots, vit + LANES), jnp.bfloat16),
            jax.ShapeDtypeStruct((rows, 1), jnp.int32),
            jax.ShapeDtypeStruct((1, entries), jnp.int32),
            jax.ShapeDtypeStruct((1, LANES), jnp.int32),
        ),
        in_specs=[
            whole(patch, rows),
            pl.BlockSpec((patch, width), lambda step: (0, step)),
            whole(vit),
            whole(1, rows),
            whole(1, rows),
            whole(1, entries),
        ],
        out_specs=(whole(slots, vit + LANES), whole(rows, 1), whole(1, entries), whole(1, LANES)),
        scratch_shapes=[pltpu.VMEM((rows, patch), jnp.bfloat16), pltpu.VMEM((rows, vit), jnp.bfloat16)],
        compiler_params=pltpu.CompilerParams(vmem_limit_bytes=VMEM_BYTES),
        cost_estimate=pl.CostEstimate(
            flops=2 * rows * patch * vit + 2 * slots * rows * vit,
            bytes_accessed=2 * patch * vit + 2 * rows * patch + 2 * slots * vit,
            transcendentals=rows,
        ),
        name="embed_and_route",
    )(
        patches.T, w_patch, vit_gain, row_owner.reshape(1, rows),
        window_slot.reshape(1, rows), block_table,
    )


def prompt_groups(query_ref, tile):
    tokens = query_ref.shape[0]
    group_size = QHEADS // KVH
    tile_rows = HEADS_TILE * tokens

    def group_step(group, carry):
        for part in range(group_size // HEADS_TILE):
            head = group * group_size + part * HEADS_TILE
            queries = jnp.concatenate(
                [
                    query_ref[:, pl.ds(pl.multiple_of((head + i) * HD, HD), HD)]
                    for i in range(HEADS_TILE)
                ],
                axis=0,
            )
            tile(group, queries, pl.ds(pl.multiple_of(head * tokens, tile_rows), tile_rows))
        return carry

    lax.fori_loop(0, KVH, group_step, 0)


def prompt_scores(queries, keys):
    return lax.dot_general(
        queries, keys, (((1,), (1,)), ((), ())), preferred_element_type=jnp.float32
    ) * (HD ** (-0.5) * LOG2E)


def with_ones(values):
    return jnp.concatenate([values, jnp.ones_like(values)], axis=1)


def head_columns(head):
    return pl.ds(pl.multiple_of(head * HD, HD), HD)


def prompt_begin(query_ref, fresh_ref, top_ref, sum_ref):
    tokens = query_ref.shape[0]
    causal = iota((tokens, tokens), 1) <= iota((tokens, tokens), 0)
    causal = jnp.concatenate([causal.astype(jnp.int32)] * HEADS_TILE, axis=0) > 0

    def tile(group, queries, rows):
        keys, values = fresh_ref[:, head_columns(group)], fresh_ref[:, head_columns(KVH + group)]
        scores = jnp.where(causal, prompt_scores(queries, keys), HIDDEN)
        top = jnp.max(scores, axis=1, keepdims=True)
        weights = jnp.exp2(scores - top).astype(jnp.bfloat16)
        top_ref[rows, :] = jnp.broadcast_to(top, (scores.shape[0], HD))
        sum_ref[rows, :] = jnp.dot(weights, with_ones(values), preferred_element_type=jnp.float32)

    prompt_groups(query_ref, tile)


def prompt_add(query_ref, top_ref, sum_ref, take, shown):
    chunk_keys = shown.shape[1]

    def tile(group, queries, rows):
        scores = jnp.where(shown, prompt_scores(queries, take(group)), HIDDEN)
        old_top = top_ref[rows, :]
        top = jnp.maximum(old_top, jnp.max(scores, axis=1, keepdims=True))
        shrink = jnp.exp2(old_top - top)
        weights = jnp.exp2(scores - jnp.concatenate([top] * (chunk_keys // HD), axis=1))
        top_ref[rows, :] = top
        sum_ref[rows, :] = sum_ref[rows, :] * jnp.concatenate([shrink, shrink], axis=1) + jnp.dot(
            weights.astype(jnp.bfloat16), with_ones(take(KVH + group)), preferred_element_type=jnp.float32
        )

    prompt_groups(query_ref, tile)


def prompt_end(out_ref, sum_ref):
    tokens = out_ref.shape[0]

    def finish(head, carry):
        blended = sum_ref[pl.ds(pl.multiple_of(head * tokens, tokens), tokens), :]
        out_ref[:, head_columns(head)] = (blended[:, :HD] / blended[:, HD:]).astype(jnp.bfloat16)
        return carry

    lax.fori_loop(0, QHEADS, finish, 0)


def listed_prompt_kernel(
    request_ref, live_ref, query_ref, fresh_ref, blocks_ref, out_ref, top_ref, sum_ref, kv_ref, sems
):
    block_tokens = kv_ref.shape[1]
    chunk_keys = CHUNK_BLOCKS * block_tokens
    live_blocks = live_ref[0, 0]
    chunks = (live_blocks + (CHUNK_BLOCKS - 1)) // CHUNK_BLOCKS

    def fetch(chunk, carry):
        def one(place, inner):
            entry = chunk * CHUNK_BLOCKS + place
            pltpu.make_async_copy(
                blocks_ref.at[request_ref[0, entry]], kv_ref.at[entry], sems.at[chunk]
            ).start()
            return inner

        return lax.fori_loop(0, CHUNK_BLOCKS, one, carry)

    lax.fori_loop(0, chunks, fetch, 0)
    prompt_begin(query_ref, fresh_ref, top_ref, sum_ref)

    def visit(chunk, carry):
        first = chunk * CHUNK_BLOCKS
        pltpu.make_async_copy(
            blocks_ref.at[pl.ds(0, CHUNK_BLOCKS)], kv_ref.at[pl.ds(first, CHUNK_BLOCKS)], sems.at[chunk]
        ).wait()
        shown = iota((1, chunk_keys), 1) < (live_blocks - first) * block_tokens
        take = lambda head: kv_ref[pl.ds(first, CHUNK_BLOCKS), :, head_columns(head)].reshape(chunk_keys, HD)
        prompt_add(query_ref, top_ref, sum_ref, take, shown)
        return carry

    lax.fori_loop(0, chunks, visit, 0)
    prompt_end(out_ref, sum_ref)


def striped_prompt_kernel(
    lanes, live_ref, query_ref, fresh_ref, target_ref, striped_ref, out_ref, vision_ref, top_ref, sum_ref
):
    extra = vision_ref.shape[1] // LANES
    regions, room, block_tokens = striped_ref.shape[0] // lanes, striped_ref.shape[1] - extra, striped_ref.shape[2]
    chunk_keys = CHUNK_BLOCKS * block_tokens
    prompt_begin(query_ref, fresh_ref, top_ref, sum_ref)
    chunks = [(live_ref[0, region] + (CHUNK_BLOCKS - 1)) // CHUNK_BLOCKS for region in range(regions)]

    def visit(turn, carry):
        region = (turn >= chunks[0]).astype(jnp.int32)
        chunk = turn - region * chunks[0]
        first = jnp.minimum(chunk * CHUNK_BLOCKS, room - CHUNK_BLOCKS)
        key = iota((1, chunk_keys), 1)
        shown = (key < (live_ref[0, region] - first) * block_tokens) & (
            key >= (chunk * CHUNK_BLOCKS - first) * block_tokens
        )
        take = lambda lane: striped_ref[region * lanes + lane, pl.ds(first, CHUNK_BLOCKS)].reshape(chunk_keys, HD)
        prompt_add(query_ref, top_ref, sum_ref, take, shown)
        return carry

    lax.fori_loop(0, chunks[0] + chunks[1], visit, 0)
    prompt_end(out_ref, sum_ref)
    rows, slots = target_ref.shape[0], striped_ref.shape[0] * block_tokens
    picked = (target_ref[...] == iota((rows, slots), 1)).astype(jnp.bfloat16)
    for tile in range(extra):
        vision_ref[:, tile * LANES : (tile + 1) * LANES] = jnp.dot(
            picked, striped_ref[:, room + tile].reshape(slots, LANES), preferred_element_type=jnp.float32
        ).astype(jnp.bfloat16)


def prompt_attention(kernel, scalars, operands, specs, outs, scratch, keys, name):
    tokens, width = operands[0].shape
    kv_width = operands[1].shape[1]
    whole = lambda shape: pl.BlockSpec(shape, lambda *_: (0,) * len(shape))
    outs = [(tokens, width)] + outs
    return pl.pallas_call(
        kernel,
        out_shape=tuple(jax.ShapeDtypeStruct(shape, jnp.bfloat16) for shape in outs),
        grid_spec=pltpu.PrefetchScalarGridSpec(
            num_scalar_prefetch=len(scalars),
            grid=(1,),
            in_specs=[spec or whole(operand.shape) for operand, spec in zip(operands, specs)],
            out_specs=tuple(whole(shape) for shape in outs),
            scratch_shapes=[
                pltpu.VMEM((QHEADS * tokens, HD), jnp.float32),
                pltpu.VMEM((QHEADS * tokens, 2 * HD), jnp.float32),
            ]
            + scratch,
        ),
        compiler_params=pltpu.CompilerParams(vmem_limit_bytes=VMEM_BYTES),
        cost_estimate=pl.CostEstimate(
            flops=4 * tokens * keys * width,
            bytes_accessed=4 * tokens * width + 2 * keys * kv_width,
            transcendentals=tokens * QHEADS * keys,
        ),
        name=name,
    )(*scalars, *operands)


def listed_prompt(request, live, queries, new_kv, blocks):
    entries, block_tokens = request.shape[1], blocks.shape[1]
    chunks = -(-entries // CHUNK_BLOCKS)
    scratch = [
        pltpu.VMEM((chunks * CHUNK_BLOCKS, block_tokens, new_kv.shape[1]), jnp.bfloat16),
        pltpu.SemaphoreType.DMA((chunks,)),
    ]
    return prompt_attention(
        listed_prompt_kernel, (request, live), (queries, new_kv, blocks),
        (None, None, pl.BlockSpec(memory_space=pl.ANY)), [], scratch,
        entries * block_tokens + queries.shape[0], "listed_prompt",
    )[0]


def striped_prompt(lanes, extra, live, queries, new_kv, target, striped):
    keys = striped.shape[1] * striped.shape[2] + queries.shape[0]
    return prompt_attention(
        functools.partial(striped_prompt_kernel, lanes), (live,), (queries, new_kv, target, striped),
        (None,) * 4, [(target.shape[0], extra * LANES)], [], keys, "striped_prompt",
    )


def stripe_kernel(lanes, steps, cache_ref, *refs):
    out_refs, held_ref, in_sems, out_sems = refs[:-3], refs[-3], refs[-2], refs[-1]
    member = lax.axis_index("seq") % lanes
    chunks = in_sems.shape[0]
    size = cache_ref.shape[0] // chunks
    taken, given = [], []
    for chunk in range(chunks):
        part = pl.ds(chunk * size, size)
        taken.append(pltpu.make_async_copy(cache_ref.at[part], held_ref.at[part], in_sems.at[chunk]))
        taken[-1].start()
    for chunk in range(chunks):
        part = pl.ds(chunk * size, size)
        taken[chunk].wait()
        for place, step in enumerate(steps):
            column = pl.multiple_of((member ^ step) * LANES, LANES)
            given.append(
                pltpu.make_async_copy(
                    held_ref.at[part, :, pl.ds(column, LANES)],
                    out_refs[place].at[part],
                    out_sems.at[chunk, place],
                )
            )
            given[-1].start()
    for copy in given:
        copy.wait()


def stripe(lanes, steps, kv_cache):
    blocks, block_tokens, _ = kv_cache.shape
    chunks = 4
    piece = jax.ShapeDtypeStruct((blocks, block_tokens, LANES), jnp.bfloat16)
    return pl.pallas_call(
        functools.partial(stripe_kernel, lanes, steps),
        out_shape=(piece,) * len(steps),
        in_specs=[pl.BlockSpec(memory_space=pl.ANY)],
        out_specs=(pl.BlockSpec(memory_space=pl.ANY),) * len(steps),
        scratch_shapes=[
            pltpu.VMEM(kv_cache.shape, jnp.bfloat16),
            pltpu.SemaphoreType.DMA((chunks,)),
            pltpu.SemaphoreType.DMA((chunks, len(steps))),
        ],
        compiler_params=pltpu.CompilerParams(vmem_limit_bytes=VMEM_BYTES),
        name="stripe",
    )(kv_cache)


def gather_kernel(lanes, steps, entries, notes_ref, attended_ref, *refs):
    piece_refs = refs[:lanes]
    out_ref, held_ref, ready_ref, wide_ref, index_ref, scalar_ref, sems, out_sems = refs[lanes:]
    blocks = piece_refs[0].shape[0]
    readers, extra = attended_ref.shape[0], attended_ref.shape[1]
    room = out_ref.shape[1] - extra
    capacity = notes_ref.shape[0] // readers
    copies = [
        pltpu.make_async_copy(piece_ref, held_ref.at[pl.ds(step * blocks, blocks)], sems.at[step])
        for step, piece_ref in zip(steps, piece_refs)
    ]
    for copy in copies:
        copy.start()

    wide_ref[...] = notes_ref[...].astype(jnp.float32)
    local = wide_ref[pl.ds(0, readers, capacity), :]
    member = wide_ref[pl.ds(1, readers, capacity), :]
    lane = iota((readers, LANES), 1)
    listed = (local >= 0.0) & (lane < entries)
    step = member.astype(jnp.int32) ^ (lax.axis_index("seq") % lanes)
    amount = jnp.sum(listed.astype(jnp.float32), axis=1, keepdims=True).astype(jnp.int32)
    index = jnp.where(listed, step * blocks + local.astype(jnp.int32), 0)
    index_ref[...] = jnp.where(lane == entries, amount, index)
    to_scalars = pltpu.make_async_copy(index_ref, scalar_ref, sems.at[lanes])
    to_scalars.start()
    result = pltpu.make_async_copy(
        attended_ref, out_ref.at[:, pl.ds(room, extra)], out_sems.at[readers]
    )
    result.start()
    to_scalars.wait()
    for copy in copies:
        copy.wait()

    def reader(number, carry):
        chunks = (scalar_ref[number, entries] + (CHUNK_BLOCKS - 1)) // CHUNK_BLOCKS
        groups = jnp.minimum(chunks * (CHUNK_BLOCKS // ROOM_STEP), room // ROOM_STEP)

        def some(group, inner):
            first = group * ROOM_STEP
            tiles = [held_ref[scalar_ref[number, first + i]] for i in range(ROOM_STEP)]
            for i, tile in enumerate(tiles):
                ready_ref[number, first + i] = tile
            return inner

        lax.fori_loop(0, groups, some, carry)
        pltpu.make_async_copy(
            ready_ref.at[number], out_ref.at[number, pl.ds(0, room)], out_sems.at[number]
        ).start()
        return carry

    lax.fori_loop(0, readers, reader, 0)
    result.wait()
    for number in range(readers):
        pltpu.make_async_copy(
            ready_ref.at[number], out_ref.at[number, pl.ds(0, room)], out_sems.at[number]
        ).wait()


def gather_stripes(lanes, steps, room, entries, arrived, attended, pieces):
    blocks, block_tokens, _ = pieces[0].shape
    slots = arrived.shape[0]
    last = arrived.shape[1] // LANES - 1
    readers, extra = attended.shape[:2]
    shape = (readers, room + extra, block_tokens, LANES)
    return pl.pallas_call(
        functools.partial(gather_kernel, lanes, steps, entries),
        out_shape=jax.ShapeDtypeStruct(shape, jnp.bfloat16),
        grid=(1,),
        in_specs=[
            pl.BlockSpec((slots, LANES), lambda _: (0, last)),
            pl.BlockSpec(attended.shape, lambda _: (0,) * 4),
        ]
        + [pl.BlockSpec(memory_space=pl.ANY)] * lanes,
        out_specs=pl.BlockSpec(memory_space=pl.ANY),
        scratch_shapes=[
            pltpu.VMEM((lanes * blocks, block_tokens, LANES), jnp.bfloat16),
            pltpu.VMEM((readers, room, block_tokens, LANES), jnp.bfloat16),
            pltpu.VMEM((slots, LANES), jnp.float32),
            pltpu.VMEM((readers, LANES), jnp.int32),
            pltpu.SMEM((readers, LANES), jnp.int32),
            pltpu.SemaphoreType.DMA((lanes + 1,)),
            pltpu.SemaphoreType.DMA((readers + 1,)),
        ],
        compiler_params=pltpu.CompilerParams(vmem_limit_bytes=VMEM_BYTES),
        cost_estimate=pl.CostEstimate(
            flops=0, bytes_accessed=4 * readers * room * block_tokens * LANES, transcendentals=0
        ),
        name="gather_stripes",
    )(arrived, attended, *pieces)


def vision_kernel(entries, rows_ref, w_ref, out_ref, qkv_ref, blend_ref):
    slots, vit = rows_ref.shape[0], w_ref.shape[0]
    inner = VHEADS * VHD
    qkv_ref[...] = jnp.dot(
        rows_ref[:, :vit], w_ref[...], preferred_element_type=jnp.float32
    ).astype(jnp.bfloat16)
    notes = rows_ref[:, vit:].astype(jnp.float32)
    window_column = jnp.sum(
        jnp.where(iota((slots, LANES), 1) == entries, notes, 0.0), axis=1, keepdims=True
    ).astype(jnp.int32)
    window_row = as_row(window_column)
    itself = iota((slots, slots), 0) == iota((slots, slots), 1)
    allowed = ((window_column == window_row) & (window_row >= 0)) | itself
    blend_ref[...] = jnp.zeros_like(blend_ref)
    for head in range(VHEADS):
        first, last = head * VHD, (head + 1) * VHD
        low, high = first // LANES * LANES, -(-last // LANES) * LANES
        column = low + iota((slots, high - low), 1)
        mine = (column >= first) & (column < last)
        part = lambda offset: qkv_ref[:, offset + low : offset + high]
        keys = jnp.where(mine, part(inner).astype(jnp.float32), 0.0).astype(jnp.bfloat16)
        values = jnp.where(mine, part(2 * inner).astype(jnp.float32), 0.0).astype(jnp.bfloat16)
        scores = lax.dot_general(
            part(0), keys, (((1,), (1,)), ((), ())), preferred_element_type=jnp.float32
        ) * VHD ** (-0.5)
        scores = jnp.where(allowed, scores, HIDDEN)
        weights = jnp.exp(scores - jnp.max(scores, axis=1, keepdims=True))
        total = jnp.sum(weights, axis=1, keepdims=True)
        blended = jnp.dot(weights.astype(jnp.bfloat16), values, preferred_element_type=jnp.float32)
        blend_ref[:, low:high] += blended / total
    devices, tiles, rows, _ = out_ref.shape
    for tile in range(tiles):
        part = blend_ref[:, tile * LANES : (tile + 1) * LANES].astype(jnp.bfloat16)
        out_ref[:, tile] = part.reshape(devices, rows, LANES)


def vision_tiles(devices, entries, arrived, w_qkv):
    slots = arrived.shape[0]
    vit, width = w_qkv.shape
    inner = VHEADS * VHD
    return pl.pallas_call(
        functools.partial(vision_kernel, entries),
        out_shape=jax.ShapeDtypeStruct((devices, inner // LANES, slots // devices, LANES), jnp.bfloat16),
        scratch_shapes=[pltpu.VMEM((slots, width), jnp.bfloat16), pltpu.VMEM((slots, inner), jnp.float32)],
        compiler_params=pltpu.CompilerParams(vmem_limit_bytes=VMEM_BYTES),
        cost_estimate=pl.CostEstimate(
            flops=2 * slots * vit * width + 4 * slots * slots * inner,
            bytes_accessed=2 * vit * width,
            transcendentals=VHEADS * slots * slots,
        ),
        name="vision_tiles",
    )(arrived, w_qkv)


def pick_kernel(target_ref, *refs):
    out_ref = refs[-1]
    returned = jnp.concatenate([ref[...] for ref in refs[:-1]], axis=0)
    rows, slots = target_ref.shape[0], returned.shape[0]
    picked = (target_ref[...] == iota((rows, slots), 1)).astype(jnp.bfloat16)
    out_ref[...] = jnp.dot(picked, returned, preferred_element_type=jnp.float32).astype(jnp.bfloat16)


def pick_rows(target, *returned):
    return pl.pallas_call(
        pick_kernel,
        out_shape=jax.ShapeDtypeStruct((target.shape[0], returned[0].shape[1]), jnp.bfloat16),
        compiler_params=pltpu.CompilerParams(vmem_limit_bytes=VMEM_BYTES),
        name="pick_rows",
    )(target, *returned)


def window_attention(qkv_rows, windows):
    total_rows = qkv_rows.shape[0]
    inner_width = VHEADS * VHD
    query_heads = qkv_rows[:, :inner_width].reshape(total_rows, VHEADS, VHD)
    key_heads = qkv_rows[:, inner_width : 2 * inner_width].reshape(total_rows, VHEADS, VHD)
    value_heads = qkv_rows[:, 2 * inner_width :].reshape(total_rows, VHEADS, VHD)
    is_live = windows >= 0
    every_row = jnp.arange(total_rows)
    scores = jnp.einsum(
        "qhd,khd->hqk", query_heads, key_heads, preferred_element_type=jnp.float32
    ) * VHD ** (-0.5)
    allowed = (windows[:, None] == windows[None, :]) & is_live[None, :] | (
        every_row[:, None] == every_row[None, :]
    )
    scores = jnp.where(allowed[None], scores, -jnp.inf)
    highest = jnp.max(scores, axis=2, keepdims=True)
    weights = jnp.exp(scores - highest)
    totals = jnp.sum(weights, axis=2)
    blended = jnp.einsum(
        "hqk,khd->qhd",
        weights.astype(jnp.bfloat16),
        value_heads,
        preferred_element_type=jnp.float32,
    )
    pieces = (blended / totals.T[:, :, None]).reshape(total_rows, inner_width)
    return pieces.astype(jnp.bfloat16)


def exchange(rows, devices):
    parts = rows.reshape((devices, rows.shape[0] // devices) + rows.shape[1:])
    return lax.all_to_all(parts, "seq", split_axis=0, concat_axis=0, tiled=True).reshape(rows.shape)


def swap(piece, step, devices):
    return lax.ppermute(piece, "seq", [(i, i ^ step) for i in range(devices)])


def vision_rows(arrived, windows, w_qkv):
    vit = w_qkv.shape[0]
    qkv_rows = jnp.dot(arrived[:, :vit], w_qkv, preferred_element_type=jnp.float32).astype(jnp.bfloat16)
    return window_attention(qkv_rows, windows)


def shards(
    patches,
    row_owner,
    window_slot,
    w_patch,
    vit_gain,
    w_qkv,
    queries,
    new_kv,
    kv_cache,
    block_table,
):
    devices = lax.axis_size("seq")
    vit = w_patch.shape[1]
    capacity = 2 * patches.shape[0] // devices
    slots = devices * capacity
    entries = block_table.shape[1]
    per_owner = 2 * entries // devices
    blocks_dev = kv_cache.shape[0]
    lanes = kv_cache.shape[2] // LANES
    striped = devices == 2 * lanes and capacity == kv_cache.shape[1] and entries + 2 <= LANES
    if striped:
        steps = sorted(range(lanes), key=lambda step: (step not in EARLY_STEPS, step < 2, step == 0))
        pieces, block_table = lax.optimization_barrier((stripe(lanes, steps, kv_cache), block_table))
        pieces = [swap(piece, step, devices) if step else piece for step, piece in zip(steps, pieces)]
        early = [steps.index(step) for step in EARLY_STEPS]
    payload, target, request, live = embed_and_route(
        patches, w_patch, vit_gain, row_owner, window_slot, block_table,
        capacity, slots, per_owner, blocks_dev, lanes if striped else None,
    )
    if striped:
        payload, *done = lax.optimization_barrier((payload, *[pieces[place] for place in early]))
        for place, piece in zip(early, done):
            pieces[place] = piece
    arrived = exchange(payload, devices)

    if not striped:
        notes = arrived[:, vit : vit + 2].astype(jnp.int32)
        asked = notes[:, 1].reshape(devices, capacity)[:, :per_owner].reshape(devices * per_owner)
        delivered = exchange(kv_cache[jnp.maximum(asked, 0)], devices)
        attended = vision_rows(arrived, notes[:, 0], w_qkv)
        delivered, attended = lax.optimization_barrier((delivered, attended))
        returned = exchange(attended, devices)
        attention_out = listed_prompt(request, live, queries, new_kv, delivered)
        return (pick_rows(target, returned), attention_out)

    most = jnp.max(arrived[:, vit + entries + 1].astype(jnp.float32))
    attended = vision_tiles(devices, entries, arrived, w_qkv)

    def finish(room):
        def run(arrived, attended, target, live, queries, new_kv, *pieces):
            outgoing = gather_stripes(lanes, steps, room, entries, arrived, attended, pieces)
            delivered = exchange(outgoing.reshape((-1,) + outgoing.shape[2:]), devices).reshape(outgoing.shape)
            attention_out, vision_out = striped_prompt(
                lanes, attended.shape[1], live, queries, new_kv, target, delivered
            )
            return (vision_out, attention_out)

        return run

    rooms = [room for room in (32, 40, 48, 56) if room < entries] + [entries]
    choice = sum((most > room).astype(jnp.int32) for room in rooms[:-1])
    return lax.switch(
        choice, [finish(room) for room in rooms], arrived, attended, target, live, queries, new_kv, *pieces
    )


def solution(mesh):
    in_specs = (
        P(("groups", "seq"), None),
        P(("groups", "seq"), None),
        P(("groups", "seq")),
        P(),
        P(),
        P(),
        P(("groups", "seq"), None),
        P(("groups", "seq"), None),
        P(("groups", "seq"), None, None),
        P(("groups", "seq"), None),
    )
    out_specs = (P(("groups", "seq"), None), P(("groups", "seq"), None))
    return jax.shard_map(shards, mesh=mesh, in_specs=in_specs, out_specs=out_specs, check_vma=False)
```

```python
import functools

import jax
import jax.numpy as jnp
from jax import lax
from jax.experimental import pallas as pl
from jax.experimental.pallas import tpu as pltpu
from jax.sharding import PartitionSpec as P

VHEADS = 8
VHD = 80
QHEADS = 32
KVH = 4
HD = 128
LANES = 128
CHUNK_BLOCKS = 16
HEADS_TILE = 2
LOG2E = 1.4426950408889634
HIDDEN = -1e30
VMEM_BYTES = 56 * 1024 * 1024
ROOM_STEP = 8
SMALL_VMEM_BYTES = 24 * 1024 * 1024
ROOMS = (28, 32, 36, 40, 48, 64)
EARLY_STEPS = (4, 2)


def iota(shape, axis):
    return lax.broadcasted_iota(jnp.int32, shape, axis)


def count(hits, axis):
    return jnp.sum(hits.astype(jnp.float32), axis=axis, keepdims=True).astype(jnp.int32)


def as_row(column):
    size = column.shape[0]
    diagonal = iota((size, size), 0) == iota((size, size), 1)
    return jnp.sum(jnp.where(diagonal, column, 0).astype(jnp.float32), axis=0, keepdims=True).astype(jnp.int32)


def as_column(row):
    size = row.shape[1]
    diagonal = iota((size, size), 0) == iota((size, size), 1)
    return jnp.sum(jnp.where(diagonal, row, 0).astype(jnp.float32), axis=1, keepdims=True).astype(jnp.int32)


def embed_kernel(
    capacity,
    per_owner,
    blocks_dev,
    lanes,
    patches_ref,
    w_ref,
    gain_ref,
    owner_ref,
    window_ref,
    table_ref,
    payload_ref,
    target_ref,
    request_ref,
    live_ref,
    turned_ref,
    embedded_ref,
):
    step = pl.program_id(0)
    width = w_ref.shape[1]

    @pl.when(step == 0)
    def _():
        turned_ref[...] = patches_ref[...].T

    piece = jnp.dot(turned_ref[...], w_ref[...], preferred_element_type=jnp.float32)
    embedded_ref[:, pl.ds(pl.multiple_of(step * width, width), width)] = piece.astype(jnp.bfloat16)

    @pl.when(step == pl.num_programs(0) - 1)
    def _():
        slots = payload_ref.shape[0]
        vit = embedded_ref.shape[1]
        rows = owner_ref.shape[1]
        owner_row = owner_ref[...]
        owner_column = as_column(owner_row)
        same = owner_column == owner_row
        first, second = iota((rows, rows), 0), iota((rows, rows), 1)
        rank_row = count(same & (first < second), 0)
        rank_column = count(same & (second < first), 1)
        target_ref[...] = owner_column * capacity + rank_column
        placed = (owner_row * capacity + rank_row) == iota((slots, rows), 0)
        windows = (
            jnp.sum(jnp.where(placed, window_ref[...] + 1, 0).astype(jnp.float32), axis=1, keepdims=True)
            - 1.0
        )
        note_list(capacity, per_owner, blocks_dev, lanes, windows, table_ref, payload_ref.at[:, vit:], request_ref, live_ref)

        widened = embedded_ref[...].astype(jnp.float32)
        factor = lax.rsqrt(jnp.mean(widened * widened, axis=1, keepdims=True) + 1e-06)
        normed = (widened * factor * gain_ref[...].reshape(1, -1)).astype(jnp.bfloat16)
        payload_ref[:, :vit] = jnp.dot(
            placed.astype(jnp.bfloat16), normed, preferred_element_type=jnp.float32
        ).astype(jnp.bfloat16)


def note_list(capacity, per_owner, blocks_dev, lanes, windows, table_ref, notes_ref, request_ref, live_ref):
    slots = notes_ref.shape[0]
    table_row = table_ref[...]
    entries = table_row.shape[1]
    live_row = table_row >= 0
    holder_row = jnp.where(live_row, table_row // blocks_dev, -1)
    local_row = jnp.where(live_row, table_row % blocks_dev, 0)
    lane = iota((slots, LANES), 1)
    before = iota((entries, entries), 0) < iota((entries, entries), 1)
    if lanes is None:
        holder_rank = count((as_column(holder_row) == holder_row) & before, 0)
        request_row = jnp.where(live_row, holder_row * per_owner + holder_rank, -1)
        first_request = jnp.sum(
            jnp.where(iota((1, entries), 1) == 0, request_row, 0).astype(jnp.float32), axis=1, keepdims=True
        ).astype(jnp.int32)
        request_ref[...] = jnp.where(live_row, request_row, first_request)
        live_ref[...] = jnp.broadcast_to(count(live_row, 1), live_ref.shape)
        placed_row = jnp.where(live_row, holder_row * capacity + holder_rank, -1)
        asked = jnp.sum(
            jnp.where(placed_row == iota((slots, entries), 0), local_row + 1, 0).astype(jnp.float32),
            axis=1,
            keepdims=True,
        )
        notes = jnp.where(lane == 0, windows, jnp.where(lane == 1, asked - 1.0, 0.0))
        notes_ref[...] = notes.astype(jnp.bfloat16)
        return
    team = lanes // 2
    regions = slots // capacity // team
    after = iota((entries, entries), 1) < iota((entries, entries), 0)
    region_row = jnp.where(live_row, holder_row // lanes * 2 + local_row % 2, -1)
    region_column = as_column(region_row)
    region_rank = count((region_column == region_row) & after, 1)
    local_column = as_column(local_row // 2)
    member_column = as_column(jnp.where(live_row, holder_row % lanes, 0))
    place = iota((slots, LANES), 0)
    slot_row, slot_region = place % capacity, place // (capacity * team)
    pad = jnp.zeros((1, LANES - entries), jnp.float32)
    notes = jnp.where(lane == entries, windows, 0.0)
    for region in range(regions):
        listed = (region_column == region) & (region_rank == iota((entries, entries), 1))
        pick = lambda column: jnp.sum(
            jnp.where(listed, column, 0).astype(jnp.float32), axis=0, keepdims=True
        )
        locals_row = jnp.concatenate([pick(local_column + 1) - 1.0, pad], axis=1)
        members_row = jnp.concatenate([pick(member_column), pad], axis=1)
        here = (slot_region == region) & (lane < entries)
        notes = jnp.where(here & (slot_row == 0), locals_row, notes)
        notes = jnp.where(here & (slot_row == 1), members_row, notes)
        amount = count(region_row == region, 1).astype(jnp.float32)
        notes = jnp.where((slot_row == 2) & (lane == region), amount, notes)
    notes_ref[...] = notes.astype(jnp.bfloat16)
    request_ref[...] = jnp.zeros(request_ref.shape, jnp.int32)
    live_ref[...] = jnp.zeros(live_ref.shape, jnp.int32)


def embed_and_route(
    patches, w_patch, vit_gain, row_owner, window_slot, block_table, capacity, slots, per_owner, blocks_dev, lanes
):
    rows, patch = patches.shape
    vit = w_patch.shape[1]
    entries = block_table.shape[1]
    width = vit // 2
    whole = lambda *shape: pl.BlockSpec(shape, lambda step: (0,) * len(shape))
    return pl.pallas_call(
        functools.partial(embed_kernel, capacity, per_owner, blocks_dev, lanes),
        grid=(vit // width,),
        out_shape=(
            jax.ShapeDtypeStruct((slots, vit + LANES), jnp.bfloat16),
            jax.ShapeDtypeStruct((rows, 1), jnp.int32),
            jax.ShapeDtypeStruct((1, entries), jnp.int32),
            jax.ShapeDtypeStruct((1, LANES), jnp.int32),
        ),
        in_specs=[
            whole(patch, rows),
            pl.BlockSpec((patch, width), lambda step: (0, step)),
            whole(vit),
            whole(1, rows),
            whole(1, rows),
            whole(1, entries),
        ],
        out_specs=(whole(slots, vit + LANES), whole(rows, 1), whole(1, entries), whole(1, LANES)),
        scratch_shapes=[pltpu.VMEM((rows, patch), jnp.bfloat16), pltpu.VMEM((rows, vit), jnp.bfloat16)],
        compiler_params=pltpu.CompilerParams(vmem_limit_bytes=VMEM_BYTES),
        cost_estimate=pl.CostEstimate(
            flops=2 * rows * patch * vit + 2 * slots * rows * vit,
            bytes_accessed=2 * patch * vit + 2 * rows * patch + 2 * slots * vit,
            transcendentals=rows,
        ),
        name="embed_and_route",
    )(
        patches.T, w_patch, vit_gain, row_owner.reshape(1, rows),
        window_slot.reshape(1, rows), block_table,
    )


def prompt_groups(query_ref, tile):
    tokens = query_ref.shape[0]
    group_size = QHEADS // KVH
    tile_rows = HEADS_TILE * tokens

    def group_step(group, carry):
        for part in range(group_size // HEADS_TILE):
            head = group * group_size + part * HEADS_TILE
            queries = jnp.concatenate(
                [
                    query_ref[:, pl.ds(pl.multiple_of((head + i) * HD, HD), HD)]
                    for i in range(HEADS_TILE)
                ],
                axis=0,
            )
            tile(group, queries, pl.ds(pl.multiple_of(head * tokens, tile_rows), tile_rows))
        return carry

    lax.fori_loop(0, KVH, group_step, 0)


def prompt_scores(queries, keys):
    return lax.dot_general(
        queries, keys, (((1,), (1,)), ((), ())), preferred_element_type=jnp.float32
    ) * (HD ** (-0.5) * LOG2E)


def with_ones(values):
    return jnp.concatenate([values, jnp.ones_like(values)], axis=1)


def head_columns(head):
    return pl.ds(pl.multiple_of(head * HD, HD), HD)


def prompt_begin(query_ref, fresh_ref, top_ref, sum_ref):
    tokens = query_ref.shape[0]
    causal = iota((tokens, tokens), 1) <= iota((tokens, tokens), 0)
    causal = jnp.concatenate([causal.astype(jnp.int32)] * HEADS_TILE, axis=0) > 0

    def tile(group, queries, rows):
        keys, values = fresh_ref[:, head_columns(group)], fresh_ref[:, head_columns(KVH + group)]
        scores = jnp.where(causal, prompt_scores(queries, keys), HIDDEN)
        top = jnp.max(scores, axis=1, keepdims=True)
        weights = jnp.exp2(scores - top).astype(jnp.bfloat16)
        top_ref[rows, :] = jnp.broadcast_to(top, (scores.shape[0], HD))
        sum_ref[rows, :] = jnp.dot(weights, with_ones(values), preferred_element_type=jnp.float32)

    prompt_groups(query_ref, tile)


def prompt_add(query_ref, top_ref, sum_ref, take, shown):
    chunk_keys = shown.shape[1]

    def tile(group, queries, rows):
        scores = jnp.where(shown, prompt_scores(queries, take(group)), HIDDEN)
        old_top = top_ref[rows, :]
        top = jnp.maximum(old_top, jnp.max(scores, axis=1, keepdims=True))
        shrink = jnp.exp2(old_top - top)
        weights = jnp.exp2(scores - jnp.concatenate([top] * (chunk_keys // HD), axis=1))
        top_ref[rows, :] = top
        sum_ref[rows, :] = sum_ref[rows, :] * jnp.concatenate([shrink, shrink], axis=1) + jnp.dot(
            weights.astype(jnp.bfloat16), with_ones(take(KVH + group)), preferred_element_type=jnp.float32
        )

    prompt_groups(query_ref, tile)


def prompt_end(out_ref, sum_ref):
    tokens = out_ref.shape[0]

    def finish(head, carry):
        blended = sum_ref[pl.ds(pl.multiple_of(head * tokens, tokens), tokens), :]
        out_ref[:, head_columns(head)] = (blended[:, :HD] / blended[:, HD:]).astype(jnp.bfloat16)
        return carry

    lax.fori_loop(0, QHEADS, finish, 0)


def listed_prompt_kernel(
    request_ref, live_ref, query_ref, fresh_ref, blocks_ref, out_ref, top_ref, sum_ref, kv_ref, sems
):
    block_tokens = kv_ref.shape[1]
    chunk_keys = CHUNK_BLOCKS * block_tokens
    live_blocks = live_ref[0, 0]
    chunks = (live_blocks + (CHUNK_BLOCKS - 1)) // CHUNK_BLOCKS

    def fetch(chunk, carry):
        def one(place, inner):
            entry = chunk * CHUNK_BLOCKS + place
            pltpu.make_async_copy(
                blocks_ref.at[request_ref[0, entry]], kv_ref.at[entry], sems.at[chunk]
            ).start()
            return inner

        return lax.fori_loop(0, CHUNK_BLOCKS, one, carry)

    lax.fori_loop(0, chunks, fetch, 0)
    prompt_begin(query_ref, fresh_ref, top_ref, sum_ref)

    def visit(chunk, carry):
        first = chunk * CHUNK_BLOCKS
        pltpu.make_async_copy(
            blocks_ref.at[pl.ds(0, CHUNK_BLOCKS)], kv_ref.at[pl.ds(first, CHUNK_BLOCKS)], sems.at[chunk]
        ).wait()
        shown = iota((1, chunk_keys), 1) < (live_blocks - first) * block_tokens
        take = lambda head: kv_ref[pl.ds(first, CHUNK_BLOCKS), :, head_columns(head)].reshape(chunk_keys, HD)
        prompt_add(query_ref, top_ref, sum_ref, take, shown)
        return carry

    lax.fori_loop(0, chunks, visit, 0)
    prompt_end(out_ref, sum_ref)


def striped_prompt_kernel(span_ref, pack_ref, target_ref, striped_ref, *refs):
    whole_ref, out_refs, (row_ref, sum_ref, top_ref) = None, refs[:-3], refs[-3:]
    out_ref = out_refs[0]
    if len(refs) > 4:
        whole_ref, vision_ref, row_ref, sum_ref, top_ref, out_ref, sem = refs
    tokens = pack_ref.shape[0]
    team = striped_ref.shape[1]
    kv_heads = team // 2
    heads = out_ref.shape[1] // HD // kv_heads
    extra = target_ref.shape[1] // LANES
    room, block_tokens = striped_ref.shape[2] - extra, striped_ref.shape[3]
    chunk_blocks = CHUNK_BLOCKS // 2
    half_keys = chunk_blocks * block_tokens
    causal = iota((tokens, tokens), 1) <= iota((tokens, tokens), 0)
    causal = jnp.concatenate([causal.astype(jnp.int32)] * heads, axis=0) > 0

    def blend(weights, values):
        return jnp.dot(weights.astype(jnp.bfloat16), with_ones(values), preferred_element_type=jnp.float32)

    def attend(kv_head, carry):
        for head in range(heads):
            row_ref[head * tokens : (head + 1) * tokens, :] = pack_ref[:, head_columns(kv_head * heads + head)]
        fresh = kv_heads * heads
        scores = prompt_scores(row_ref[...], pack_ref[:, head_columns(fresh + kv_head)])
        scores = jnp.where(causal, scores, HIDDEN)
        top = jnp.max(scores, axis=1, keepdims=True)
        top_ref[...] = jnp.broadcast_to(top, top_ref.shape)
        sum_ref[...] = blend(jnp.exp2(scores - top), pack_ref[:, head_columns(fresh + kv_heads + kv_head)])

        chunks = [
            (jnp.maximum(span_ref[0, 2 * half], span_ref[0, 2 * half + 1]) + (chunk_blocks - 1)) // chunk_blocks
            for half in range(2)
        ]

        def visit(turn, inner):
            half = (turn >= chunks[0]).astype(jnp.int32)
            done = (turn - half * chunks[0]) * chunk_blocks
            keys, values, shown = [], [], []
            for parity in range(2):
                region = 2 * half + parity
                amount, base = span_ref[0, region], span_ref[1, region]
                first = jnp.minimum(base + done, room - chunk_blocks)
                part = pl.ds(first, chunk_blocks)
                keys.append(striped_ref[region, kv_head, part].reshape(half_keys, HD))
                values.append(striped_ref[region, kv_heads + kv_head, part].reshape(half_keys, HD))
                key = iota((1, half_keys), 1)
                shown.append(
                    (
                        (key < (base + amount - first) * block_tokens)
                        & (key >= (base + done - first) * block_tokens)
                    ).astype(jnp.int32)
                )
            keys, values = jnp.concatenate(keys, axis=0), jnp.concatenate(values, axis=0)
            shown = jnp.concatenate(shown, axis=1) > 0
            scores = jnp.where(shown, prompt_scores(row_ref[...], keys), HIDDEN)
            old_top = top_ref[...]
            top = jnp.maximum(old_top, jnp.max(scores, axis=1, keepdims=True))
            shrink = jnp.exp2(old_top - top)
            weights = jnp.exp2(scores - jnp.concatenate([top] * (2 * half_keys // HD), axis=1))
            top_ref[...] = top
            sum_ref[...] = sum_ref[...] * jnp.concatenate([shrink, shrink], axis=1) + blend(weights, values)
            return inner

        lax.fori_loop(0, chunks[0] + chunks[1], visit, 0)
        for head in range(heads):
            blended = sum_ref[head * tokens : (head + 1) * tokens, :]
            out_ref[:, head_columns(kv_head * heads + head)] = (
                blended[:, :HD] / blended[:, HD:]
            ).astype(jnp.bfloat16)
        return carry

    lax.fori_loop(0, kv_heads, attend, 0)
    if whole_ref is not None:
        width = out_ref.shape[1]
        start = pl.multiple_of(lax.axis_index("seq") % 2 * width, width)
        copy = pltpu.make_async_copy(out_ref, whole_ref.at[:, pl.ds(start, width)], sem)
        copy.start()
        regions, team, _, block_tokens, _ = striped_ref.shape
        slots = regions * team * block_tokens
        picked = (target_ref[:, :1] == iota((tokens, slots), 1)).astype(jnp.bfloat16)
        for tile in range(extra):
            vision_ref[:, tile * LANES : (tile + 1) * LANES] = jnp.dot(
                picked, striped_ref[:, :, room + tile].reshape(slots, LANES), preferred_element_type=jnp.float32
            ).astype(jnp.bfloat16)
        copy.wait()


def put_half_kernel(back_ref, whole_ref, out_ref, sem):
    width = back_ref.shape[1]
    start = pl.multiple_of((1 - lax.axis_index("seq") % 2) * width, width)
    copy = pltpu.make_async_copy(back_ref, out_ref.at[:, pl.ds(start, width)], sem)
    copy.start()
    copy.wait()


def put_half(whole, back):
    return pl.pallas_call(
        put_half_kernel,
        out_shape=jax.ShapeDtypeStruct(whole.shape, whole.dtype),
        in_specs=[pl.BlockSpec(memory_space=pltpu.VMEM), pl.BlockSpec(memory_space=pl.ANY)],
        out_specs=pl.BlockSpec(memory_space=pl.ANY),
        scratch_shapes=[pltpu.SemaphoreType.DMA],
        input_output_aliases={1: 0},
        compiler_params=pltpu.CompilerParams(vmem_limit_bytes=SMALL_VMEM_BYTES),
        name="put_half",
    )(back, whole)


def prompt_attention(kernel, scalars, operands, specs, outs, scratch, keys, name):
    tokens, width = operands[0].shape
    kv_width = operands[1].shape[1]
    whole = lambda shape: pl.BlockSpec(shape, lambda *_: (0,) * len(shape))
    outs = [(tokens, width)] + outs
    return pl.pallas_call(
        kernel,
        out_shape=tuple(jax.ShapeDtypeStruct(shape, jnp.bfloat16) for shape in outs),
        grid_spec=pltpu.PrefetchScalarGridSpec(
            num_scalar_prefetch=len(scalars),
            grid=(1,),
            in_specs=[spec or whole(operand.shape) for operand, spec in zip(operands, specs)],
            out_specs=tuple(whole(shape) for shape in outs),
            scratch_shapes=[
                pltpu.VMEM((QHEADS * tokens, HD), jnp.float32),
                pltpu.VMEM((QHEADS * tokens, 2 * HD), jnp.float32),
            ]
            + scratch,
        ),
        compiler_params=pltpu.CompilerParams(vmem_limit_bytes=VMEM_BYTES),
        cost_estimate=pl.CostEstimate(
            flops=4 * tokens * keys * width,
            bytes_accessed=4 * tokens * width + 2 * keys * kv_width,
            transcendentals=tokens * QHEADS * keys,
        ),
        name=name,
    )(*scalars, *operands)


def listed_prompt(request, live, queries, new_kv, blocks):
    entries, block_tokens = request.shape[1], blocks.shape[1]
    chunks = -(-entries // CHUNK_BLOCKS)
    scratch = [
        pltpu.VMEM((chunks * CHUNK_BLOCKS, block_tokens, new_kv.shape[1]), jnp.bfloat16),
        pltpu.SemaphoreType.DMA((chunks,)),
    ]
    return prompt_attention(
        listed_prompt_kernel, (request, live), (queries, new_kv, blocks),
        (None, None, pl.BlockSpec(memory_space=pl.ANY)), [], scratch,
        entries * block_tokens + queries.shape[0], "listed_prompt",
    )[0]


def striped_prompt(lanes, extra, span, pack, target, striped, pick):
    tokens = pack.shape[0]
    devices, held, block_tokens, _ = striped.shape
    team = lanes // 2
    split = striped.reshape(devices // team, team, held, block_tokens, LANES)
    width = pack.shape[1] - team * HD
    rows = 2 * width // team // HD * tokens
    shapes = [(tokens, 2 * width), (tokens, extra * LANES)] if pick else [(tokens, width)]
    wide_target = jnp.broadcast_to(target, (tokens, extra * LANES))
    vmem = pl.BlockSpec(memory_space=pltpu.VMEM)
    return pl.pallas_call(
        striped_prompt_kernel,
        out_shape=tuple(jax.ShapeDtypeStruct(shape, jnp.bfloat16) for shape in shapes),
        in_specs=[pl.BlockSpec(memory_space=pltpu.SMEM), vmem, vmem, vmem],
        out_specs=(pl.BlockSpec(memory_space=pl.ANY), vmem) if pick else (vmem,),
        scratch_shapes=[
            pltpu.VMEM((rows, HD), jnp.bfloat16),
            pltpu.VMEM((rows, 2 * HD), jnp.float32),
            pltpu.VMEM((rows, HD), jnp.float32),
        ]
        + [pltpu.VMEM((tokens, width), jnp.bfloat16), pltpu.SemaphoreType.DMA] * pick,
        compiler_params=pltpu.CompilerParams(vmem_limit_bytes=SMALL_VMEM_BYTES),
        cost_estimate=pl.CostEstimate(
            flops=4 * tokens * held * block_tokens * width,
            bytes_accessed=4 * tokens * width + 2 * held * block_tokens * team * HD,
            transcendentals=tokens * width // HD * held * block_tokens,
        ),
        name="striped_prompt_pick" if pick else "striped_prompt",
    )(span, pack, wide_target, split)


def stripe_kernel(lanes, steps, cache_ref, *refs):
    out_refs, held_ref, in_sems, out_sems = refs[:-3], refs[-3], refs[-2], refs[-1]
    member = lax.axis_index("seq") % lanes
    team = lanes // 2
    chunks = in_sems.shape[0]
    half = cache_ref.shape[0]
    size = half // chunks
    taken, given = [], []
    for chunk in range(chunks):
        part = pl.ds(chunk * size, size)
        taken.append(pltpu.make_async_copy(cache_ref.at[part], held_ref.at[part], in_sems.at[chunk]))
        taken[-1].start()
    for chunk in range(chunks):
        part = pl.ds(chunk * size, size)
        taken[chunk].wait()
        for place, step in enumerate(steps):
            lane = member ^ step
            parity, column = lane // team, lane % team // 2 * KVH + lane % 2
            for core in range(2):
                start = pl.multiple_of((column + 2 * core) * LANES, LANES)
                given.append(
                    pltpu.make_async_copy(
                        held_ref.at[part, parity, :, pl.ds(start, LANES)],
                        out_refs[place].at[pl.ds(core * half + chunk * size, size)],
                        out_sems.at[chunk, 2 * place + core],
                    )
                )
                given[-1].start()
    for copy in given:
        copy.wait()


def stripe(lanes, steps, kv_cache):
    blocks, block_tokens, width = kv_cache.shape
    chunks = 4
    kv_cache = kv_cache.reshape(blocks // 2, 2, block_tokens, width)
    piece = jax.ShapeDtypeStruct((blocks, block_tokens, LANES), jnp.bfloat16)
    return pl.pallas_call(
        functools.partial(stripe_kernel, lanes, steps),
        out_shape=(piece,) * len(steps),
        in_specs=[pl.BlockSpec(memory_space=pl.ANY)],
        out_specs=(pl.BlockSpec(memory_space=pl.ANY),) * len(steps),
        scratch_shapes=[
            pltpu.VMEM(kv_cache.shape, jnp.bfloat16),
            pltpu.SemaphoreType.DMA((chunks,)),
            pltpu.SemaphoreType.DMA((chunks, 2 * len(steps))),
        ],
        compiler_params=pltpu.CompilerParams(vmem_limit_bytes=VMEM_BYTES),
        name="stripe",
    )(kv_cache)


def gather_kernel(lanes, steps, entries, notes_ref, attended_ref, *refs):
    piece_refs = refs[:lanes]
    out_ref, held_ref, narrow_ref, wide_ref, index_ref, scalar_ref, sems = refs[lanes:]
    blocks = piece_refs[0].shape[0]
    readers, extra = attended_ref.shape[0], attended_ref.shape[1]
    room = out_ref.shape[1] - extra
    half = blocks // 2
    capacity = notes_ref.shape[0] // readers
    column = pl.ds(notes_ref.shape[1] - LANES, LANES)
    noted = pltpu.make_async_copy(notes_ref.at[:, column], narrow_ref, sems.at[lanes + 1])
    noted.start()
    copies = [
        pltpu.make_async_copy(piece_ref, held_ref.at[pl.ds(step * blocks, blocks)], sems.at[step])
        for step, piece_ref in zip(steps, piece_refs)
    ]
    for copy in copies:
        copy.start()

    noted.wait()
    wide_ref[...] = narrow_ref[...].astype(jnp.float32)
    local = wide_ref[pl.ds(0, readers, capacity), :]
    member = wide_ref[pl.ds(1, readers, capacity), :]
    lane = iota((readers, LANES), 1)
    listed = (local >= 0.0) & (lane < entries)
    step = member.astype(jnp.int32) ^ (lax.axis_index("seq") % lanes)
    amount = jnp.sum(listed.astype(jnp.float32), axis=1, keepdims=True).astype(jnp.int32)
    index = jnp.where(listed, step * blocks + local.astype(jnp.int32), 0)
    out_ref[...] = jnp.zeros_like(out_ref)
    index_ref[...] = jnp.where(lane == entries, amount, index)
    to_scalars = pltpu.make_async_copy(index_ref, scalar_ref, sems.at[lanes])
    to_scalars.start()
    to_scalars.wait()
    for copy in copies:
        copy.wait()

    def some_of(reader, chip, base):
        def some(group, inner):
            first = group * ROOM_STEP
            spots = [scalar_ref[reader, first + i] for i in range(ROOM_STEP)]
            places = [jnp.minimum(base + first + i, room) for i in range(ROOM_STEP)]
            for core in range(2):
                tiles = [held_ref[spot + core * half] for spot in spots]
                for place, tile in zip(places, tiles):
                    out_ref[2 * chip + core, place] = tile
            return inner

        return some

    def turn(reader, base):
        amount = scalar_ref[reader, entries]
        some = some_of(reader, reader // 2, base)
        lax.fori_loop(0, (amount + (ROOM_STEP - 1)) // ROOM_STEP, some, 0)
        return jnp.where(reader % 2 == 0, amount, 0)

    lax.fori_loop(0, readers, turn, 0)
    out_ref[:, room:] = attended_ref[...]


def gather_stripes(lanes, steps, room, entries, arrived, attended, pieces):
    blocks, block_tokens, _ = pieces[0].shape
    slots = arrived.shape[0]
    readers, extra = attended.shape[:2]
    shape = (readers, room + extra, block_tokens, LANES)
    return pl.pallas_call(
        functools.partial(gather_kernel, lanes, steps, entries),
        out_shape=jax.ShapeDtypeStruct(shape, jnp.bfloat16),
        in_specs=[pl.BlockSpec(memory_space=pl.ANY), pl.BlockSpec(memory_space=pltpu.VMEM)]
        + [pl.BlockSpec(memory_space=pl.ANY)] * lanes,
        out_specs=pl.BlockSpec(memory_space=pltpu.VMEM),
        scratch_shapes=[
            pltpu.VMEM((lanes * blocks, block_tokens, LANES), jnp.bfloat16),
            pltpu.VMEM((slots, LANES), jnp.bfloat16),
            pltpu.VMEM((slots, LANES), jnp.float32),
            pltpu.VMEM((readers, LANES), jnp.int32),
            pltpu.SMEM((readers, LANES), jnp.int32),
            pltpu.SemaphoreType.DMA((lanes + 2,)),
        ],
        compiler_params=pltpu.CompilerParams(vmem_limit_bytes=SMALL_VMEM_BYTES),
        cost_estimate=pl.CostEstimate(
            flops=0, bytes_accessed=4 * readers * room * block_tokens * LANES, transcendentals=0
        ),
        name="gather_stripes",
    )(arrived, attended, *pieces)


def vision_kernel(
    entries, rooms, rows_ref, w_hbm_ref, out_ref, own_ref, other_ref, choice_ref, w_ref, qkv_ref, blend_ref, wide_ref, sems
):
    slots, vit = rows_ref.shape[0], w_ref.shape[0]
    inner = VHEADS * VHD
    copies = []
    for third in range(3):
        part = pl.ds(third * inner, inner)
        copies.append(pltpu.make_async_copy(w_hbm_ref.at[:, part], w_ref.at[:, part], sems.at[third]))
        copies[-1].start()
    notes = rows_ref[:, vit:].astype(jnp.float32)
    wide_ref[...] = notes
    device = lax.axis_index("seq")
    capacity = slots // out_ref.shape[0]
    first_row = (device - device % 2) * capacity + 2
    amounts = [wide_ref[pl.ds(first_row + i * capacity, 1), :].astype(jnp.int32) for i in range(2)]
    second = device % 2 > 0
    nothing = jnp.zeros_like(amounts[0])
    own_ref[...] = jnp.concatenate(
        [jnp.where(second, amounts[1], amounts[0]), jnp.where(second, amounts[0], nothing)], axis=0
    )
    other_ref[...] = jnp.concatenate(
        [jnp.where(second, amounts[0], amounts[1]), jnp.where(second, nothing, amounts[0])], axis=0
    )
    chips = out_ref.shape[0] // 2
    pooled = wide_ref[pl.ds(2, chips, 2 * capacity), :] + wide_ref[pl.ds(2 + capacity, chips, 2 * capacity), :]
    needed = jnp.max(jnp.where(iota((chips, LANES), 1) < entries, pooled, 0.0)).astype(jnp.int32)
    choice = 0
    for room in rooms:
        choice = choice + jnp.where(needed > room, 1, 0)
    choice_ref[0, 0] = choice
    window_column = jnp.sum(
        jnp.where(iota((slots, LANES), 1) == entries, notes, 0.0), axis=1, keepdims=True
    ).astype(jnp.int32)
    window_row = as_row(window_column)
    itself = iota((slots, slots), 0) == iota((slots, slots), 1)
    allowed = ((window_column == window_row) & (window_row >= 0)) | itself
    blend_ref[...] = jnp.zeros_like(blend_ref)
    for third, copy in enumerate(copies):
        part = slice(third * inner, (third + 1) * inner)
        copy.wait()
        qkv_ref[:, part] = jnp.dot(
            rows_ref[:, :vit], w_ref[:, part], preferred_element_type=jnp.float32
        ).astype(jnp.bfloat16)
    for head in range(VHEADS):
        first, last = head * VHD, (head + 1) * VHD
        low, high = first // LANES * LANES, -(-last // LANES) * LANES
        column = low + iota((slots, high - low), 1)
        mine = (column >= first) & (column < last)
        part = lambda offset: qkv_ref[:, offset + low : offset + high]
        keys = jnp.where(mine, part(inner).astype(jnp.float32), 0.0).astype(jnp.bfloat16)
        values = jnp.where(mine, part(2 * inner).astype(jnp.float32), 0.0).astype(jnp.bfloat16)
        scores = lax.dot_general(
            part(0), keys, (((1,), (1,)), ((), ())), preferred_element_type=jnp.float32
        ) * VHD ** (-0.5)
        scores = jnp.where(allowed, scores, HIDDEN)
        weights = jnp.exp(scores - jnp.max(scores, axis=1, keepdims=True))
        total = jnp.sum(weights, axis=1, keepdims=True)
        blended = jnp.dot(weights.astype(jnp.bfloat16), values, preferred_element_type=jnp.float32)
        blend_ref[:, low:high] += blended / total
    devices, tiles, rows, _ = out_ref.shape
    for tile in range(tiles):
        part = blend_ref[:, tile * LANES : (tile + 1) * LANES].astype(jnp.bfloat16)
        out_ref[:, tile] = part.reshape(devices, rows, LANES)


def vision_tiles(devices, entries, rooms, arrived, w_qkv):
    slots = arrived.shape[0]
    vit, width = w_qkv.shape
    inner = VHEADS * VHD
    return pl.pallas_call(
        functools.partial(vision_kernel, entries, rooms),
        out_shape=(
            jax.ShapeDtypeStruct((devices, inner // LANES, slots // devices, LANES), jnp.bfloat16),
            jax.ShapeDtypeStruct((2, LANES), jnp.int32),
            jax.ShapeDtypeStruct((2, LANES), jnp.int32),
            jax.ShapeDtypeStruct((1, 1), jnp.int32),
        ),
        in_specs=[pl.BlockSpec(memory_space=pltpu.VMEM), pl.BlockSpec(memory_space=pl.ANY)],
        out_specs=(pl.BlockSpec(memory_space=pltpu.VMEM),) * 3 + (pl.BlockSpec(memory_space=pltpu.SMEM),),
        scratch_shapes=[
            pltpu.VMEM((vit, width), jnp.bfloat16),
            pltpu.VMEM((slots, width), jnp.bfloat16),
            pltpu.VMEM((slots, inner), jnp.float32),
            pltpu.VMEM((slots, LANES), jnp.float32),
            pltpu.SemaphoreType.DMA((3,)),
        ],
        compiler_params=pltpu.CompilerParams(vmem_limit_bytes=VMEM_BYTES),
        cost_estimate=pl.CostEstimate(
            flops=2 * slots * vit * width + 4 * slots * slots * inner,
            bytes_accessed=2 * vit * width,
            transcendentals=VHEADS * slots * slots,
        ),
        name="vision_tiles",
    )(arrived, w_qkv)


def pick_kernel(target_ref, *refs):
    out_ref = refs[-1]
    returned = jnp.concatenate([ref[...] for ref in refs[:-1]], axis=0)
    rows, slots = target_ref.shape[0], returned.shape[0]
    picked = (target_ref[...] == iota((rows, slots), 1)).astype(jnp.bfloat16)
    out_ref[...] = jnp.dot(picked, returned, preferred_element_type=jnp.float32).astype(jnp.bfloat16)


def pick_rows(target, *returned):
    return pl.pallas_call(
        pick_kernel,
        out_shape=jax.ShapeDtypeStruct((target.shape[0], returned[0].shape[1]), jnp.bfloat16),
        compiler_params=pltpu.CompilerParams(vmem_limit_bytes=VMEM_BYTES),
        name="pick_rows",
    )(target, *returned)


def window_attention(qkv_rows, windows):
    total_rows = qkv_rows.shape[0]
    inner_width = VHEADS * VHD
    query_heads = qkv_rows[:, :inner_width].reshape(total_rows, VHEADS, VHD)
    key_heads = qkv_rows[:, inner_width : 2 * inner_width].reshape(total_rows, VHEADS, VHD)
    value_heads = qkv_rows[:, 2 * inner_width :].reshape(total_rows, VHEADS, VHD)
    is_live = windows >= 0
    every_row = jnp.arange(total_rows)
    scores = jnp.einsum(
        "qhd,khd->hqk", query_heads, key_heads, preferred_element_type=jnp.float32
    ) * VHD ** (-0.5)
    allowed = (windows[:, None] == windows[None, :]) & is_live[None, :] | (
        every_row[:, None] == every_row[None, :]
    )
    scores = jnp.where(allowed[None], scores, -jnp.inf)
    highest = jnp.max(scores, axis=2, keepdims=True)
    weights = jnp.exp(scores - highest)
    totals = jnp.sum(weights, axis=2)
    blended = jnp.einsum(
        "hqk,khd->qhd",
        weights.astype(jnp.bfloat16),
        value_heads,
        preferred_element_type=jnp.float32,
    )
    pieces = (blended / totals.T[:, :, None]).reshape(total_rows, inner_width)
    return pieces.astype(jnp.bfloat16)


def exchange(rows, devices):
    parts = rows.reshape((devices, rows.shape[0] // devices) + rows.shape[1:])
    return lax.all_to_all(parts, "seq", split_axis=0, concat_axis=0, tiled=True).reshape(rows.shape)


def core_index():
    return lax.axis_index("seq") % 2


def head_half(queries, new_kv, core):
    width, kv_width = queries.shape[1] // 2, new_kv.shape[1] // 4
    part = lambda array, start, size: lax.dynamic_slice_in_dim(array, start, size, 1)
    return jnp.concatenate(
        [
            part(queries, core * width, width),
            part(new_kv, core * kv_width, kv_width),
            part(new_kv, 2 * kv_width + core * kv_width, kv_width),
        ],
        axis=1,
    )


def swap(piece, step, devices):
    return lax.ppermute(piece, "seq", [(i, i ^ step) for i in range(devices)])


def vision_rows(arrived, windows, w_qkv):
    vit = w_qkv.shape[0]
    qkv_rows = jnp.dot(arrived[:, :vit], w_qkv, preferred_element_type=jnp.float32).astype(jnp.bfloat16)
    return window_attention(qkv_rows, windows)


def shards(
    patches,
    row_owner,
    window_slot,
    w_patch,
    vit_gain,
    w_qkv,
    queries,
    new_kv,
    kv_cache,
    block_table,
):
    devices = lax.axis_size("seq")
    vit = w_patch.shape[1]
    capacity = 2 * patches.shape[0] // devices
    slots = devices * capacity
    entries = block_table.shape[1]
    per_owner = 2 * entries // devices
    blocks_dev = kv_cache.shape[0]
    lanes = kv_cache.shape[2] // LANES
    striped = devices == 2 * lanes and capacity == kv_cache.shape[1] and entries + 2 <= LANES
    if striped:
        steps = sorted(range(lanes), key=lambda step: (step not in EARLY_STEPS, step < 2, step == 0))
        pieces, block_table = lax.optimization_barrier((stripe(lanes, steps, kv_cache), block_table))
        pieces = [swap(piece, step, devices) if step else piece for step, piece in zip(steps, pieces)]
        early = [steps.index(step) for step in EARLY_STEPS]
    payload, target, request, live = embed_and_route(
        patches, w_patch, vit_gain, row_owner, window_slot, block_table,
        capacity, slots, per_owner, blocks_dev, lanes if striped else None,
    )
    if striped:
        payload, *done = lax.optimization_barrier((payload, *[pieces[place] for place in early]))
        for place, piece in zip(early, done):
            pieces[place] = piece
    arrived = exchange(payload, devices)

    if not striped:
        notes = arrived[:, vit : vit + 2].astype(jnp.int32)
        asked = notes[:, 1].reshape(devices, capacity)[:, :per_owner].reshape(devices * per_owner)
        delivered = exchange(kv_cache[jnp.maximum(asked, 0)], devices)
        attended = vision_rows(arrived, notes[:, 0], w_qkv)
        delivered, attended = lax.optimization_barrier((delivered, attended))
        returned = exchange(attended, devices)
        attention_out = listed_prompt(request, live, queries, new_kv, delivered)
        return (pick_rows(target, returned), attention_out)

    rooms = [room for room in ROOMS if room < 2 * entries] + [2 * entries]
    attended, own_span, other_span, choice = vision_tiles(devices, entries, rooms[:-1], arrived, w_qkv)

    def finish(room):
        def run(arrived, attended, target, own_span, other_span, queries, new_kv, *pieces):
            outgoing = gather_stripes(lanes, steps, room, entries, arrived, attended, pieces)
            delivered = exchange(outgoing.reshape((-1,) + outgoing.shape[2:]), devices).reshape(outgoing.shape)
            extra = attended.shape[1]
            own_pack, other_pack = [head_half(queries, new_kv, core) for core in (core_index(), 1 - core_index())]
            other_pack = swap(other_pack, 1, devices)
            (other_out,) = striped_prompt(lanes, extra, other_span, other_pack, target, delivered, False)
            back = swap(other_out, 1, devices)
            own_out, vision_out = striped_prompt(lanes, extra, own_span, own_pack, target, delivered, True)
            return (vision_out, put_half(own_out, back))

        return run

    return lax.switch(
        choice[0, 0], [finish(room) for room in rooms],
        arrived, attended, target, own_span, other_span, queries, new_kv, *pieces,
    )


def solution(mesh):
    in_specs = (
        P(("groups", "seq"), None),
        P(("groups", "seq"), None),
        P(("groups", "seq")),
        P(),
        P(),
        P(),
        P(("groups", "seq"), None),
        P(("groups", "seq"), None),
        P(("groups", "seq"), None, None),
        P(("groups", "seq"), None),
    )
    out_specs = (P(("groups", "seq"), None), P(("groups", "seq"), None))
    return jax.shard_map(shards, mesh=mesh, in_specs=in_specs, out_specs=out_specs, check_vma=False)
```

```python
import functools

import jax
import jax.numpy as jnp
from jax import lax
from jax.experimental import pallas as pl
from jax.experimental.pallas import tpu as pltpu
from jax.sharding import PartitionSpec as P

VHEADS = 8
VHD = 80
QHEADS = 32
KVH = 4
HD = 128
LANES = 128
CHUNK_BLOCKS = 16
HEADS_TILE = 2
LOG2E = 1.4426950408889634
HIDDEN = -1e30
VMEM_BYTES = 56 * 1024 * 1024
ROOM_STEP = 8
QUAD = 4
SMALL_VMEM_BYTES = 24 * 1024 * 1024
ROOMS = (28, 32, 36, 40, 48, 64)
STEPS = (2, 3, 4, 5, 6, 7, 1, 0)


def iota(shape, axis):
    return lax.broadcasted_iota(jnp.int32, shape, axis)


def count(hits, axis):
    return jnp.sum(hits.astype(jnp.float32), axis=axis, keepdims=True).astype(jnp.int32)


def as_row(column):
    size = column.shape[0]
    diagonal = iota((size, size), 0) == iota((size, size), 1)
    return jnp.sum(jnp.where(diagonal, column, 0).astype(jnp.float32), axis=0, keepdims=True).astype(jnp.int32)


def as_column(row):
    size = row.shape[1]
    diagonal = iota((size, size), 0) == iota((size, size), 1)
    return jnp.sum(jnp.where(diagonal, row, 0).astype(jnp.float32), axis=1, keepdims=True).astype(jnp.int32)


def embed_kernel(
    capacity,
    per_owner,
    blocks_dev,
    lanes,
    patches_ref,
    w_ref,
    gain_ref,
    owner_ref,
    window_ref,
    table_ref,
    payload_ref,
    target_ref,
    request_ref,
    live_ref,
    turned_ref,
    embedded_ref,
):
    step = pl.program_id(0)
    width = w_ref.shape[1]

    @pl.when(step == 0)
    def _():
        turned_ref[...] = patches_ref[...].T

    piece = jnp.dot(turned_ref[...], w_ref[...], preferred_element_type=jnp.float32)
    embedded_ref[:, pl.ds(pl.multiple_of(step * width, width), width)] = piece.astype(jnp.bfloat16)

    @pl.when(step == pl.num_programs(0) - 1)
    def _():
        slots = payload_ref.shape[0]
        vit = embedded_ref.shape[1]
        rows = owner_ref.shape[1]
        owner_row = owner_ref[...]
        owner_column = as_column(owner_row)
        same = owner_column == owner_row
        first, second = iota((rows, rows), 0), iota((rows, rows), 1)
        rank_row = count(same & (first < second), 0)
        rank_column = count(same & (second < first), 1)
        target_ref[...] = owner_column * capacity + rank_column
        placed = (owner_row * capacity + rank_row) == iota((slots, rows), 0)
        windows = (
            jnp.sum(jnp.where(placed, window_ref[...] + 1, 0).astype(jnp.float32), axis=1, keepdims=True)
            - 1.0
        )
        note_list(capacity, per_owner, blocks_dev, lanes, windows, table_ref, payload_ref.at[:, vit:], request_ref, live_ref)

        widened = embedded_ref[...].astype(jnp.float32)
        factor = lax.rsqrt(jnp.mean(widened * widened, axis=1, keepdims=True) + 1e-06)
        normed = (widened * factor * gain_ref[...].reshape(1, -1)).astype(jnp.bfloat16)
        payload_ref[:, :vit] = jnp.dot(
            placed.astype(jnp.bfloat16), normed, preferred_element_type=jnp.float32
        ).astype(jnp.bfloat16)


def note_list(capacity, per_owner, blocks_dev, lanes, windows, table_ref, notes_ref, request_ref, live_ref):
    slots = notes_ref.shape[0]
    table_row = table_ref[...]
    entries = table_row.shape[1]
    live_row = table_row >= 0
    holder_row = jnp.where(live_row, table_row // blocks_dev, -1)
    local_row = jnp.where(live_row, table_row % blocks_dev, 0)
    lane = iota((slots, LANES), 1)
    before = iota((entries, entries), 0) < iota((entries, entries), 1)
    if lanes is None:
        holder_rank = count((as_column(holder_row) == holder_row) & before, 0)
        request_row = jnp.where(live_row, holder_row * per_owner + holder_rank, -1)
        first_request = jnp.sum(
            jnp.where(iota((1, entries), 1) == 0, request_row, 0).astype(jnp.float32), axis=1, keepdims=True
        ).astype(jnp.int32)
        request_ref[...] = jnp.where(live_row, request_row, first_request)
        live_ref[...] = jnp.broadcast_to(count(live_row, 1), live_ref.shape)
        placed_row = jnp.where(live_row, holder_row * capacity + holder_rank, -1)
        asked = jnp.sum(
            jnp.where(placed_row == iota((slots, entries), 0), local_row + 1, 0).astype(jnp.float32),
            axis=1,
            keepdims=True,
        )
        notes = jnp.where(lane == 0, windows, jnp.where(lane == 1, asked - 1.0, 0.0))
        notes_ref[...] = notes.astype(jnp.bfloat16)
        return
    team = lanes // 2
    regions = slots // capacity // team
    after = iota((entries, entries), 1) < iota((entries, entries), 0)
    region_row = jnp.where(live_row, holder_row // lanes * 2 + local_row % 2, -1)
    region_column = as_column(region_row)
    region_rank = count((region_column == region_row) & after, 1)
    local_column = as_column(local_row // 2)
    member_column = as_column(jnp.where(live_row, holder_row % lanes, 0))
    place = iota((slots, LANES), 0)
    slot_row, slot_region = place % capacity, place // (capacity * team)
    pad = jnp.zeros((1, LANES - entries), jnp.float32)
    notes = jnp.where(lane == entries, windows, 0.0)
    for region in range(regions):
        listed = (region_column == region) & (region_rank == iota((entries, entries), 1))
        pick = lambda column: jnp.sum(
            jnp.where(listed, column, 0).astype(jnp.float32), axis=0, keepdims=True
        )
        locals_row = jnp.concatenate([pick(local_column + 1) - 1.0, pad], axis=1)
        members_row = jnp.concatenate([pick(member_column), pad], axis=1)
        here = (slot_region == region) & (lane < entries)
        notes = jnp.where(here & (slot_row == 0), locals_row, notes)
        notes = jnp.where(here & (slot_row == 1), members_row, notes)
        amount = count(region_row == region, 1).astype(jnp.float32)
        notes = jnp.where((slot_row == 2) & (lane == region), amount, notes)
    notes_ref[...] = notes.astype(jnp.bfloat16)
    request_ref[...] = jnp.zeros(request_ref.shape, jnp.int32)
    live_ref[...] = jnp.zeros(live_ref.shape, jnp.int32)


def embed_and_route(
    patches, w_patch, vit_gain, row_owner, window_slot, block_table, capacity, slots, per_owner, blocks_dev, lanes
):
    rows, patch = patches.shape
    vit = w_patch.shape[1]
    entries = block_table.shape[1]
    width = vit // 2
    whole = lambda *shape: pl.BlockSpec(shape, lambda step: (0,) * len(shape))
    return pl.pallas_call(
        functools.partial(embed_kernel, capacity, per_owner, blocks_dev, lanes),
        grid=(vit // width,),
        out_shape=(
            jax.ShapeDtypeStruct((slots, vit + LANES), jnp.bfloat16),
            jax.ShapeDtypeStruct((rows, 1), jnp.int32),
            jax.ShapeDtypeStruct((1, entries), jnp.int32),
            jax.ShapeDtypeStruct((1, LANES), jnp.int32),
        ),
        in_specs=[
            whole(patch, rows),
            pl.BlockSpec((patch, width), lambda step: (0, step)),
            whole(vit),
            whole(1, rows),
            whole(1, rows),
            whole(1, entries),
        ],
        out_specs=(whole(slots, vit + LANES), whole(rows, 1), whole(1, entries), whole(1, LANES)),
        scratch_shapes=[pltpu.VMEM((rows, patch), jnp.bfloat16), pltpu.VMEM((rows, vit), jnp.bfloat16)],
        compiler_params=pltpu.CompilerParams(vmem_limit_bytes=VMEM_BYTES),
        cost_estimate=pl.CostEstimate(
            flops=2 * rows * patch * vit + 2 * slots * rows * vit,
            bytes_accessed=2 * patch * vit + 2 * rows * patch + 2 * slots * vit,
            transcendentals=rows,
        ),
        name="embed_and_route",
    )(
        patches.T, w_patch, vit_gain, row_owner.reshape(1, rows),
        window_slot.reshape(1, rows), block_table,
    )


def prompt_groups(query_ref, tile):
    tokens = query_ref.shape[0]
    group_size = QHEADS // KVH
    tile_rows = HEADS_TILE * tokens

    def group_step(group, carry):
        for part in range(group_size // HEADS_TILE):
            head = group * group_size + part * HEADS_TILE
            queries = jnp.concatenate(
                [
                    query_ref[:, pl.ds(pl.multiple_of((head + i) * HD, HD), HD)]
                    for i in range(HEADS_TILE)
                ],
                axis=0,
            )
            tile(group, queries, pl.ds(pl.multiple_of(head * tokens, tile_rows), tile_rows))
        return carry

    lax.fori_loop(0, KVH, group_step, 0)


def prompt_scores(queries, keys):
    return lax.dot_general(
        queries, keys, (((1,), (1,)), ((), ())), preferred_element_type=jnp.float32
    ) * (HD ** (-0.5) * LOG2E)


def with_ones(values):
    return jnp.concatenate([values, jnp.ones_like(values)], axis=1)


def head_columns(head):
    return pl.ds(pl.multiple_of(head * HD, HD), HD)


def prompt_begin(query_ref, fresh_ref, top_ref, sum_ref):
    tokens = query_ref.shape[0]
    causal = iota((tokens, tokens), 1) <= iota((tokens, tokens), 0)
    causal = jnp.concatenate([causal.astype(jnp.int32)] * HEADS_TILE, axis=0) > 0

    def tile(group, queries, rows):
        keys, values = fresh_ref[:, head_columns(group)], fresh_ref[:, head_columns(KVH + group)]
        scores = jnp.where(causal, prompt_scores(queries, keys), HIDDEN)
        top = jnp.max(scores, axis=1, keepdims=True)
        weights = jnp.exp2(scores - top).astype(jnp.bfloat16)
        top_ref[rows, :] = jnp.broadcast_to(top, (scores.shape[0], HD))
        sum_ref[rows, :] = jnp.dot(weights, with_ones(values), preferred_element_type=jnp.float32)

    prompt_groups(query_ref, tile)


def prompt_add(query_ref, top_ref, sum_ref, take, shown):
    chunk_keys = shown.shape[1]

    def tile(group, queries, rows):
        scores = jnp.where(shown, prompt_scores(queries, take(group)), HIDDEN)
        old_top = top_ref[rows, :]
        top = jnp.maximum(old_top, jnp.max(scores, axis=1, keepdims=True))
        shrink = jnp.exp2(old_top - top)
        weights = jnp.exp2(scores - jnp.concatenate([top] * (chunk_keys // HD), axis=1))
        top_ref[rows, :] = top
        sum_ref[rows, :] = sum_ref[rows, :] * jnp.concatenate([shrink, shrink], axis=1) + jnp.dot(
            weights.astype(jnp.bfloat16), with_ones(take(KVH + group)), preferred_element_type=jnp.float32
        )

    prompt_groups(query_ref, tile)


def prompt_end(out_ref, sum_ref):
    tokens = out_ref.shape[0]

    def finish(head, carry):
        blended = sum_ref[pl.ds(pl.multiple_of(head * tokens, tokens), tokens), :]
        out_ref[:, head_columns(head)] = (blended[:, :HD] / blended[:, HD:]).astype(jnp.bfloat16)
        return carry

    lax.fori_loop(0, QHEADS, finish, 0)


def listed_prompt_kernel(
    request_ref, live_ref, query_ref, fresh_ref, blocks_ref, out_ref, top_ref, sum_ref, kv_ref, sems
):
    block_tokens = kv_ref.shape[1]
    chunk_keys = CHUNK_BLOCKS * block_tokens
    live_blocks = live_ref[0, 0]
    chunks = (live_blocks + (CHUNK_BLOCKS - 1)) // CHUNK_BLOCKS

    def fetch(chunk, carry):
        def one(place, inner):
            entry = chunk * CHUNK_BLOCKS + place
            pltpu.make_async_copy(
                blocks_ref.at[request_ref[0, entry]], kv_ref.at[entry], sems.at[chunk]
            ).start()
            return inner

        return lax.fori_loop(0, CHUNK_BLOCKS, one, carry)

    lax.fori_loop(0, chunks, fetch, 0)
    prompt_begin(query_ref, fresh_ref, top_ref, sum_ref)

    def visit(chunk, carry):
        first = chunk * CHUNK_BLOCKS
        pltpu.make_async_copy(
            blocks_ref.at[pl.ds(0, CHUNK_BLOCKS)], kv_ref.at[pl.ds(first, CHUNK_BLOCKS)], sems.at[chunk]
        ).wait()
        shown = iota((1, chunk_keys), 1) < (live_blocks - first) * block_tokens
        take = lambda head: kv_ref[pl.ds(first, CHUNK_BLOCKS), :, head_columns(head)].reshape(chunk_keys, HD)
        prompt_add(query_ref, top_ref, sum_ref, take, shown)
        return carry

    lax.fori_loop(0, chunks, visit, 0)
    prompt_end(out_ref, sum_ref)


def striped_prompt_kernel(span_ref, pack_ref, target_ref, striped_ref, *refs):
    whole_ref, out_refs, (row_ref, sum_ref, top_ref) = None, refs[:-3], refs[-3:]
    out_ref = out_refs[0]
    if len(refs) > 4:
        whole_ref, vision_ref, row_ref, sum_ref, top_ref, out_ref, sem = refs
    tokens = pack_ref.shape[0]
    team = striped_ref.shape[1]
    kv_heads = team // 2
    heads = out_ref.shape[1] // HD // kv_heads
    extra = target_ref.shape[1] // LANES
    room, block_tokens = striped_ref.shape[2] - extra, striped_ref.shape[3]
    causal = iota((tokens, tokens), 1) <= iota((tokens, tokens), 0)
    causal = jnp.concatenate([causal.astype(jnp.int32)] * heads, axis=0) > 0

    def blend(weights, values):
        return jnp.dot(weights.astype(jnp.bfloat16), with_ones(values), preferred_element_type=jnp.float32)

    def attend(kv_head, carry):
        for head in range(heads):
            row_ref[head * tokens : (head + 1) * tokens, :] = pack_ref[:, head_columns(kv_head * heads + head)]
        fresh = kv_heads * heads
        scores = prompt_scores(row_ref[...], pack_ref[:, head_columns(fresh + kv_head)])
        scores = jnp.where(causal, scores, HIDDEN)
        top = jnp.max(scores, axis=1, keepdims=True)
        top_ref[...] = jnp.broadcast_to(top, top_ref.shape)
        sum_ref[...] = blend(jnp.exp2(scores - top), pack_ref[:, head_columns(fresh + kv_heads + kv_head)])

        regions = striped_ref.shape[0]
        ends = []
        for region in range(regions):
            ends.append((span_ref[0, region] + (QUAD - 1)) // QUAD + (ends[-1] if ends else 0))
        quad_keys, quads = QUAD * block_tokens, CHUNK_BLOCKS // QUAD

        def visit(turn, inner):
            lane = iota((1, quads * quad_keys), 1)
            keys, values = [], []
            bound = jnp.zeros_like(lane)
            least = jnp.zeros_like(lane)
            for i in range(quads):
                quad = turn * quads + i
                region = sum((quad >= end).astype(jnp.int32) for end in ends[:-1])
                start = 0
                for end, number in zip(ends[:-1], range(1, regions)):
                    start = jnp.where(region >= number, end, start)
                done = (quad - start) * QUAD
                amount, base = span_ref[0, region], span_ref[1, region]
                first = jnp.minimum(base + done, room - QUAD)
                part = pl.ds(first, QUAD)
                keys.append(striped_ref[region, kv_head, part].reshape(quad_keys, HD))
                values.append(striped_ref[region, kv_heads + kv_head, part].reshape(quad_keys, HD))
                here = lane // quad_keys == i
                bound = jnp.where(here, (base + amount - first) * block_tokens, bound)
                least = jnp.where(here, (base + done - first) * block_tokens, least)
            keys, values = jnp.concatenate(keys, axis=0), jnp.concatenate(values, axis=0)
            key = lane % quad_keys
            shown = (key < bound) & (key >= least)
            scores = jnp.where(shown, prompt_scores(row_ref[...], keys), HIDDEN)
            old_top = top_ref[...]
            top = jnp.maximum(old_top, jnp.max(scores, axis=1, keepdims=True))
            shrink = jnp.exp2(old_top - top)
            weights = jnp.exp2(scores - jnp.concatenate([top] * (quads * quad_keys // HD), axis=1))
            top_ref[...] = top
            sum_ref[...] = sum_ref[...] * jnp.concatenate([shrink, shrink], axis=1) + blend(weights, values)
            return inner

        lax.fori_loop(0, (ends[-1] + (quads - 1)) // quads, visit, 0)
        for head in range(heads):
            blended = sum_ref[head * tokens : (head + 1) * tokens, :]
            out_ref[:, head_columns(kv_head * heads + head)] = (
                blended[:, :HD] / blended[:, HD:]
            ).astype(jnp.bfloat16)
        return carry

    lax.fori_loop(0, kv_heads, attend, 0)
    if whole_ref is not None:
        width = out_ref.shape[1]
        start = pl.multiple_of(lax.axis_index("seq") % 2 * width, width)
        copy = pltpu.make_async_copy(out_ref, whole_ref.at[:, pl.ds(start, width)], sem)
        copy.start()
        regions, team, _, block_tokens, _ = striped_ref.shape
        slots = regions * team * block_tokens
        picked = (target_ref[:, :1] == iota((tokens, slots), 1)).astype(jnp.bfloat16)
        for tile in range(extra):
            vision_ref[:, tile * LANES : (tile + 1) * LANES] = jnp.dot(
                picked, striped_ref[:, :, room + tile].reshape(slots, LANES), preferred_element_type=jnp.float32
            ).astype(jnp.bfloat16)
        copy.wait()


def put_half_kernel(back_ref, whole_ref, out_ref, sem):
    width = back_ref.shape[1]
    start = pl.multiple_of((1 - lax.axis_index("seq") % 2) * width, width)
    copy = pltpu.make_async_copy(back_ref, out_ref.at[:, pl.ds(start, width)], sem)
    copy.start()
    copy.wait()


def put_half(whole, back):
    return pl.pallas_call(
        put_half_kernel,
        out_shape=jax.ShapeDtypeStruct(whole.shape, whole.dtype),
        in_specs=[pl.BlockSpec(memory_space=pltpu.VMEM), pl.BlockSpec(memory_space=pl.ANY)],
        out_specs=pl.BlockSpec(memory_space=pl.ANY),
        scratch_shapes=[pltpu.SemaphoreType.DMA],
        input_output_aliases={1: 0},
        compiler_params=pltpu.CompilerParams(vmem_limit_bytes=SMALL_VMEM_BYTES),
        name="put_half",
    )(back, whole)


def prompt_attention(kernel, scalars, operands, specs, outs, scratch, keys, name):
    tokens, width = operands[0].shape
    kv_width = operands[1].shape[1]
    whole = lambda shape: pl.BlockSpec(shape, lambda *_: (0,) * len(shape))
    outs = [(tokens, width)] + outs
    return pl.pallas_call(
        kernel,
        out_shape=tuple(jax.ShapeDtypeStruct(shape, jnp.bfloat16) for shape in outs),
        grid_spec=pltpu.PrefetchScalarGridSpec(
            num_scalar_prefetch=len(scalars),
            grid=(1,),
            in_specs=[spec or whole(operand.shape) for operand, spec in zip(operands, specs)],
            out_specs=tuple(whole(shape) for shape in outs),
            scratch_shapes=[
                pltpu.VMEM((QHEADS * tokens, HD), jnp.float32),
                pltpu.VMEM((QHEADS * tokens, 2 * HD), jnp.float32),
            ]
            + scratch,
        ),
        compiler_params=pltpu.CompilerParams(vmem_limit_bytes=VMEM_BYTES),
        cost_estimate=pl.CostEstimate(
            flops=4 * tokens * keys * width,
            bytes_accessed=4 * tokens * width + 2 * keys * kv_width,
            transcendentals=tokens * QHEADS * keys,
        ),
        name=name,
    )(*scalars, *operands)


def listed_prompt(request, live, queries, new_kv, blocks):
    entries, block_tokens = request.shape[1], blocks.shape[1]
    chunks = -(-entries // CHUNK_BLOCKS)
    scratch = [
        pltpu.VMEM((chunks * CHUNK_BLOCKS, block_tokens, new_kv.shape[1]), jnp.bfloat16),
        pltpu.SemaphoreType.DMA((chunks,)),
    ]
    return prompt_attention(
        listed_prompt_kernel, (request, live), (queries, new_kv, blocks),
        (None, None, pl.BlockSpec(memory_space=pl.ANY)), [], scratch,
        entries * block_tokens + queries.shape[0], "listed_prompt",
    )[0]


def striped_prompt(lanes, extra, span, pack, target, striped, pick):
    tokens = pack.shape[0]
    devices, held, block_tokens, _ = striped.shape
    team = lanes // 2
    split = striped.reshape(devices // team, team, held, block_tokens, LANES)
    width = pack.shape[1] - team * HD
    rows = 2 * width // team // HD * tokens
    shapes = [(tokens, 2 * width), (tokens, extra * LANES)] if pick else [(tokens, width)]
    wide_target = jnp.broadcast_to(target, (tokens, extra * LANES))
    vmem = pl.BlockSpec(memory_space=pltpu.VMEM)
    return pl.pallas_call(
        striped_prompt_kernel,
        out_shape=tuple(jax.ShapeDtypeStruct(shape, jnp.bfloat16) for shape in shapes),
        in_specs=[pl.BlockSpec(memory_space=pltpu.SMEM), vmem, vmem, vmem],
        out_specs=(pl.BlockSpec(memory_space=pl.ANY), vmem) if pick else (vmem,),
        scratch_shapes=[
            pltpu.VMEM((rows, HD), jnp.bfloat16),
            pltpu.VMEM((rows, 2 * HD), jnp.float32),
            pltpu.VMEM((rows, HD), jnp.float32),
        ]
        + [pltpu.VMEM((tokens, width), jnp.bfloat16), pltpu.SemaphoreType.DMA] * pick,
        compiler_params=pltpu.CompilerParams(vmem_limit_bytes=SMALL_VMEM_BYTES),
        cost_estimate=pl.CostEstimate(
            flops=4 * tokens * held * block_tokens * width,
            bytes_accessed=4 * tokens * width + 2 * held * block_tokens * team * HD,
            transcendentals=tokens * width // HD * held * block_tokens,
        ),
        name="striped_prompt_pick" if pick else "striped_prompt",
    )(span, pack, wide_target, split)


def stripe_kernel(lanes, steps, cache_ref, *refs):
    out_refs, held_ref, in_sems, out_sems = refs[:-3], refs[-3], refs[-2], refs[-1]
    member = lax.axis_index("seq") % lanes
    team = lanes // 2
    chunks = in_sems.shape[0]
    half = cache_ref.shape[0]
    size = half // chunks
    taken, given = [], []
    for chunk in range(chunks):
        part = pl.ds(chunk * size, size)
        taken.append(pltpu.make_async_copy(cache_ref.at[part], held_ref.at[part], in_sems.at[chunk]))
        taken[-1].start()
    for chunk in range(chunks):
        part = pl.ds(chunk * size, size)
        taken[chunk].wait()
        for place, step in enumerate(steps):
            lane = member ^ step
            parity, column = lane // team, lane % team // 2 * KVH + lane % 2
            for core in range(2):
                start = pl.multiple_of((column + 2 * core) * LANES, LANES)
                given.append(
                    pltpu.make_async_copy(
                        held_ref.at[part, parity, :, pl.ds(start, LANES)],
                        out_refs[place].at[pl.ds(core * half + chunk * size, size)],
                        out_sems.at[chunk, 2 * place + core],
                    )
                )
                given[-1].start()
    for copy in given:
        copy.wait()


def stripe(lanes, steps, kv_cache):
    blocks, block_tokens, width = kv_cache.shape
    chunks = 4
    kv_cache = kv_cache.reshape(blocks // 2, 2, block_tokens, width)
    piece = jax.ShapeDtypeStruct((blocks, block_tokens, LANES), jnp.bfloat16)
    return pl.pallas_call(
        functools.partial(stripe_kernel, lanes, steps),
        out_shape=(piece,) * len(steps),
        in_specs=[pl.BlockSpec(memory_space=pl.ANY)],
        out_specs=(pl.BlockSpec(memory_space=pl.ANY),) * len(steps),
        scratch_shapes=[
            pltpu.VMEM(kv_cache.shape, jnp.bfloat16),
            pltpu.SemaphoreType.DMA((chunks,)),
            pltpu.SemaphoreType.DMA((chunks, 2 * len(steps))),
        ],
        compiler_params=pltpu.CompilerParams(vmem_limit_bytes=VMEM_BYTES),
        name="stripe",
    )(kv_cache)


def gather_kernel(lanes, steps, entries, notes_ref, attended_ref, *refs):
    piece_refs = refs[:lanes]
    out_ref, held_ref, narrow_ref, wide_ref, index_ref, scalar_ref, sems = refs[lanes:]
    blocks = piece_refs[0].shape[0]
    readers, extra = attended_ref.shape[0], attended_ref.shape[1]
    room = out_ref.shape[1] - extra
    half = blocks // 2
    capacity = notes_ref.shape[0] // readers
    column = pl.ds(notes_ref.shape[1] - LANES, LANES)
    noted = pltpu.make_async_copy(notes_ref.at[:, column], narrow_ref, sems.at[lanes + 1])
    noted.start()
    copies = [
        pltpu.make_async_copy(piece_ref, held_ref.at[pl.ds(step * blocks, blocks)], sems.at[step])
        for step, piece_ref in zip(steps, piece_refs)
    ]
    for copy in copies:
        copy.start()

    noted.wait()
    wide_ref[...] = narrow_ref[...].astype(jnp.float32)
    local = wide_ref[pl.ds(0, readers, capacity), :]
    member = wide_ref[pl.ds(1, readers, capacity), :]
    lane = iota((readers, LANES), 1)
    listed = (local >= 0.0) & (lane < entries)
    step = member.astype(jnp.int32) ^ (lax.axis_index("seq") % lanes)
    amount = jnp.sum(listed.astype(jnp.float32), axis=1, keepdims=True).astype(jnp.int32)
    index = jnp.where(listed, step * blocks + local.astype(jnp.int32), 0)
    out_ref[...] = jnp.zeros_like(out_ref)
    index_ref[...] = jnp.where(lane == entries, amount, index)
    to_scalars = pltpu.make_async_copy(index_ref, scalar_ref, sems.at[lanes])
    to_scalars.start()
    to_scalars.wait()
    for copy in copies:
        copy.wait()

    def some_of(reader, chip, base):
        def some(group, inner):
            first = group * ROOM_STEP
            spots = [scalar_ref[reader, first + i] for i in range(ROOM_STEP)]
            places = [jnp.minimum(base + first + i, room) for i in range(ROOM_STEP)]
            for core in range(2):
                tiles = [held_ref[spot + core * half] for spot in spots]
                for place, tile in zip(places, tiles):
                    out_ref[2 * chip + core, place] = tile
            return inner

        return some

    def turn(reader, base):
        amount = scalar_ref[reader, entries]
        some = some_of(reader, reader // 2, base)
        lax.fori_loop(0, (amount + (ROOM_STEP - 1)) // ROOM_STEP, some, 0)
        return jnp.where(reader % 2 == 0, amount, 0)

    lax.fori_loop(0, readers, turn, 0)
    out_ref[:, room:] = attended_ref[...]


def gather_stripes(lanes, steps, room, entries, arrived, attended, pieces):
    blocks, block_tokens, _ = pieces[0].shape
    slots = arrived.shape[0]
    readers, extra = attended.shape[:2]
    shape = (readers, room + extra, block_tokens, LANES)
    return pl.pallas_call(
        functools.partial(gather_kernel, lanes, steps, entries),
        out_shape=jax.ShapeDtypeStruct(shape, jnp.bfloat16),
        in_specs=[pl.BlockSpec(memory_space=pl.ANY), pl.BlockSpec(memory_space=pltpu.VMEM)]
        + [pl.BlockSpec(memory_space=pl.ANY)] * lanes,
        out_specs=pl.BlockSpec(memory_space=pltpu.VMEM),
        scratch_shapes=[
            pltpu.VMEM((lanes * blocks, block_tokens, LANES), jnp.bfloat16),
            pltpu.VMEM((slots, LANES), jnp.bfloat16),
            pltpu.VMEM((slots, LANES), jnp.float32),
            pltpu.VMEM((readers, LANES), jnp.int32),
            pltpu.SMEM((readers, LANES), jnp.int32),
            pltpu.SemaphoreType.DMA((lanes + 2,)),
        ],
        compiler_params=pltpu.CompilerParams(vmem_limit_bytes=SMALL_VMEM_BYTES),
        cost_estimate=pl.CostEstimate(
            flops=0, bytes_accessed=4 * readers * room * block_tokens * LANES, transcendentals=0
        ),
        name="gather_stripes",
    )(arrived, attended, *pieces)


def vision_kernel(
    entries, rooms, rows_ref, w_hbm_ref, out_ref, own_ref, other_ref, choice_ref, w_ref, qkv_ref, blend_ref, wide_ref, sems
):
    slots, vit = rows_ref.shape[0], w_ref.shape[0]
    inner = VHEADS * VHD
    copies = []
    for third in range(3):
        part = pl.ds(third * inner, inner)
        copies.append(pltpu.make_async_copy(w_hbm_ref.at[:, part], w_ref.at[:, part], sems.at[third]))
        copies[-1].start()
    notes = rows_ref[:, vit:].astype(jnp.float32)
    wide_ref[...] = notes
    device = lax.axis_index("seq")
    capacity = slots // out_ref.shape[0]
    first_row = (device - device % 2) * capacity + 2
    amounts = [wide_ref[pl.ds(first_row + i * capacity, 1), :].astype(jnp.int32) for i in range(2)]
    second = device % 2 > 0
    nothing = jnp.zeros_like(amounts[0])
    own_ref[...] = jnp.concatenate(
        [jnp.where(second, amounts[1], amounts[0]), jnp.where(second, amounts[0], nothing)], axis=0
    )
    other_ref[...] = jnp.concatenate(
        [jnp.where(second, amounts[0], amounts[1]), jnp.where(second, nothing, amounts[0])], axis=0
    )
    chips = out_ref.shape[0] // 2
    pooled = wide_ref[pl.ds(2, chips, 2 * capacity), :] + wide_ref[pl.ds(2 + capacity, chips, 2 * capacity), :]
    needed = jnp.max(jnp.where(iota((chips, LANES), 1) < entries, pooled, 0.0)).astype(jnp.int32)
    choice = 0
    for room in rooms:
        choice = choice + jnp.where(needed > room, 1, 0)
    choice_ref[0, 0] = choice
    window_column = jnp.sum(
        jnp.where(iota((slots, LANES), 1) == entries, notes, 0.0), axis=1, keepdims=True
    ).astype(jnp.int32)
    window_row = as_row(window_column)
    itself = iota((slots, slots), 0) == iota((slots, slots), 1)
    allowed = ((window_column == window_row) & (window_row >= 0)) | itself
    blend_ref[...] = jnp.zeros_like(blend_ref)
    for third, copy in enumerate(copies):
        part = slice(third * inner, (third + 1) * inner)
        copy.wait()
        qkv_ref[:, part] = jnp.dot(
            rows_ref[:, :vit], w_ref[:, part], preferred_element_type=jnp.float32
        ).astype(jnp.bfloat16)
    for head in range(VHEADS):
        first, last = head * VHD, (head + 1) * VHD
        low, high = first // LANES * LANES, -(-last // LANES) * LANES
        column = low + iota((slots, high - low), 1)
        mine = (column >= first) & (column < last)
        part = lambda offset: qkv_ref[:, offset + low : offset + high]
        keys = jnp.where(mine, part(inner).astype(jnp.float32), 0.0).astype(jnp.bfloat16)
        values = jnp.where(mine, part(2 * inner).astype(jnp.float32), 0.0).astype(jnp.bfloat16)
        scores = lax.dot_general(
            part(0), keys, (((1,), (1,)), ((), ())), preferred_element_type=jnp.float32
        ) * VHD ** (-0.5)
        scores = jnp.where(allowed, scores, HIDDEN)
        weights = jnp.exp(scores - jnp.max(scores, axis=1, keepdims=True))
        total = jnp.sum(weights, axis=1, keepdims=True)
        blended = jnp.dot(weights.astype(jnp.bfloat16), values, preferred_element_type=jnp.float32)
        blend_ref[:, low:high] += blended / total
    devices, tiles, rows, _ = out_ref.shape
    for tile in range(tiles):
        part = blend_ref[:, tile * LANES : (tile + 1) * LANES].astype(jnp.bfloat16)
        out_ref[:, tile] = part.reshape(devices, rows, LANES)


def vision_tiles(devices, entries, rooms, arrived, w_qkv):
    slots = arrived.shape[0]
    vit, width = w_qkv.shape
    inner = VHEADS * VHD
    return pl.pallas_call(
        functools.partial(vision_kernel, entries, rooms),
        out_shape=(
            jax.ShapeDtypeStruct((devices, inner // LANES, slots // devices, LANES), jnp.bfloat16),
            jax.ShapeDtypeStruct((2, LANES), jnp.int32),
            jax.ShapeDtypeStruct((2, LANES), jnp.int32),
            jax.ShapeDtypeStruct((1, 1), jnp.int32),
        ),
        in_specs=[pl.BlockSpec(memory_space=pltpu.VMEM), pl.BlockSpec(memory_space=pl.ANY)],
        out_specs=(pl.BlockSpec(memory_space=pltpu.VMEM),) * 3 + (pl.BlockSpec(memory_space=pltpu.SMEM),),
        scratch_shapes=[
            pltpu.VMEM((vit, width), jnp.bfloat16),
            pltpu.VMEM((slots, width), jnp.bfloat16),
            pltpu.VMEM((slots, inner), jnp.float32),
            pltpu.VMEM((slots, LANES), jnp.float32),
            pltpu.SemaphoreType.DMA((3,)),
        ],
        compiler_params=pltpu.CompilerParams(vmem_limit_bytes=VMEM_BYTES),
        cost_estimate=pl.CostEstimate(
            flops=2 * slots * vit * width + 4 * slots * slots * inner,
            bytes_accessed=2 * vit * width,
            transcendentals=VHEADS * slots * slots,
        ),
        name="vision_tiles",
    )(arrived, w_qkv)


def pick_kernel(target_ref, *refs):
    out_ref = refs[-1]
    returned = jnp.concatenate([ref[...] for ref in refs[:-1]], axis=0)
    rows, slots = target_ref.shape[0], returned.shape[0]
    picked = (target_ref[...] == iota((rows, slots), 1)).astype(jnp.bfloat16)
    out_ref[...] = jnp.dot(picked, returned, preferred_element_type=jnp.float32).astype(jnp.bfloat16)


def pick_rows(target, *returned):
    return pl.pallas_call(
        pick_kernel,
        out_shape=jax.ShapeDtypeStruct((target.shape[0], returned[0].shape[1]), jnp.bfloat16),
        compiler_params=pltpu.CompilerParams(vmem_limit_bytes=VMEM_BYTES),
        name="pick_rows",
    )(target, *returned)


def window_attention(qkv_rows, windows):
    total_rows = qkv_rows.shape[0]
    inner_width = VHEADS * VHD
    query_heads = qkv_rows[:, :inner_width].reshape(total_rows, VHEADS, VHD)
    key_heads = qkv_rows[:, inner_width : 2 * inner_width].reshape(total_rows, VHEADS, VHD)
    value_heads = qkv_rows[:, 2 * inner_width :].reshape(total_rows, VHEADS, VHD)
    is_live = windows >= 0
    every_row = jnp.arange(total_rows)
    scores = jnp.einsum(
        "qhd,khd->hqk", query_heads, key_heads, preferred_element_type=jnp.float32
    ) * VHD ** (-0.5)
    allowed = (windows[:, None] == windows[None, :]) & is_live[None, :] | (
        every_row[:, None] == every_row[None, :]
    )
    scores = jnp.where(allowed[None], scores, -jnp.inf)
    highest = jnp.max(scores, axis=2, keepdims=True)
    weights = jnp.exp(scores - highest)
    totals = jnp.sum(weights, axis=2)
    blended = jnp.einsum(
        "hqk,khd->qhd",
        weights.astype(jnp.bfloat16),
        value_heads,
        preferred_element_type=jnp.float32,
    )
    pieces = (blended / totals.T[:, :, None]).reshape(total_rows, inner_width)
    return pieces.astype(jnp.bfloat16)


def exchange(rows, devices):
    parts = rows.reshape((devices, rows.shape[0] // devices) + rows.shape[1:])
    return lax.all_to_all(parts, "seq", split_axis=0, concat_axis=0, tiled=True).reshape(rows.shape)


def core_index():
    return lax.axis_index("seq") % 2


def head_half(queries, new_kv, core):
    width, kv_width = queries.shape[1] // 2, new_kv.shape[1] // 4
    part = lambda array, start, size: lax.dynamic_slice_in_dim(array, start, size, 1)
    return jnp.concatenate(
        [
            part(queries, core * width, width),
            part(new_kv, core * kv_width, kv_width),
            part(new_kv, 2 * kv_width + core * kv_width, kv_width),
        ],
        axis=1,
    )


def swap(piece, step, devices):
    return lax.ppermute(piece, "seq", [(i, i ^ step) for i in range(devices)])


def vision_rows(arrived, windows, w_qkv):
    vit = w_qkv.shape[0]
    qkv_rows = jnp.dot(arrived[:, :vit], w_qkv, preferred_element_type=jnp.float32).astype(jnp.bfloat16)
    return window_attention(qkv_rows, windows)


def shards(
    patches,
    row_owner,
    window_slot,
    w_patch,
    vit_gain,
    w_qkv,
    queries,
    new_kv,
    kv_cache,
    block_table,
):
    devices = lax.axis_size("seq")
    vit = w_patch.shape[1]
    capacity = 2 * patches.shape[0] // devices
    slots = devices * capacity
    entries = block_table.shape[1]
    per_owner = 2 * entries // devices
    blocks_dev = kv_cache.shape[0]
    lanes = kv_cache.shape[2] // LANES
    striped = devices == 2 * lanes and lanes == len(STEPS) and capacity == kv_cache.shape[1] and entries + 2 <= LANES
    if striped:
        steps = STEPS
        pieces = stripe(lanes, steps, kv_cache)
        pieces = [swap(piece, step, devices) if step else piece for step, piece in zip(steps, pieces)]
    payload, target, request, live = embed_and_route(
        patches, w_patch, vit_gain, row_owner, window_slot, block_table,
        capacity, slots, per_owner, blocks_dev, lanes if striped else None,
    )
    arrived = exchange(payload, devices)

    if not striped:
        notes = arrived[:, vit : vit + 2].astype(jnp.int32)
        asked = notes[:, 1].reshape(devices, capacity)[:, :per_owner].reshape(devices * per_owner)
        delivered = exchange(kv_cache[jnp.maximum(asked, 0)], devices)
        attended = vision_rows(arrived, notes[:, 0], w_qkv)
        delivered, attended = lax.optimization_barrier((delivered, attended))
        returned = exchange(attended, devices)
        attention_out = listed_prompt(request, live, queries, new_kv, delivered)
        return (pick_rows(target, returned), attention_out)

    rooms = [room for room in ROOMS if room < 2 * entries] + [2 * entries]
    attended, own_span, other_span, choice = vision_tiles(devices, entries, rooms[:-1], arrived, w_qkv)

    def finish(room):
        def run(arrived, attended, target, own_span, other_span, queries, new_kv, *pieces):
            outgoing = gather_stripes(lanes, steps, room, entries, arrived, attended, pieces)
            delivered = exchange(outgoing.reshape((-1,) + outgoing.shape[2:]), devices).reshape(outgoing.shape)
            extra = attended.shape[1]
            own_pack, other_pack = [head_half(queries, new_kv, core) for core in (core_index(), 1 - core_index())]
            other_pack = swap(other_pack, 1, devices)
            (other_out,) = striped_prompt(lanes, extra, other_span, other_pack, target, delivered, False)
            back = swap(other_out, 1, devices)
            own_out, vision_out = striped_prompt(lanes, extra, own_span, own_pack, target, delivered, True)
            return (vision_out, put_half(own_out, back))

        return run

    return lax.switch(
        choice[0, 0], [finish(room) for room in rooms],
        arrived, attended, target, own_span, other_span, queries, new_kv, *pieces,
    )


def solution(mesh):
    in_specs = (
        P(("groups", "seq"), None),
        P(("groups", "seq"), None),
        P(("groups", "seq")),
        P(),
        P(),
        P(),
        P(("groups", "seq"), None),
        P(("groups", "seq"), None),
        P(("groups", "seq"), None, None),
        P(("groups", "seq"), None),
    )
    out_specs = (P(("groups", "seq"), None), P(("groups", "seq"), None))
    return jax.shard_map(shards, mesh=mesh, in_specs=in_specs, out_specs=out_specs, check_vma=False)
```

```python
import functools

import jax
import jax.numpy as jnp
from jax import lax
from jax.experimental import pallas as pl
from jax.experimental.pallas import tpu as pltpu
from jax.sharding import PartitionSpec as P

VHEADS = 8
VHD = 80
QHEADS = 32
KVH = 4
HD = 128
LANES = 128
CHUNK_BLOCKS = 16
HEADS_TILE = 2
LOG2E = 1.4426950408889634
HIDDEN = -1e30
VMEM_BYTES = 56 * 1024 * 1024
ROOM_STEP = 8
QUAD = 4
SMALL_VMEM_BYTES = 24 * 1024 * 1024
ROOMS = (32, 36, 38, 40, 44, 64)
STEPS = (2, 3, 4, 5, 6, 7, 1, 0)


def iota(shape, axis):
    return lax.broadcasted_iota(jnp.int32, shape, axis)


def count(hits, axis):
    return jnp.sum(hits.astype(jnp.float32), axis=axis, keepdims=True).astype(jnp.int32)


def as_row(column):
    size = column.shape[0]
    diagonal = iota((size, size), 0) == iota((size, size), 1)
    return jnp.sum(jnp.where(diagonal, column, 0).astype(jnp.float32), axis=0, keepdims=True).astype(jnp.int32)


def as_column(row):
    size = row.shape[1]
    diagonal = iota((size, size), 0) == iota((size, size), 1)
    return jnp.sum(jnp.where(diagonal, row, 0).astype(jnp.float32), axis=1, keepdims=True).astype(jnp.int32)


def embed_kernel(
    capacity,
    per_owner,
    blocks_dev,
    lanes,
    patches_ref,
    w_ref,
    gain_ref,
    owner_ref,
    window_ref,
    table_ref,
    payload_ref,
    target_ref,
    request_ref,
    live_ref,
    turned_ref,
    embedded_ref,
):
    step = pl.program_id(0)
    width = w_ref.shape[1]

    @pl.when(step == 0)
    def _():
        turned_ref[...] = patches_ref[...].T

    piece = jnp.dot(turned_ref[...], w_ref[...], preferred_element_type=jnp.float32)
    embedded_ref[:, pl.ds(pl.multiple_of(step * width, width), width)] = piece.astype(jnp.bfloat16)

    @pl.when(step == pl.num_programs(0) - 1)
    def _():
        slots = payload_ref.shape[0]
        vit = embedded_ref.shape[1]
        rows = owner_ref.shape[1]
        owner_row = owner_ref[...]
        owner_column = as_column(owner_row)
        same = owner_column == owner_row
        first, second = iota((rows, rows), 0), iota((rows, rows), 1)
        rank_row = count(same & (first < second), 0)
        rank_column = count(same & (second < first), 1)
        target_ref[...] = owner_column * capacity + rank_column
        placed = (owner_row * capacity + rank_row) == iota((slots, rows), 0)
        windows = (
            jnp.sum(jnp.where(placed, window_ref[...] + 1, 0).astype(jnp.float32), axis=1, keepdims=True)
            - 1.0
        )
        note_list(capacity, per_owner, blocks_dev, lanes, windows, table_ref, payload_ref.at[:, vit:], request_ref, live_ref)

        widened = embedded_ref[...].astype(jnp.float32)
        factor = lax.rsqrt(jnp.mean(widened * widened, axis=1, keepdims=True) + 1e-06)
        normed = (widened * factor * gain_ref[...].reshape(1, -1)).astype(jnp.bfloat16)
        payload_ref[:, :vit] = jnp.dot(
            placed.astype(jnp.bfloat16), normed, preferred_element_type=jnp.float32
        ).astype(jnp.bfloat16)


def note_list(capacity, per_owner, blocks_dev, lanes, windows, table_ref, notes_ref, request_ref, live_ref):
    slots = notes_ref.shape[0]
    table_row = table_ref[...]
    entries = table_row.shape[1]
    live_row = table_row >= 0
    holder_row = jnp.where(live_row, table_row // blocks_dev, -1)
    local_row = jnp.where(live_row, table_row % blocks_dev, 0)
    lane = iota((slots, LANES), 1)
    before = iota((entries, entries), 0) < iota((entries, entries), 1)
    if lanes is None:
        holder_rank = count((as_column(holder_row) == holder_row) & before, 0)
        request_row = jnp.where(live_row, holder_row * per_owner + holder_rank, -1)
        first_request = jnp.sum(
            jnp.where(iota((1, entries), 1) == 0, request_row, 0).astype(jnp.float32), axis=1, keepdims=True
        ).astype(jnp.int32)
        request_ref[...] = jnp.where(live_row, request_row, first_request)
        live_ref[...] = jnp.broadcast_to(count(live_row, 1), live_ref.shape)
        placed_row = jnp.where(live_row, holder_row * capacity + holder_rank, -1)
        asked = jnp.sum(
            jnp.where(placed_row == iota((slots, entries), 0), local_row + 1, 0).astype(jnp.float32),
            axis=1,
            keepdims=True,
        )
        notes = jnp.where(lane == 0, windows, jnp.where(lane == 1, asked - 1.0, 0.0))
        notes_ref[...] = notes.astype(jnp.bfloat16)
        return
    team = lanes // 2
    regions = slots // capacity // team
    after = iota((entries, entries), 1) < iota((entries, entries), 0)
    region_row = jnp.where(live_row, holder_row // lanes * 2 + local_row % 2, -1)
    region_column = as_column(region_row)
    region_rank = count((region_column == region_row) & after, 1)
    local_column = as_column(local_row // 2)
    member_column = as_column(jnp.where(live_row, holder_row % lanes, 0))
    place = iota((slots, LANES), 0)
    slot_row, slot_region = place % capacity, place // (capacity * team)
    pad = jnp.zeros((1, LANES - entries), jnp.float32)
    notes = jnp.where(lane == entries, windows, 0.0)
    for region in range(regions):
        listed = (region_column == region) & (region_rank == iota((entries, entries), 1))
        pick = lambda column: jnp.sum(
            jnp.where(listed, column, 0).astype(jnp.float32), axis=0, keepdims=True
        )
        locals_row = jnp.concatenate([pick(local_column + 1) - 1.0, pad], axis=1)
        members_row = jnp.concatenate([pick(member_column), pad], axis=1)
        here = (slot_region == region) & (lane < entries)
        notes = jnp.where(here & (slot_row == 0), locals_row, notes)
        notes = jnp.where(here & (slot_row == 1), members_row, notes)
        amount = count(region_row == region, 1).astype(jnp.float32)
        notes = jnp.where((slot_row == 2) & (lane == region), amount, notes)
    notes_ref[...] = notes.astype(jnp.bfloat16)
    request_ref[...] = jnp.zeros(request_ref.shape, jnp.int32)
    live_ref[...] = jnp.zeros(live_ref.shape, jnp.int32)


def embed_and_route(
    patches, w_patch, vit_gain, row_owner, window_slot, block_table, capacity, slots, per_owner, blocks_dev, lanes
):
    rows, patch = patches.shape
    vit = w_patch.shape[1]
    entries = block_table.shape[1]
    width = vit // 2
    whole = lambda *shape: pl.BlockSpec(shape, lambda step: (0,) * len(shape))
    return pl.pallas_call(
        functools.partial(embed_kernel, capacity, per_owner, blocks_dev, lanes),
        grid=(vit // width,),
        out_shape=(
            jax.ShapeDtypeStruct((slots, vit + LANES), jnp.bfloat16),
            jax.ShapeDtypeStruct((rows, 1), jnp.int32),
            jax.ShapeDtypeStruct((1, entries), jnp.int32),
            jax.ShapeDtypeStruct((1, LANES), jnp.int32),
        ),
        in_specs=[
            whole(patch, rows),
            pl.BlockSpec((patch, width), lambda step: (0, step)),
            whole(vit),
            whole(1, rows),
            whole(1, rows),
            whole(1, entries),
        ],
        out_specs=(whole(slots, vit + LANES), whole(rows, 1), whole(1, entries), whole(1, LANES)),
        scratch_shapes=[pltpu.VMEM((rows, patch), jnp.bfloat16), pltpu.VMEM((rows, vit), jnp.bfloat16)],
        compiler_params=pltpu.CompilerParams(vmem_limit_bytes=VMEM_BYTES),
        cost_estimate=pl.CostEstimate(
            flops=2 * rows * patch * vit + 2 * slots * rows * vit,
            bytes_accessed=2 * patch * vit + 2 * rows * patch + 2 * slots * vit,
            transcendentals=rows,
        ),
        name="embed_and_route",
    )(
        patches.T, w_patch, vit_gain, row_owner.reshape(1, rows),
        window_slot.reshape(1, rows), block_table,
    )


def prompt_groups(query_ref, tile):
    tokens = query_ref.shape[0]
    group_size = QHEADS // KVH
    tile_rows = HEADS_TILE * tokens

    def group_step(group, carry):
        for part in range(group_size // HEADS_TILE):
            head = group * group_size + part * HEADS_TILE
            queries = jnp.concatenate(
                [
                    query_ref[:, pl.ds(pl.multiple_of((head + i) * HD, HD), HD)]
                    for i in range(HEADS_TILE)
                ],
                axis=0,
            )
            tile(group, queries, pl.ds(pl.multiple_of(head * tokens, tile_rows), tile_rows))
        return carry

    lax.fori_loop(0, KVH, group_step, 0)


def prompt_scores(queries, keys):
    return lax.dot_general(
        queries, keys, (((1,), (1,)), ((), ())), preferred_element_type=jnp.float32
    ) * (HD ** (-0.5) * LOG2E)


def with_ones(values):
    return jnp.concatenate([values, jnp.ones_like(values)], axis=1)


def head_columns(head):
    return pl.ds(pl.multiple_of(head * HD, HD), HD)


def prompt_begin(query_ref, fresh_ref, top_ref, sum_ref):
    tokens = query_ref.shape[0]
    causal = iota((tokens, tokens), 1) <= iota((tokens, tokens), 0)
    causal = jnp.concatenate([causal.astype(jnp.int32)] * HEADS_TILE, axis=0) > 0

    def tile(group, queries, rows):
        keys, values = fresh_ref[:, head_columns(group)], fresh_ref[:, head_columns(KVH + group)]
        scores = jnp.where(causal, prompt_scores(queries, keys), HIDDEN)
        top = jnp.max(scores, axis=1, keepdims=True)
        weights = jnp.exp2(scores - top).astype(jnp.bfloat16)
        top_ref[rows, :] = jnp.broadcast_to(top, (scores.shape[0], HD))
        sum_ref[rows, :] = jnp.dot(weights, with_ones(values), preferred_element_type=jnp.float32)

    prompt_groups(query_ref, tile)


def prompt_add(query_ref, top_ref, sum_ref, take, shown):
    chunk_keys = shown.shape[1]

    def tile(group, queries, rows):
        scores = jnp.where(shown, prompt_scores(queries, take(group)), HIDDEN)
        old_top = top_ref[rows, :]
        top = jnp.maximum(old_top, jnp.max(scores, axis=1, keepdims=True))
        shrink = jnp.exp2(old_top - top)
        weights = jnp.exp2(scores - jnp.concatenate([top] * (chunk_keys // HD), axis=1))
        top_ref[rows, :] = top
        sum_ref[rows, :] = sum_ref[rows, :] * jnp.concatenate([shrink, shrink], axis=1) + jnp.dot(
            weights.astype(jnp.bfloat16), with_ones(take(KVH + group)), preferred_element_type=jnp.float32
        )

    prompt_groups(query_ref, tile)


def prompt_end(out_ref, sum_ref):
    tokens = out_ref.shape[0]

    def finish(head, carry):
        blended = sum_ref[pl.ds(pl.multiple_of(head * tokens, tokens), tokens), :]
        out_ref[:, head_columns(head)] = (blended[:, :HD] / blended[:, HD:]).astype(jnp.bfloat16)
        return carry

    lax.fori_loop(0, QHEADS, finish, 0)


def listed_prompt_kernel(
    request_ref, live_ref, query_ref, fresh_ref, blocks_ref, out_ref, top_ref, sum_ref, kv_ref, sems
):
    block_tokens = kv_ref.shape[1]
    chunk_keys = CHUNK_BLOCKS * block_tokens
    live_blocks = live_ref[0, 0]
    chunks = (live_blocks + (CHUNK_BLOCKS - 1)) // CHUNK_BLOCKS

    def fetch(chunk, carry):
        def one(place, inner):
            entry = chunk * CHUNK_BLOCKS + place
            pltpu.make_async_copy(
                blocks_ref.at[request_ref[0, entry]], kv_ref.at[entry], sems.at[chunk]
            ).start()
            return inner

        return lax.fori_loop(0, CHUNK_BLOCKS, one, carry)

    lax.fori_loop(0, chunks, fetch, 0)
    prompt_begin(query_ref, fresh_ref, top_ref, sum_ref)

    def visit(chunk, carry):
        first = chunk * CHUNK_BLOCKS
        pltpu.make_async_copy(
            blocks_ref.at[pl.ds(0, CHUNK_BLOCKS)], kv_ref.at[pl.ds(first, CHUNK_BLOCKS)], sems.at[chunk]
        ).wait()
        shown = iota((1, chunk_keys), 1) < (live_blocks - first) * block_tokens
        take = lambda head: kv_ref[pl.ds(first, CHUNK_BLOCKS), :, head_columns(head)].reshape(chunk_keys, HD)
        prompt_add(query_ref, top_ref, sum_ref, take, shown)
        return carry

    lax.fori_loop(0, chunks, visit, 0)
    prompt_end(out_ref, sum_ref)


def striped_prompt_kernel(span_ref, pack_ref, target_ref, striped_ref, *refs):
    whole_ref, out_refs, (row_ref, sum_ref, top_ref) = None, refs[:-3], refs[-3:]
    out_ref = out_refs[0]
    if len(refs) > 4:
        whole_ref, vision_ref, row_ref, sum_ref, top_ref, out_ref, sem = refs
    tokens = pack_ref.shape[0]
    team = striped_ref.shape[1]
    kv_heads = team // 2
    heads = out_ref.shape[1] // HD // kv_heads
    extra = target_ref.shape[1] // LANES
    room, block_tokens = striped_ref.shape[2] - extra, striped_ref.shape[3]
    causal = iota((tokens, tokens), 1) <= iota((tokens, tokens), 0)
    causal = jnp.concatenate([causal.astype(jnp.int32)] * heads, axis=0) > 0

    def blend(weights, values):
        return jnp.dot(weights.astype(jnp.bfloat16), with_ones(values), preferred_element_type=jnp.float32)

    def attend(kv_head, carry):
        for head in range(heads):
            row_ref[head * tokens : (head + 1) * tokens, :] = pack_ref[:, head_columns(kv_head * heads + head)]
        fresh = kv_heads * heads
        scores = prompt_scores(row_ref[...], pack_ref[:, head_columns(fresh + kv_head)])
        scores = jnp.where(causal, scores, HIDDEN)
        top = jnp.max(scores, axis=1, keepdims=True)
        top_ref[...] = jnp.broadcast_to(top, top_ref.shape)
        sum_ref[...] = blend(jnp.exp2(scores - top), pack_ref[:, head_columns(fresh + kv_heads + kv_head)])

        regions = striped_ref.shape[0]
        ends = []
        for region in range(regions):
            ends.append((span_ref[0, region] + (QUAD - 1)) // QUAD + (ends[-1] if ends else 0))
        quad_keys, quads = QUAD * block_tokens, CHUNK_BLOCKS // QUAD

        def visit(turn, inner):
            lane = iota((1, quads * quad_keys), 1)
            keys, values = [], []
            bound = jnp.zeros_like(lane)
            least = jnp.zeros_like(lane)
            for i in range(quads):
                quad = turn * quads + i
                region = sum((quad >= end).astype(jnp.int32) for end in ends[:-1])
                start = 0
                for end, number in zip(ends[:-1], range(1, regions)):
                    start = jnp.where(region >= number, end, start)
                done = (quad - start) * QUAD
                amount, base = span_ref[0, region], span_ref[1, region]
                first = jnp.minimum(base + done, room - QUAD)
                part = pl.ds(first, QUAD)
                keys.append(striped_ref[region, kv_head, part].reshape(quad_keys, HD))
                values.append(striped_ref[region, kv_heads + kv_head, part].reshape(quad_keys, HD))
                here = lane // quad_keys == i
                bound = jnp.where(here, (base + amount - first) * block_tokens, bound)
                least = jnp.where(here, (base + done - first) * block_tokens, least)
            keys, values = jnp.concatenate(keys, axis=0), jnp.concatenate(values, axis=0)
            key = lane % quad_keys
            shown = (key < bound) & (key >= least)
            scores = jnp.where(shown, prompt_scores(row_ref[...], keys), HIDDEN)
            old_top = top_ref[...]
            top = jnp.maximum(old_top, jnp.max(scores, axis=1, keepdims=True))
            shrink = jnp.exp2(old_top - top)
            weights = jnp.exp2(scores - jnp.concatenate([top] * (quads * quad_keys // HD), axis=1))
            top_ref[...] = top
            sum_ref[...] = sum_ref[...] * jnp.concatenate([shrink, shrink], axis=1) + blend(weights, values)
            return inner

        lax.fori_loop(0, (ends[-1] + (quads - 1)) // quads, visit, 0)
        for head in range(heads):
            blended = sum_ref[head * tokens : (head + 1) * tokens, :]
            out_ref[:, head_columns(kv_head * heads + head)] = (
                blended[:, :HD] / blended[:, HD:]
            ).astype(jnp.bfloat16)
        return carry

    lax.fori_loop(0, kv_heads, attend, 0)
    if whole_ref is not None:
        width = out_ref.shape[1]
        start = pl.multiple_of(lax.axis_index("seq") % 2 * width, width)
        copy = pltpu.make_async_copy(out_ref, whole_ref.at[:, pl.ds(start, width)], sem)
        copy.start()
        regions, team, _, block_tokens, _ = striped_ref.shape
        slots = regions * team * block_tokens
        picked = (target_ref[:, :1] == iota((tokens, slots), 1)).astype(jnp.bfloat16)
        for tile in range(extra):
            vision_ref[:, tile * LANES : (tile + 1) * LANES] = jnp.dot(
                picked, striped_ref[:, :, room + tile].reshape(slots, LANES), preferred_element_type=jnp.float32
            ).astype(jnp.bfloat16)
        copy.wait()


def put_half_kernel(back_ref, whole_ref, out_ref, sem):
    width = back_ref.shape[1]
    start = pl.multiple_of((1 - lax.axis_index("seq") % 2) * width, width)
    copy = pltpu.make_async_copy(back_ref, out_ref.at[:, pl.ds(start, width)], sem)
    copy.start()
    copy.wait()


def put_half(whole, back):
    return pl.pallas_call(
        put_half_kernel,
        out_shape=jax.ShapeDtypeStruct(whole.shape, whole.dtype),
        in_specs=[pl.BlockSpec(memory_space=pltpu.VMEM), pl.BlockSpec(memory_space=pl.ANY)],
        out_specs=pl.BlockSpec(memory_space=pl.ANY),
        scratch_shapes=[pltpu.SemaphoreType.DMA],
        input_output_aliases={1: 0},
        compiler_params=pltpu.CompilerParams(vmem_limit_bytes=SMALL_VMEM_BYTES),
        name="put_half",
    )(back, whole)


def prompt_attention(kernel, scalars, operands, specs, outs, scratch, keys, name):
    tokens, width = operands[0].shape
    kv_width = operands[1].shape[1]
    whole = lambda shape: pl.BlockSpec(shape, lambda *_: (0,) * len(shape))
    outs = [(tokens, width)] + outs
    return pl.pallas_call(
        kernel,
        out_shape=tuple(jax.ShapeDtypeStruct(shape, jnp.bfloat16) for shape in outs),
        grid_spec=pltpu.PrefetchScalarGridSpec(
            num_scalar_prefetch=len(scalars),
            grid=(1,),
            in_specs=[spec or whole(operand.shape) for operand, spec in zip(operands, specs)],
            out_specs=tuple(whole(shape) for shape in outs),
            scratch_shapes=[
                pltpu.VMEM((QHEADS * tokens, HD), jnp.float32),
                pltpu.VMEM((QHEADS * tokens, 2 * HD), jnp.float32),
            ]
            + scratch,
        ),
        compiler_params=pltpu.CompilerParams(vmem_limit_bytes=VMEM_BYTES),
        cost_estimate=pl.CostEstimate(
            flops=4 * tokens * keys * width,
            bytes_accessed=4 * tokens * width + 2 * keys * kv_width,
            transcendentals=tokens * QHEADS * keys,
        ),
        name=name,
    )(*scalars, *operands)


def listed_prompt(request, live, queries, new_kv, blocks):
    entries, block_tokens = request.shape[1], blocks.shape[1]
    chunks = -(-entries // CHUNK_BLOCKS)
    scratch = [
        pltpu.VMEM((chunks * CHUNK_BLOCKS, block_tokens, new_kv.shape[1]), jnp.bfloat16),
        pltpu.SemaphoreType.DMA((chunks,)),
    ]
    return prompt_attention(
        listed_prompt_kernel, (request, live), (queries, new_kv, blocks),
        (None, None, pl.BlockSpec(memory_space=pl.ANY)), [], scratch,
        entries * block_tokens + queries.shape[0], "listed_prompt",
    )[0]


def striped_prompt(lanes, extra, span, pack, target, striped, pick):
    tokens = pack.shape[0]
    devices, held, block_tokens, _ = striped.shape
    team = lanes // 2
    split = striped.reshape(devices // team, team, held, block_tokens, LANES)
    width = pack.shape[1] - team * HD
    rows = 2 * width // team // HD * tokens
    shapes = [(tokens, 2 * width), (tokens, extra * LANES)] if pick else [(tokens, width)]
    wide_target = jnp.broadcast_to(target, (tokens, extra * LANES))
    vmem = pl.BlockSpec(memory_space=pltpu.VMEM)
    return pl.pallas_call(
        striped_prompt_kernel,
        out_shape=tuple(jax.ShapeDtypeStruct(shape, jnp.bfloat16) for shape in shapes),
        in_specs=[pl.BlockSpec(memory_space=pltpu.SMEM), vmem, vmem, vmem],
        out_specs=(pl.BlockSpec(memory_space=pl.ANY), vmem) if pick else (vmem,),
        scratch_shapes=[
            pltpu.VMEM((rows, HD), jnp.bfloat16),
            pltpu.VMEM((rows, 2 * HD), jnp.float32),
            pltpu.VMEM((rows, HD), jnp.float32),
        ]
        + [pltpu.VMEM((tokens, width), jnp.bfloat16), pltpu.SemaphoreType.DMA] * pick,
        compiler_params=pltpu.CompilerParams(vmem_limit_bytes=SMALL_VMEM_BYTES),
        cost_estimate=pl.CostEstimate(
            flops=4 * tokens * held * block_tokens * width,
            bytes_accessed=4 * tokens * width + 2 * held * block_tokens * team * HD,
            transcendentals=tokens * width // HD * held * block_tokens,
        ),
        name="striped_prompt_pick" if pick else "striped_prompt",
    )(span, pack, wide_target, split)


def stripe_kernel(lanes, steps, cache_ref, *refs):
    out_refs, held_ref, in_sems, out_sems = refs[:-3], refs[-3], refs[-2], refs[-1]
    member = lax.axis_index("seq") % lanes
    team = lanes // 2
    chunks = in_sems.shape[0]
    half = cache_ref.shape[0]
    size = half // chunks
    taken, given = [], []
    for chunk in range(chunks):
        part = pl.ds(chunk * size, size)
        taken.append(pltpu.make_async_copy(cache_ref.at[part], held_ref.at[part], in_sems.at[chunk]))
        taken[-1].start()
    for chunk in range(chunks):
        part = pl.ds(chunk * size, size)
        taken[chunk].wait()
        for place, step in enumerate(steps):
            lane = member ^ step
            parity, column = lane // team, lane % team // 2 * KVH + lane % 2
            for core in range(2):
                start = pl.multiple_of((column + 2 * core) * LANES, LANES)
                given.append(
                    pltpu.make_async_copy(
                        held_ref.at[part, parity, :, pl.ds(start, LANES)],
                        out_refs[place].at[pl.ds(core * half + chunk * size, size)],
                        out_sems.at[chunk, 2 * place + core],
                    )
                )
                given[-1].start()
    for copy in given:
        copy.wait()


def stripe(lanes, steps, kv_cache):
    blocks, block_tokens, width = kv_cache.shape
    chunks = 4
    kv_cache = kv_cache.reshape(blocks // 2, 2, block_tokens, width)
    piece = jax.ShapeDtypeStruct((blocks, block_tokens, LANES), jnp.bfloat16)
    return pl.pallas_call(
        functools.partial(stripe_kernel, lanes, steps),
        out_shape=(piece,) * len(steps),
        in_specs=[pl.BlockSpec(memory_space=pl.ANY)],
        out_specs=(pl.BlockSpec(memory_space=pl.ANY),) * len(steps),
        scratch_shapes=[
            pltpu.VMEM(kv_cache.shape, jnp.bfloat16),
            pltpu.SemaphoreType.DMA((chunks,)),
            pltpu.SemaphoreType.DMA((chunks, 2 * len(steps))),
        ],
        compiler_params=pltpu.CompilerParams(vmem_limit_bytes=VMEM_BYTES),
        name="stripe",
    )(kv_cache)


def gather_kernel(lanes, steps, entries, notes_ref, attended_ref, *refs):
    piece_refs = refs[:lanes]
    out_ref, ready_ref, held_ref, narrow_ref, wide_ref, index_ref, scalar_ref, sems, out_sems = refs[lanes:]
    blocks = piece_refs[0].shape[0]
    readers, extra = attended_ref.shape[0], attended_ref.shape[1]
    room = out_ref.shape[1] - extra
    half = blocks // 2
    capacity = notes_ref.shape[0] // readers
    column = pl.ds(notes_ref.shape[1] - LANES, LANES)
    noted = pltpu.make_async_copy(notes_ref.at[:, column], narrow_ref, sems.at[lanes + 1])
    noted.start()
    copies = [
        pltpu.make_async_copy(piece_ref, held_ref.at[pl.ds(step * blocks, blocks)], sems.at[step])
        for step, piece_ref in zip(steps, piece_refs)
    ]
    for copy in copies:
        copy.start()

    noted.wait()
    wide_ref[...] = narrow_ref[...].astype(jnp.float32)
    local = wide_ref[pl.ds(0, readers, capacity), :]
    member = wide_ref[pl.ds(1, readers, capacity), :]
    lane = iota((readers, LANES), 1)
    listed = (local >= 0.0) & (lane < entries)
    step = member.astype(jnp.int32) ^ (lax.axis_index("seq") % lanes)
    amount = jnp.sum(listed.astype(jnp.float32), axis=1, keepdims=True).astype(jnp.int32)
    index = jnp.where(listed, step * blocks + local.astype(jnp.int32), 0)
    ready_ref[...] = jnp.zeros_like(ready_ref)
    index_ref[...] = jnp.where(lane == entries, amount, index)
    to_scalars = pltpu.make_async_copy(index_ref, scalar_ref, sems.at[lanes])
    to_scalars.start()
    to_scalars.wait()
    for copy in copies:
        copy.wait()

    def some_of(reader, chip, base):
        def some(group, inner):
            first = group * ROOM_STEP
            spots = [scalar_ref[reader, first + i] for i in range(ROOM_STEP)]
            places = [jnp.minimum(base + first + i, room) for i in range(ROOM_STEP)]
            for core in range(2):
                tiles = [held_ref[spot + core * half] for spot in spots]
                for place, tile in zip(places, tiles):
                    ready_ref[2 * chip + core, place] = tile
            return inner

        return some

    def give(reader):
        return pltpu.make_async_copy(ready_ref.at[reader], out_ref.at[reader], out_sems.at[reader])

    def turn(chip, carry):
        base = 0
        for part in range(2):
            amount = scalar_ref[2 * chip + part, entries]
            some = some_of(2 * chip + part, chip, base)
            lax.fori_loop(0, (amount + (ROOM_STEP - 1)) // ROOM_STEP, some, 0)
            base = amount
        for core in range(2):
            reader = 2 * chip + core
            ready_ref[reader, room:] = attended_ref[reader]
            give(reader).start()
        return carry

    lax.fori_loop(0, readers // 2, turn, 0)
    for reader in range(readers):
        give(reader).wait()


def gather_stripes(lanes, steps, room, entries, arrived, attended, pieces):
    blocks, block_tokens, _ = pieces[0].shape
    slots = arrived.shape[0]
    readers, extra = attended.shape[:2]
    shape = (readers, room + extra, block_tokens, LANES)
    return pl.pallas_call(
        functools.partial(gather_kernel, lanes, steps, entries),
        out_shape=pltpu.HBM(shape, jnp.bfloat16),
        in_specs=[pl.BlockSpec(memory_space=pl.ANY), pl.BlockSpec(memory_space=pltpu.VMEM)]
        + [pl.BlockSpec(memory_space=pl.ANY)] * lanes,
        out_specs=pl.BlockSpec(memory_space=pl.ANY),
        scratch_shapes=[
            pltpu.VMEM(shape, jnp.bfloat16),
            pltpu.VMEM((lanes * blocks, block_tokens, LANES), jnp.bfloat16),
            pltpu.VMEM((slots, LANES), jnp.bfloat16),
            pltpu.VMEM((slots, LANES), jnp.float32),
            pltpu.VMEM((readers, LANES), jnp.int32),
            pltpu.SMEM((readers, LANES), jnp.int32),
            pltpu.SemaphoreType.DMA((lanes + 2,)),
            pltpu.SemaphoreType.DMA((readers,)),
        ],
        compiler_params=pltpu.CompilerParams(vmem_limit_bytes=SMALL_VMEM_BYTES),
        cost_estimate=pl.CostEstimate(
            flops=0, bytes_accessed=4 * readers * room * block_tokens * LANES, transcendentals=0
        ),
        name="gather_stripes",
    )(arrived, attended, *pieces)


def vision_kernel(
    entries, rooms, rows_ref, w_hbm_ref, out_ref, own_ref, other_ref, choice_ref, w_ref, qkv_ref, blend_ref, wide_ref, sems
):
    slots, vit = rows_ref.shape[0], w_ref.shape[0]
    inner = VHEADS * VHD
    copies = []
    for third in range(3):
        part = pl.ds(third * inner, inner)
        copies.append(pltpu.make_async_copy(w_hbm_ref.at[:, part], w_ref.at[:, part], sems.at[third]))
        copies[-1].start()
    notes = rows_ref[:, vit:].astype(jnp.float32)
    wide_ref[...] = notes
    device = lax.axis_index("seq")
    capacity = slots // out_ref.shape[0]
    first_row = (device - device % 2) * capacity + 2
    amounts = [wide_ref[pl.ds(first_row + i * capacity, 1), :].astype(jnp.int32) for i in range(2)]
    second = device % 2 > 0
    nothing = jnp.zeros_like(amounts[0])
    own_ref[...] = jnp.concatenate(
        [jnp.where(second, amounts[1], amounts[0]), jnp.where(second, amounts[0], nothing)], axis=0
    )
    other_ref[...] = jnp.concatenate(
        [jnp.where(second, amounts[0], amounts[1]), jnp.where(second, nothing, amounts[0])], axis=0
    )
    chips = out_ref.shape[0] // 2
    pooled = wide_ref[pl.ds(2, chips, 2 * capacity), :] + wide_ref[pl.ds(2 + capacity, chips, 2 * capacity), :]
    needed = jnp.max(jnp.where(iota((chips, LANES), 1) < entries, pooled, 0.0)).astype(jnp.int32)
    choice = 0
    for room in rooms:
        choice = choice + jnp.where(needed > room, 1, 0)
    choice_ref[0, 0] = choice
    window_column = jnp.sum(
        jnp.where(iota((slots, LANES), 1) == entries, notes, 0.0), axis=1, keepdims=True
    ).astype(jnp.int32)
    window_row = as_row(window_column)
    itself = iota((slots, slots), 0) == iota((slots, slots), 1)
    allowed = ((window_column == window_row) & (window_row >= 0)) | itself
    blend_ref[...] = jnp.zeros_like(blend_ref)
    for third, copy in enumerate(copies):
        part = slice(third * inner, (third + 1) * inner)
        copy.wait()
        qkv_ref[:, part] = jnp.dot(
            rows_ref[:, :vit], w_ref[:, part], preferred_element_type=jnp.float32
        ).astype(jnp.bfloat16)
    for head in range(VHEADS):
        first, last = head * VHD, (head + 1) * VHD
        low, high = first // LANES * LANES, -(-last // LANES) * LANES
        column = low + iota((slots, high - low), 1)
        mine = (column >= first) & (column < last)
        part = lambda offset: qkv_ref[:, offset + low : offset + high]
        keys = jnp.where(mine, part(inner).astype(jnp.float32), 0.0).astype(jnp.bfloat16)
        values = jnp.where(mine, part(2 * inner).astype(jnp.float32), 0.0).astype(jnp.bfloat16)
        scores = lax.dot_general(
            part(0), keys, (((1,), (1,)), ((), ())), preferred_element_type=jnp.float32
        ) * VHD ** (-0.5)
        scores = jnp.where(allowed, scores, HIDDEN)
        weights = jnp.exp(scores - jnp.max(scores, axis=1, keepdims=True))
        total = jnp.sum(weights, axis=1, keepdims=True)
        blended = jnp.dot(weights.astype(jnp.bfloat16), values, preferred_element_type=jnp.float32)
        blend_ref[:, low:high] += blended / total
    devices, tiles, rows, _ = out_ref.shape
    for tile in range(tiles):
        part = blend_ref[:, tile * LANES : (tile + 1) * LANES].astype(jnp.bfloat16)
        out_ref[:, tile] = part.reshape(devices, rows, LANES)


def vision_tiles(devices, entries, rooms, arrived, w_qkv):
    slots = arrived.shape[0]
    vit, width = w_qkv.shape
    inner = VHEADS * VHD
    return pl.pallas_call(
        functools.partial(vision_kernel, entries, rooms),
        out_shape=(
            jax.ShapeDtypeStruct((devices, inner // LANES, slots // devices, LANES), jnp.bfloat16),
            jax.ShapeDtypeStruct((2, LANES), jnp.int32),
            jax.ShapeDtypeStruct((2, LANES), jnp.int32),
            jax.ShapeDtypeStruct((1, 1), jnp.int32),
        ),
        in_specs=[pl.BlockSpec(memory_space=pltpu.VMEM), pl.BlockSpec(memory_space=pl.ANY)],
        out_specs=(pl.BlockSpec(memory_space=pltpu.VMEM),) * 3 + (pl.BlockSpec(memory_space=pltpu.SMEM),),
        scratch_shapes=[
            pltpu.VMEM((vit, width), jnp.bfloat16),
            pltpu.VMEM((slots, width), jnp.bfloat16),
            pltpu.VMEM((slots, inner), jnp.float32),
            pltpu.VMEM((slots, LANES), jnp.float32),
            pltpu.SemaphoreType.DMA((3,)),
        ],
        compiler_params=pltpu.CompilerParams(vmem_limit_bytes=VMEM_BYTES),
        cost_estimate=pl.CostEstimate(
            flops=2 * slots * vit * width + 4 * slots * slots * inner,
            bytes_accessed=2 * vit * width,
            transcendentals=VHEADS * slots * slots,
        ),
        name="vision_tiles",
    )(arrived, w_qkv)


def pick_kernel(target_ref, *refs):
    out_ref = refs[-1]
    returned = jnp.concatenate([ref[...] for ref in refs[:-1]], axis=0)
    rows, slots = target_ref.shape[0], returned.shape[0]
    picked = (target_ref[...] == iota((rows, slots), 1)).astype(jnp.bfloat16)
    out_ref[...] = jnp.dot(picked, returned, preferred_element_type=jnp.float32).astype(jnp.bfloat16)


def pick_rows(target, *returned):
    return pl.pallas_call(
        pick_kernel,
        out_shape=jax.ShapeDtypeStruct((target.shape[0], returned[0].shape[1]), jnp.bfloat16),
        compiler_params=pltpu.CompilerParams(vmem_limit_bytes=VMEM_BYTES),
        name="pick_rows",
    )(target, *returned)


def window_attention(qkv_rows, windows):
    total_rows = qkv_rows.shape[0]
    inner_width = VHEADS * VHD
    query_heads = qkv_rows[:, :inner_width].reshape(total_rows, VHEADS, VHD)
    key_heads = qkv_rows[:, inner_width : 2 * inner_width].reshape(total_rows, VHEADS, VHD)
    value_heads = qkv_rows[:, 2 * inner_width :].reshape(total_rows, VHEADS, VHD)
    is_live = windows >= 0
    every_row = jnp.arange(total_rows)
    scores = jnp.einsum(
        "qhd,khd->hqk", query_heads, key_heads, preferred_element_type=jnp.float32
    ) * VHD ** (-0.5)
    allowed = (windows[:, None] == windows[None, :]) & is_live[None, :] | (
        every_row[:, None] == every_row[None, :]
    )
    scores = jnp.where(allowed[None], scores, -jnp.inf)
    highest = jnp.max(scores, axis=2, keepdims=True)
    weights = jnp.exp(scores - highest)
    totals = jnp.sum(weights, axis=2)
    blended = jnp.einsum(
        "hqk,khd->qhd",
        weights.astype(jnp.bfloat16),
        value_heads,
        preferred_element_type=jnp.float32,
    )
    pieces = (blended / totals.T[:, :, None]).reshape(total_rows, inner_width)
    return pieces.astype(jnp.bfloat16)


def exchange(rows, devices):
    parts = rows.reshape((devices, rows.shape[0] // devices) + rows.shape[1:])
    return lax.all_to_all(parts, "seq", split_axis=0, concat_axis=0, tiled=True).reshape(rows.shape)


def core_index():
    return lax.axis_index("seq") % 2


def head_half(queries, new_kv, core):
    width, kv_width = queries.shape[1] // 2, new_kv.shape[1] // 4
    part = lambda array, start, size: lax.dynamic_slice_in_dim(array, start, size, 1)
    return jnp.concatenate(
        [
            part(queries, core * width, width),
            part(new_kv, core * kv_width, kv_width),
            part(new_kv, 2 * kv_width + core * kv_width, kv_width),
        ],
        axis=1,
    )


def swap(piece, step, devices):
    return lax.ppermute(piece, "seq", [(i, i ^ step) for i in range(devices)])


def vision_rows(arrived, windows, w_qkv):
    vit = w_qkv.shape[0]
    qkv_rows = jnp.dot(arrived[:, :vit], w_qkv, preferred_element_type=jnp.float32).astype(jnp.bfloat16)
    return window_attention(qkv_rows, windows)


def shards(
    patches,
    row_owner,
    window_slot,
    w_patch,
    vit_gain,
    w_qkv,
    queries,
    new_kv,
    kv_cache,
    block_table,
):
    devices = lax.axis_size("seq")
    vit = w_patch.shape[1]
    capacity = 2 * patches.shape[0] // devices
    slots = devices * capacity
    entries = block_table.shape[1]
    per_owner = 2 * entries // devices
    blocks_dev = kv_cache.shape[0]
    lanes = kv_cache.shape[2] // LANES
    striped = devices == 2 * lanes and lanes == len(STEPS) and capacity == kv_cache.shape[1] and entries + 2 <= LANES
    if striped:
        steps = STEPS
        pieces = stripe(lanes, steps, kv_cache)
        pieces = [swap(piece, step, devices) if step else piece for step, piece in zip(steps, pieces)]
    payload, target, request, live = embed_and_route(
        patches, w_patch, vit_gain, row_owner, window_slot, block_table,
        capacity, slots, per_owner, blocks_dev, lanes if striped else None,
    )
    arrived = exchange(payload, devices)

    if not striped:
        notes = arrived[:, vit : vit + 2].astype(jnp.int32)
        asked = notes[:, 1].reshape(devices, capacity)[:, :per_owner].reshape(devices * per_owner)
        delivered = exchange(kv_cache[jnp.maximum(asked, 0)], devices)
        attended = vision_rows(arrived, notes[:, 0], w_qkv)
        delivered, attended = lax.optimization_barrier((delivered, attended))
        returned = exchange(attended, devices)
        attention_out = listed_prompt(request, live, queries, new_kv, delivered)
        return (pick_rows(target, returned), attention_out)

    rooms = [room for room in ROOMS if room < 2 * entries] + [2 * entries]
    attended, own_span, other_span, choice = vision_tiles(devices, entries, rooms[:-1], arrived, w_qkv)

    def finish(room):
        def run(arrived, attended, target, own_span, other_span, queries, new_kv, *pieces):
            outgoing = gather_stripes(lanes, steps, room, entries, arrived, attended, pieces)
            delivered = exchange(outgoing.reshape((-1,) + outgoing.shape[2:]), devices).reshape(outgoing.shape)
            extra = attended.shape[1]
            own_pack, other_pack = [head_half(queries, new_kv, core) for core in (core_index(), 1 - core_index())]
            other_pack = swap(other_pack, 1, devices)
            (other_out,) = striped_prompt(lanes, extra, other_span, other_pack, target, delivered, False)
            back = swap(other_out, 1, devices)
            own_out, vision_out = striped_prompt(lanes, extra, own_span, own_pack, target, delivered, True)
            return (vision_out, put_half(own_out, back))

        return run

    return lax.switch(
        choice[0, 0], [finish(room) for room in rooms],
        arrived, attended, target, own_span, other_span, queries, new_kv, *pieces,
    )


def solution(mesh):
    in_specs = (
        P(("groups", "seq"), None),
        P(("groups", "seq"), None),
        P(("groups", "seq")),
        P(),
        P(),
        P(),
        P(("groups", "seq"), None),
        P(("groups", "seq"), None),
        P(("groups", "seq"), None, None),
        P(("groups", "seq"), None),
    )
    out_specs = (P(("groups", "seq"), None), P(("groups", "seq"), None))
    return jax.shard_map(shards, mesh=mesh, in_specs=in_specs, out_specs=out_specs, check_vma=False)
```

```python
import functools

import jax
import jax.numpy as jnp
from jax import lax
from jax.experimental import pallas as pl
from jax.experimental.pallas import tpu as pltpu
from jax.sharding import PartitionSpec as P

VHEADS = 8
VHD = 80
QHEADS = 32
KVH = 4
HD = 128
LANES = 128
CHUNK_BLOCKS = 16
HEADS_TILE = 2
LOG2E = 1.4426950408889634
HIDDEN = -1e30
VMEM_BYTES = 56 * 1024 * 1024
ROOM_STEP = 8
QUAD = 4
SMALL_VMEM_BYTES = 24 * 1024 * 1024
ROOMS = (32, 36, 38, 40, 44, 64)
STEPS = (2, 3, 4, 5, 6, 7, 1, 0)


def iota(shape, axis):
    return lax.broadcasted_iota(jnp.int32, shape, axis)


def count(hits, axis):
    return jnp.sum(hits.astype(jnp.float32), axis=axis, keepdims=True).astype(jnp.int32)


def as_row(column):
    size = column.shape[0]
    diagonal = iota((size, size), 0) == iota((size, size), 1)
    return jnp.sum(jnp.where(diagonal, column, 0).astype(jnp.float32), axis=0, keepdims=True).astype(jnp.int32)


def as_column(row):
    size = row.shape[1]
    diagonal = iota((size, size), 0) == iota((size, size), 1)
    return jnp.sum(jnp.where(diagonal, row, 0).astype(jnp.float32), axis=1, keepdims=True).astype(jnp.int32)


def embed_kernel(
    capacity,
    per_owner,
    blocks_dev,
    lanes,
    patches_ref,
    w_ref,
    gain_ref,
    owner_ref,
    window_ref,
    table_ref,
    payload_ref,
    target_ref,
    request_ref,
    live_ref,
    turned_ref,
    embedded_ref,
):
    step = pl.program_id(0)
    width = w_ref.shape[1]

    @pl.when(step == 0)
    def _():
        turned_ref[...] = patches_ref[...].T

    piece = jnp.dot(turned_ref[...], w_ref[...], preferred_element_type=jnp.float32)
    embedded_ref[:, pl.ds(pl.multiple_of(step * width, width), width)] = piece.astype(jnp.bfloat16)

    @pl.when(step == pl.num_programs(0) - 1)
    def _():
        slots = payload_ref.shape[0]
        vit = embedded_ref.shape[1]
        rows = owner_ref.shape[1]
        owner_row = owner_ref[...]
        owner_column = as_column(owner_row)
        same = owner_column == owner_row
        first, second = iota((rows, rows), 0), iota((rows, rows), 1)
        rank_row = count(same & (first < second), 0)
        rank_column = count(same & (second < first), 1)
        target_ref[...] = owner_column * capacity + rank_column
        placed = (owner_row * capacity + rank_row) == iota((slots, rows), 0)
        windows = (
            jnp.sum(jnp.where(placed, window_ref[...] + 1, 0).astype(jnp.float32), axis=1, keepdims=True)
            - 1.0
        )
        note_list(capacity, per_owner, blocks_dev, lanes, windows, table_ref, payload_ref.at[:, vit:], request_ref, live_ref)

        widened = embedded_ref[...].astype(jnp.float32)
        factor = lax.rsqrt(jnp.mean(widened * widened, axis=1, keepdims=True) + 1e-06)
        normed = (widened * factor * gain_ref[...].reshape(1, -1)).astype(jnp.bfloat16)
        payload_ref[:, :vit] = jnp.dot(
            placed.astype(jnp.bfloat16), normed, preferred_element_type=jnp.float32
        ).astype(jnp.bfloat16)


def note_list(capacity, per_owner, blocks_dev, lanes, windows, table_ref, notes_ref, request_ref, live_ref):
    slots = notes_ref.shape[0]
    table_row = table_ref[...]
    entries = table_row.shape[1]
    live_row = table_row >= 0
    holder_row = jnp.where(live_row, table_row // blocks_dev, -1)
    local_row = jnp.where(live_row, table_row % blocks_dev, 0)
    lane = iota((slots, LANES), 1)
    before = iota((entries, entries), 0) < iota((entries, entries), 1)
    if lanes is None:
        holder_rank = count((as_column(holder_row) == holder_row) & before, 0)
        request_row = jnp.where(live_row, holder_row * per_owner + holder_rank, -1)
        first_request = jnp.sum(
            jnp.where(iota((1, entries), 1) == 0, request_row, 0).astype(jnp.float32), axis=1, keepdims=True
        ).astype(jnp.int32)
        request_ref[...] = jnp.where(live_row, request_row, first_request)
        live_ref[...] = jnp.broadcast_to(count(live_row, 1), live_ref.shape)
        placed_row = jnp.where(live_row, holder_row * capacity + holder_rank, -1)
        asked = jnp.sum(
            jnp.where(placed_row == iota((slots, entries), 0), local_row + 1, 0).astype(jnp.float32),
            axis=1,
            keepdims=True,
        )
        notes = jnp.where(lane == 0, windows, jnp.where(lane == 1, asked - 1.0, 0.0))
        notes_ref[...] = notes.astype(jnp.bfloat16)
        return
    team = lanes // 2
    regions = slots // capacity // team
    after = iota((entries, entries), 1) < iota((entries, entries), 0)
    region_row = jnp.where(live_row, holder_row // lanes * 2 + local_row % 2, -1)
    region_column = as_column(region_row)
    region_rank = count((region_column == region_row) & after, 1)
    local_column = as_column(local_row // 2)
    member_column = as_column(jnp.where(live_row, holder_row % lanes, 0))
    place = iota((slots, LANES), 0)
    slot_row, slot_region = place % capacity, place // (capacity * team)
    pad = jnp.zeros((1, LANES - entries), jnp.float32)
    notes = jnp.where(lane == entries, windows, 0.0)
    for region in range(regions):
        listed = (region_column == region) & (region_rank == iota((entries, entries), 1))
        pick = lambda column: jnp.sum(
            jnp.where(listed, column, 0).astype(jnp.float32), axis=0, keepdims=True
        )
        locals_row = jnp.concatenate([pick(local_column + 1) - 1.0, pad], axis=1)
        members_row = jnp.concatenate([pick(member_column), pad], axis=1)
        here = (slot_region == region) & (lane < entries)
        notes = jnp.where(here & (slot_row == 0), locals_row, notes)
        notes = jnp.where(here & (slot_row == 1), members_row, notes)
        amount = count(region_row == region, 1).astype(jnp.float32)
        notes = jnp.where((slot_row == 2) & (lane == region), amount, notes)
    notes_ref[...] = notes.astype(jnp.bfloat16)
    request_ref[...] = jnp.zeros(request_ref.shape, jnp.int32)
    live_ref[...] = jnp.zeros(live_ref.shape, jnp.int32)


def embed_and_route(
    patches, w_patch, vit_gain, row_owner, window_slot, block_table, capacity, slots, per_owner, blocks_dev, lanes
):
    rows, patch = patches.shape
    vit = w_patch.shape[1]
    entries = block_table.shape[1]
    width = vit // 2
    whole = lambda *shape: pl.BlockSpec(shape, lambda step: (0,) * len(shape))
    return pl.pallas_call(
        functools.partial(embed_kernel, capacity, per_owner, blocks_dev, lanes),
        grid=(vit // width,),
        out_shape=(
            jax.ShapeDtypeStruct((slots, vit + LANES), jnp.bfloat16),
            jax.ShapeDtypeStruct((rows, 1), jnp.int32),
            jax.ShapeDtypeStruct((1, entries), jnp.int32),
            jax.ShapeDtypeStruct((1, LANES), jnp.int32),
        ),
        in_specs=[
            whole(patch, rows),
            pl.BlockSpec((patch, width), lambda step: (0, step)),
            whole(vit),
            whole(1, rows),
            whole(1, rows),
            whole(1, entries),
        ],
        out_specs=(whole(slots, vit + LANES), whole(rows, 1), whole(1, entries), whole(1, LANES)),
        scratch_shapes=[pltpu.VMEM((rows, patch), jnp.bfloat16), pltpu.VMEM((rows, vit), jnp.bfloat16)],
        compiler_params=pltpu.CompilerParams(vmem_limit_bytes=VMEM_BYTES),
        cost_estimate=pl.CostEstimate(
            flops=2 * rows * patch * vit + 2 * slots * rows * vit,
            bytes_accessed=2 * patch * vit + 2 * rows * patch + 2 * slots * vit,
            transcendentals=rows,
        ),
        name="embed_and_route",
    )(
        patches.T, w_patch, vit_gain, row_owner.reshape(1, rows),
        window_slot.reshape(1, rows), block_table,
    )


def prompt_groups(query_ref, tile):
    tokens = query_ref.shape[0]
    group_size = QHEADS // KVH
    tile_rows = HEADS_TILE * tokens

    def group_step(group, carry):
        for part in range(group_size // HEADS_TILE):
            head = group * group_size + part * HEADS_TILE
            queries = jnp.concatenate(
                [
                    query_ref[:, pl.ds(pl.multiple_of((head + i) * HD, HD), HD)]
                    for i in range(HEADS_TILE)
                ],
                axis=0,
            )
            tile(group, queries, pl.ds(pl.multiple_of(head * tokens, tile_rows), tile_rows))
        return carry

    lax.fori_loop(0, KVH, group_step, 0)


def prompt_scores(queries, keys):
    return lax.dot_general(
        queries, keys, (((1,), (1,)), ((), ())), preferred_element_type=jnp.float32
    ) * (HD ** (-0.5) * LOG2E)


def with_ones(values):
    return jnp.concatenate([values, jnp.ones_like(values)], axis=1)


def head_columns(head):
    return pl.ds(pl.multiple_of(head * HD, HD), HD)


def prompt_begin(query_ref, fresh_ref, top_ref, sum_ref):
    tokens = query_ref.shape[0]
    causal = iota((tokens, tokens), 1) <= iota((tokens, tokens), 0)
    causal = jnp.concatenate([causal.astype(jnp.int32)] * HEADS_TILE, axis=0) > 0

    def tile(group, queries, rows):
        keys, values = fresh_ref[:, head_columns(group)], fresh_ref[:, head_columns(KVH + group)]
        scores = jnp.where(causal, prompt_scores(queries, keys), HIDDEN)
        top = jnp.max(scores, axis=1, keepdims=True)
        weights = jnp.exp2(scores - top).astype(jnp.bfloat16)
        top_ref[rows, :] = jnp.broadcast_to(top, (scores.shape[0], HD))
        sum_ref[rows, :] = jnp.dot(weights, with_ones(values), preferred_element_type=jnp.float32)

    prompt_groups(query_ref, tile)


def prompt_add(query_ref, top_ref, sum_ref, take, shown):
    chunk_keys = shown.shape[1]

    def tile(group, queries, rows):
        scores = jnp.where(shown, prompt_scores(queries, take(group)), HIDDEN)
        old_top = top_ref[rows, :]
        top = jnp.maximum(old_top, jnp.max(scores, axis=1, keepdims=True))
        shrink = jnp.exp2(old_top - top)
        weights = jnp.exp2(scores - jnp.concatenate([top] * (chunk_keys // HD), axis=1))
        top_ref[rows, :] = top
        sum_ref[rows, :] = sum_ref[rows, :] * jnp.concatenate([shrink, shrink], axis=1) + jnp.dot(
            weights.astype(jnp.bfloat16), with_ones(take(KVH + group)), preferred_element_type=jnp.float32
        )

    prompt_groups(query_ref, tile)


def prompt_end(out_ref, sum_ref):
    tokens = out_ref.shape[0]

    def finish(head, carry):
        blended = sum_ref[pl.ds(pl.multiple_of(head * tokens, tokens), tokens), :]
        out_ref[:, head_columns(head)] = (blended[:, :HD] / blended[:, HD:]).astype(jnp.bfloat16)
        return carry

    lax.fori_loop(0, QHEADS, finish, 0)


def listed_prompt_kernel(
    request_ref, live_ref, query_ref, fresh_ref, blocks_ref, out_ref, top_ref, sum_ref, kv_ref, sems
):
    block_tokens = kv_ref.shape[1]
    chunk_keys = CHUNK_BLOCKS * block_tokens
    live_blocks = live_ref[0, 0]
    chunks = (live_blocks + (CHUNK_BLOCKS - 1)) // CHUNK_BLOCKS

    def fetch(chunk, carry):
        def one(place, inner):
            entry = chunk * CHUNK_BLOCKS + place
            pltpu.make_async_copy(
                blocks_ref.at[request_ref[0, entry]], kv_ref.at[entry], sems.at[chunk]
            ).start()
            return inner

        return lax.fori_loop(0, CHUNK_BLOCKS, one, carry)

    lax.fori_loop(0, chunks, fetch, 0)
    prompt_begin(query_ref, fresh_ref, top_ref, sum_ref)

    def visit(chunk, carry):
        first = chunk * CHUNK_BLOCKS
        pltpu.make_async_copy(
            blocks_ref.at[pl.ds(0, CHUNK_BLOCKS)], kv_ref.at[pl.ds(first, CHUNK_BLOCKS)], sems.at[chunk]
        ).wait()
        shown = iota((1, chunk_keys), 1) < (live_blocks - first) * block_tokens
        take = lambda head: kv_ref[pl.ds(first, CHUNK_BLOCKS), :, head_columns(head)].reshape(chunk_keys, HD)
        prompt_add(query_ref, top_ref, sum_ref, take, shown)
        return carry

    lax.fori_loop(0, chunks, visit, 0)
    prompt_end(out_ref, sum_ref)


def striped_prompt_kernel(span_ref, pack_ref, target_ref, striped_ref, *refs):
    whole_ref, out_refs, (row_ref, sum_ref, top_ref) = None, refs[:-3], refs[-3:]
    out_ref = out_refs[0]
    if len(refs) > 4:
        whole_ref, vision_ref, row_ref, sum_ref, top_ref, out_ref, sem = refs
    tokens = pack_ref.shape[0]
    team = striped_ref.shape[1]
    kv_heads = team // 2
    heads = out_ref.shape[1] // HD // kv_heads
    extra = target_ref.shape[1] // LANES
    room, block_tokens = striped_ref.shape[2] - extra, striped_ref.shape[3]
    causal = iota((tokens, tokens), 1) <= iota((tokens, tokens), 0)
    causal = jnp.concatenate([causal.astype(jnp.int32)] * heads, axis=0) > 0

    def blend(weights, values):
        return jnp.dot(weights.astype(jnp.bfloat16), with_ones(values), preferred_element_type=jnp.float32)

    def attend(kv_head, carry):
        for head in range(heads):
            row_ref[head * tokens : (head + 1) * tokens, :] = pack_ref[:, head_columns(kv_head * heads + head)]
        fresh = kv_heads * heads
        scores = prompt_scores(row_ref[...], pack_ref[:, head_columns(fresh + kv_head)])
        scores = jnp.where(causal, scores, HIDDEN)
        top = jnp.max(scores, axis=1, keepdims=True)
        top_ref[...] = jnp.broadcast_to(top, top_ref.shape)
        sum_ref[...] = blend(jnp.exp2(scores - top), pack_ref[:, head_columns(fresh + kv_heads + kv_head)])

        regions = striped_ref.shape[0]
        ends = []
        for region in range(regions):
            ends.append((span_ref[0, region] + (QUAD - 1)) // QUAD + (ends[-1] if ends else 0))
        quad_keys, quads = QUAD * block_tokens, CHUNK_BLOCKS // QUAD

        def visit(turn, inner):
            lane = iota((1, quads * quad_keys), 1)
            keys, values = [], []
            bound = jnp.zeros_like(lane)
            least = jnp.zeros_like(lane)
            for i in range(quads):
                quad = turn * quads + i
                region = sum((quad >= end).astype(jnp.int32) for end in ends[:-1])
                start = 0
                for end, number in zip(ends[:-1], range(1, regions)):
                    start = jnp.where(region >= number, end, start)
                done = (quad - start) * QUAD
                amount, base = span_ref[0, region], span_ref[1, region]
                first = jnp.minimum(base + done, room - QUAD)
                part = pl.ds(first, QUAD)
                keys.append(striped_ref[region, kv_head, part].reshape(quad_keys, HD))
                values.append(striped_ref[region, kv_heads + kv_head, part].reshape(quad_keys, HD))
                here = lane // quad_keys == i
                bound = jnp.where(here, (base + amount - first) * block_tokens, bound)
                least = jnp.where(here, (base + done - first) * block_tokens, least)
            keys, values = jnp.concatenate(keys, axis=0), jnp.concatenate(values, axis=0)
            key = lane % quad_keys
            shown = (key < bound) & (key >= least)
            scores = jnp.where(shown, prompt_scores(row_ref[...], keys), HIDDEN)
            old_top = top_ref[...]
            top = jnp.maximum(old_top, jnp.max(scores, axis=1, keepdims=True))
            shrink = jnp.exp2(old_top - top)
            weights = jnp.exp2(scores - jnp.concatenate([top] * (quads * quad_keys // HD), axis=1))
            top_ref[...] = top
            sum_ref[...] = sum_ref[...] * jnp.concatenate([shrink, shrink], axis=1) + blend(weights, values)
            return inner

        lax.fori_loop(0, (ends[-1] + (quads - 1)) // quads, visit, 0)
        for head in range(heads):
            blended = sum_ref[head * tokens : (head + 1) * tokens, :]
            out_ref[:, head_columns(kv_head * heads + head)] = (
                blended[:, :HD] / blended[:, HD:]
            ).astype(jnp.bfloat16)
        return carry

    lax.fori_loop(0, kv_heads, attend, 0)
    if whole_ref is not None:
        width = out_ref.shape[1]
        start = pl.multiple_of(lax.axis_index("seq") % 2 * width, width)
        copy = pltpu.make_async_copy(out_ref, whole_ref.at[:, pl.ds(start, width)], sem)
        copy.start()
        regions, team, _, block_tokens, _ = striped_ref.shape
        slots = regions * team * block_tokens
        picked = (target_ref[:, :1] == iota((tokens, slots), 1)).astype(jnp.bfloat16)
        for tile in range(extra):
            vision_ref[:, tile * LANES : (tile + 1) * LANES] = jnp.dot(
                picked, striped_ref[:, :, room + tile].reshape(slots, LANES), preferred_element_type=jnp.float32
            ).astype(jnp.bfloat16)
        copy.wait()


def put_half_kernel(back_ref, whole_ref, out_ref, sem):
    width = back_ref.shape[1]
    start = pl.multiple_of((1 - lax.axis_index("seq") % 2) * width, width)
    copy = pltpu.make_async_copy(back_ref, out_ref.at[:, pl.ds(start, width)], sem)
    copy.start()
    copy.wait()


def put_half(whole, back):
    return pl.pallas_call(
        put_half_kernel,
        out_shape=jax.ShapeDtypeStruct(whole.shape, whole.dtype),
        in_specs=[pl.BlockSpec(memory_space=pltpu.VMEM), pl.BlockSpec(memory_space=pl.ANY)],
        out_specs=pl.BlockSpec(memory_space=pl.ANY),
        scratch_shapes=[pltpu.SemaphoreType.DMA],
        input_output_aliases={1: 0},
        compiler_params=pltpu.CompilerParams(vmem_limit_bytes=SMALL_VMEM_BYTES),
        name="put_half",
    )(back, whole)


def prompt_attention(kernel, scalars, operands, specs, outs, scratch, keys, name):
    tokens, width = operands[0].shape
    kv_width = operands[1].shape[1]
    whole = lambda shape: pl.BlockSpec(shape, lambda *_: (0,) * len(shape))
    outs = [(tokens, width)] + outs
    return pl.pallas_call(
        kernel,
        out_shape=tuple(jax.ShapeDtypeStruct(shape, jnp.bfloat16) for shape in outs),
        grid_spec=pltpu.PrefetchScalarGridSpec(
            num_scalar_prefetch=len(scalars),
            grid=(1,),
            in_specs=[spec or whole(operand.shape) for operand, spec in zip(operands, specs)],
            out_specs=tuple(whole(shape) for shape in outs),
            scratch_shapes=[
                pltpu.VMEM((QHEADS * tokens, HD), jnp.float32),
                pltpu.VMEM((QHEADS * tokens, 2 * HD), jnp.float32),
            ]
            + scratch,
        ),
        compiler_params=pltpu.CompilerParams(vmem_limit_bytes=VMEM_BYTES),
        cost_estimate=pl.CostEstimate(
            flops=4 * tokens * keys * width,
            bytes_accessed=4 * tokens * width + 2 * keys * kv_width,
            transcendentals=tokens * QHEADS * keys,
        ),
        name=name,
    )(*scalars, *operands)


def listed_prompt(request, live, queries, new_kv, blocks):
    entries, block_tokens = request.shape[1], blocks.shape[1]
    chunks = -(-entries // CHUNK_BLOCKS)
    scratch = [
        pltpu.VMEM((chunks * CHUNK_BLOCKS, block_tokens, new_kv.shape[1]), jnp.bfloat16),
        pltpu.SemaphoreType.DMA((chunks,)),
    ]
    return prompt_attention(
        listed_prompt_kernel, (request, live), (queries, new_kv, blocks),
        (None, None, pl.BlockSpec(memory_space=pl.ANY)), [], scratch,
        entries * block_tokens + queries.shape[0], "listed_prompt",
    )[0]


def striped_prompt(lanes, extra, span, pack, target, striped, pick):
    tokens = pack.shape[0]
    devices, held, block_tokens, _ = striped.shape
    team = lanes // 2
    split = striped.reshape(devices // team, team, held, block_tokens, LANES)
    width = pack.shape[1] - team * HD
    rows = 2 * width // team // HD * tokens
    shapes = [(tokens, 2 * width), (tokens, extra * LANES)] if pick else [(tokens, width)]
    wide_target = jnp.broadcast_to(target, (tokens, extra * LANES))
    vmem = pl.BlockSpec(memory_space=pltpu.VMEM)
    return pl.pallas_call(
        striped_prompt_kernel,
        out_shape=tuple(jax.ShapeDtypeStruct(shape, jnp.bfloat16) for shape in shapes),
        in_specs=[pl.BlockSpec(memory_space=pltpu.SMEM), vmem, vmem, vmem],
        out_specs=(pl.BlockSpec(memory_space=pl.ANY), vmem) if pick else (vmem,),
        scratch_shapes=[
            pltpu.VMEM((rows, HD), jnp.bfloat16),
            pltpu.VMEM((rows, 2 * HD), jnp.float32),
            pltpu.VMEM((rows, HD), jnp.float32),
        ]
        + [pltpu.VMEM((tokens, width), jnp.bfloat16), pltpu.SemaphoreType.DMA] * pick,
        compiler_params=pltpu.CompilerParams(vmem_limit_bytes=SMALL_VMEM_BYTES),
        cost_estimate=pl.CostEstimate(
            flops=4 * tokens * held * block_tokens * width,
            bytes_accessed=4 * tokens * width + 2 * held * block_tokens * team * HD,
            transcendentals=tokens * width // HD * held * block_tokens,
        ),
        name="striped_prompt_pick" if pick else "striped_prompt",
    )(span, pack, wide_target, split)


def stripe_kernel(lanes, steps, cache_ref, *refs):
    out_refs, held_ref, in_sems, out_sems = refs[:-3], refs[-3], refs[-2], refs[-1]
    member = lax.axis_index("seq") % lanes
    team = lanes // 2
    chunks = in_sems.shape[0]
    half = cache_ref.shape[0]
    size = half // chunks
    taken, given = [], []
    for chunk in range(chunks):
        part = pl.ds(chunk * size, size)
        taken.append(pltpu.make_async_copy(cache_ref.at[part], held_ref.at[part], in_sems.at[chunk]))
        taken[-1].start()
    for chunk in range(chunks):
        part = pl.ds(chunk * size, size)
        taken[chunk].wait()
        for place, step in enumerate(steps):
            lane = member ^ step
            parity, column = lane // team, lane % team // 2 * KVH + lane % 2
            for core in range(2):
                start = pl.multiple_of((column + 2 * core) * LANES, LANES)
                given.append(
                    pltpu.make_async_copy(
                        held_ref.at[part, parity, :, pl.ds(start, LANES)],
                        out_refs[place].at[pl.ds(core * half + chunk * size, size)],
                        out_sems.at[chunk, 2 * place + core],
                    )
                )
                given[-1].start()
    for copy in given:
        copy.wait()


def stripe(lanes, steps, kv_cache):
    blocks, block_tokens, width = kv_cache.shape
    chunks = 4
    kv_cache = kv_cache.reshape(blocks // 2, 2, block_tokens, width)
    piece = jax.ShapeDtypeStruct((blocks, block_tokens, LANES), jnp.bfloat16)
    return pl.pallas_call(
        functools.partial(stripe_kernel, lanes, steps),
        out_shape=(piece,) * len(steps),
        in_specs=[pl.BlockSpec(memory_space=pl.ANY)],
        out_specs=(pl.BlockSpec(memory_space=pl.ANY),) * len(steps),
        scratch_shapes=[
            pltpu.VMEM(kv_cache.shape, jnp.bfloat16),
            pltpu.SemaphoreType.DMA((chunks,)),
            pltpu.SemaphoreType.DMA((chunks, 2 * len(steps))),
        ],
        compiler_params=pltpu.CompilerParams(vmem_limit_bytes=VMEM_BYTES),
        name="stripe",
    )(kv_cache)


def gather_kernel(lanes, steps, entries, notes_ref, attended_ref, *refs):
    piece_refs = refs[:lanes]
    out_ref, ready_ref, held_ref, narrow_ref, wide_ref, index_ref, scalar_ref, sems, out_sems = refs[lanes:]
    blocks = piece_refs[0].shape[0]
    readers, extra = attended_ref.shape[0], attended_ref.shape[1]
    room = out_ref.shape[1] - extra
    half = blocks // 2
    capacity = notes_ref.shape[0] // readers
    column = pl.ds(notes_ref.shape[1] - LANES, LANES)
    noted = pltpu.make_async_copy(notes_ref.at[:, column], narrow_ref, sems.at[lanes + 1])
    noted.start()
    copies = [
        pltpu.make_async_copy(piece_ref, held_ref.at[pl.ds(step * blocks, blocks)], sems.at[step])
        for step, piece_ref in zip(steps, piece_refs)
    ]
    for copy in copies:
        copy.start()

    noted.wait()
    wide_ref[: narrow_ref.shape[0], :] = narrow_ref[...].astype(jnp.float32)
    local = wide_ref[pl.ds(0, readers, capacity), :]
    member = wide_ref[pl.ds(1, readers, capacity), :]
    lane = iota((readers, LANES), 1)
    listed = (local >= 0.0) & (lane < entries)
    step = member.astype(jnp.int32) ^ (lax.axis_index("seq") % lanes)
    amount = jnp.sum(listed.astype(jnp.float32), axis=1, keepdims=True).astype(jnp.int32)
    index = jnp.where(listed, step * blocks + local.astype(jnp.int32), 0)
    ready_ref[...] = jnp.zeros_like(ready_ref)
    index_ref[...] = jnp.where(lane == entries, amount, index)
    to_scalars = pltpu.make_async_copy(index_ref, scalar_ref, sems.at[lanes])
    to_scalars.start()
    to_scalars.wait()
    for copy in copies:
        copy.wait()

    def some_of(reader, chip, base):
        def some(group, inner):
            first = group * ROOM_STEP
            spots = [scalar_ref[reader, first + i] for i in range(ROOM_STEP)]
            places = [jnp.minimum(base + first + i, room) for i in range(ROOM_STEP)]
            for core in range(2):
                tiles = [held_ref[spot + core * half] for spot in spots]
                for place, tile in zip(places, tiles):
                    ready_ref[2 * chip + core, place] = tile
            return inner

        return some

    def give(reader):
        return pltpu.make_async_copy(ready_ref.at[reader], out_ref.at[reader], out_sems.at[reader])

    def turn(chip, carry):
        base = 0
        for part in range(2):
            amount = scalar_ref[2 * chip + part, entries]
            some = some_of(2 * chip + part, chip, base)
            lax.fori_loop(0, (amount + (ROOM_STEP - 1)) // ROOM_STEP, some, 0)
            base = amount
        for core in range(2):
            reader = 2 * chip + core
            ready_ref[reader, room:] = attended_ref[reader]
            give(reader).start()
        return carry

    lax.fori_loop(0, readers // 2, turn, 0)
    for reader in range(readers):
        give(reader).wait()


def gather_stripes(lanes, steps, room, entries, arrived, attended, pieces):
    blocks, block_tokens, _ = pieces[0].shape
    slots = arrived.shape[0]
    readers, extra = attended.shape[:2]
    shape = (readers, room + extra, block_tokens, LANES)
    return pl.pallas_call(
        functools.partial(gather_kernel, lanes, steps, entries),
        out_shape=pltpu.HBM(shape, jnp.bfloat16),
        in_specs=[pl.BlockSpec(memory_space=pl.ANY), pl.BlockSpec(memory_space=pltpu.VMEM)]
        + [pl.BlockSpec(memory_space=pl.ANY)] * lanes,
        out_specs=pl.BlockSpec(memory_space=pl.ANY),
        scratch_shapes=[
            pltpu.VMEM(shape, jnp.bfloat16),
            pltpu.VMEM((lanes * blocks, block_tokens, LANES), jnp.bfloat16),
            pltpu.VMEM((slots, LANES), jnp.bfloat16),
            pltpu.VMEM((slots + 64, LANES), jnp.float32),
            pltpu.VMEM((readers, LANES), jnp.int32),
            pltpu.SMEM((readers, LANES), jnp.int32),
            pltpu.SemaphoreType.DMA((lanes + 2,)),
            pltpu.SemaphoreType.DMA((readers,)),
        ],
        compiler_params=pltpu.CompilerParams(vmem_limit_bytes=SMALL_VMEM_BYTES),
        cost_estimate=pl.CostEstimate(
            flops=0, bytes_accessed=4 * readers * room * block_tokens * LANES, transcendentals=0
        ),
        name="gather_stripes",
    )(arrived, attended, *pieces)


def vision_kernel(
    entries, rooms, rows_ref, w_hbm_ref, out_ref, own_ref, other_ref, choice_ref, w_ref, qkv_ref, blend_ref, wide_ref, sems
):
    slots, vit = rows_ref.shape[0], w_ref.shape[0]
    inner = VHEADS * VHD
    copies = []
    for third in range(3):
        part = pl.ds(third * inner, inner)
        copies.append(pltpu.make_async_copy(w_hbm_ref.at[:, part], w_ref.at[:, part], sems.at[third]))
        copies[-1].start()
    notes = rows_ref[:, vit:].astype(jnp.float32)
    wide_ref[:slots, :] = notes
    device = lax.axis_index("seq")
    capacity = slots // out_ref.shape[0]
    first_row = (device - device % 2) * capacity + 2
    amounts = [wide_ref[pl.ds(first_row + i * capacity, 1), :].astype(jnp.int32) for i in range(2)]
    second = device % 2 > 0
    nothing = jnp.zeros_like(amounts[0])
    own_ref[...] = jnp.concatenate(
        [jnp.where(second, amounts[1], amounts[0]), jnp.where(second, amounts[0], nothing)], axis=0
    )
    other_ref[...] = jnp.concatenate(
        [jnp.where(second, amounts[0], amounts[1]), jnp.where(second, nothing, amounts[0])], axis=0
    )
    chips = out_ref.shape[0] // 2
    pooled = wide_ref[pl.ds(2, chips, 2 * capacity), :] + wide_ref[pl.ds(2 + capacity, chips, 2 * capacity), :]
    needed = jnp.max(jnp.where(iota((chips, LANES), 1) < entries, pooled, 0.0)).astype(jnp.int32)
    choice = 0
    for room in rooms:
        choice = choice + jnp.where(needed > room, 1, 0)
    choice_ref[0, 0] = choice
    window_column = jnp.sum(
        jnp.where(iota((slots, LANES), 1) == entries, notes, 0.0), axis=1, keepdims=True
    ).astype(jnp.int32)
    window_row = as_row(window_column)
    itself = iota((slots, slots), 0) == iota((slots, slots), 1)
    allowed = ((window_column == window_row) & (window_row >= 0)) | itself
    blend_ref[...] = jnp.zeros_like(blend_ref)
    for third, copy in enumerate(copies):
        part = slice(third * inner, (third + 1) * inner)
        copy.wait()
        qkv_ref[:, part] = jnp.dot(
            rows_ref[:, :vit], w_ref[:, part], preferred_element_type=jnp.float32
        ).astype(jnp.bfloat16)
    for head in range(VHEADS):
        first, last = head * VHD, (head + 1) * VHD
        low, high = first // LANES * LANES, -(-last // LANES) * LANES
        column = low + iota((slots, high - low), 1)
        mine = (column >= first) & (column < last)
        part = lambda offset: qkv_ref[:, offset + low : offset + high]
        keys = jnp.where(mine, part(inner).astype(jnp.float32), 0.0).astype(jnp.bfloat16)
        values = jnp.where(mine, part(2 * inner).astype(jnp.float32), 0.0).astype(jnp.bfloat16)
        scores = lax.dot_general(
            part(0), keys, (((1,), (1,)), ((), ())), preferred_element_type=jnp.float32
        ) * VHD ** (-0.5)
        scores = jnp.where(allowed, scores, HIDDEN)
        weights = jnp.exp(scores - jnp.max(scores, axis=1, keepdims=True))
        total = jnp.sum(weights, axis=1, keepdims=True)
        blended = jnp.dot(weights.astype(jnp.bfloat16), values, preferred_element_type=jnp.float32)
        blend_ref[:, low:high] += blended / total
    devices, tiles, rows, _ = out_ref.shape
    for tile in range(tiles):
        part = blend_ref[:, tile * LANES : (tile + 1) * LANES].astype(jnp.bfloat16)
        out_ref[:, tile] = part.reshape(devices, rows, LANES)


def vision_tiles(devices, entries, rooms, arrived, w_qkv):
    slots = arrived.shape[0]
    vit, width = w_qkv.shape
    inner = VHEADS * VHD
    return pl.pallas_call(
        functools.partial(vision_kernel, entries, rooms),
        out_shape=(
            jax.ShapeDtypeStruct((devices, inner // LANES, slots // devices, LANES), jnp.bfloat16),
            jax.ShapeDtypeStruct((2, LANES), jnp.int32),
            jax.ShapeDtypeStruct((2, LANES), jnp.int32),
            jax.ShapeDtypeStruct((1, 1), jnp.int32),
        ),
        in_specs=[pl.BlockSpec(memory_space=pltpu.VMEM), pl.BlockSpec(memory_space=pl.ANY)],
        out_specs=(pl.BlockSpec(memory_space=pltpu.VMEM),) * 3 + (pl.BlockSpec(memory_space=pltpu.SMEM),),
        scratch_shapes=[
            pltpu.VMEM((vit, width), jnp.bfloat16),
            pltpu.VMEM((slots, width), jnp.bfloat16),
            pltpu.VMEM((slots, inner), jnp.float32),
            pltpu.VMEM((slots + 64, LANES), jnp.float32),
            pltpu.SemaphoreType.DMA((3,)),
        ],
        compiler_params=pltpu.CompilerParams(vmem_limit_bytes=VMEM_BYTES),
        cost_estimate=pl.CostEstimate(
            flops=2 * slots * vit * width + 4 * slots * slots * inner,
            bytes_accessed=2 * vit * width,
            transcendentals=VHEADS * slots * slots,
        ),
        name="vision_tiles",
    )(arrived, w_qkv)


def pick_kernel(target_ref, *refs):
    out_ref = refs[-1]
    returned = jnp.concatenate([ref[...] for ref in refs[:-1]], axis=0)
    rows, slots = target_ref.shape[0], returned.shape[0]
    picked = (target_ref[...] == iota((rows, slots), 1)).astype(jnp.bfloat16)
    out_ref[...] = jnp.dot(picked, returned, preferred_element_type=jnp.float32).astype(jnp.bfloat16)


def pick_rows(target, *returned):
    return pl.pallas_call(
        pick_kernel,
        out_shape=jax.ShapeDtypeStruct((target.shape[0], returned[0].shape[1]), jnp.bfloat16),
        compiler_params=pltpu.CompilerParams(vmem_limit_bytes=VMEM_BYTES),
        name="pick_rows",
    )(target, *returned)


def window_attention(qkv_rows, windows):
    total_rows = qkv_rows.shape[0]
    inner_width = VHEADS * VHD
    query_heads = qkv_rows[:, :inner_width].reshape(total_rows, VHEADS, VHD)
    key_heads = qkv_rows[:, inner_width : 2 * inner_width].reshape(total_rows, VHEADS, VHD)
    value_heads = qkv_rows[:, 2 * inner_width :].reshape(total_rows, VHEADS, VHD)
    is_live = windows >= 0
    every_row = jnp.arange(total_rows)
    scores = jnp.einsum(
        "qhd,khd->hqk", query_heads, key_heads, preferred_element_type=jnp.float32
    ) * VHD ** (-0.5)
    allowed = (windows[:, None] == windows[None, :]) & is_live[None, :] | (
        every_row[:, None] == every_row[None, :]
    )
    scores = jnp.where(allowed[None], scores, -jnp.inf)
    highest = jnp.max(scores, axis=2, keepdims=True)
    weights = jnp.exp(scores - highest)
    totals = jnp.sum(weights, axis=2)
    blended = jnp.einsum(
        "hqk,khd->qhd",
        weights.astype(jnp.bfloat16),
        value_heads,
        preferred_element_type=jnp.float32,
    )
    pieces = (blended / totals.T[:, :, None]).reshape(total_rows, inner_width)
    return pieces.astype(jnp.bfloat16)


def exchange(rows, devices):
    parts = rows.reshape((devices, rows.shape[0] // devices) + rows.shape[1:])
    return lax.all_to_all(parts, "seq", split_axis=0, concat_axis=0, tiled=True).reshape(rows.shape)


def core_index():
    return lax.axis_index("seq") % 2


def head_half(queries, new_kv, core):
    width, kv_width = queries.shape[1] // 2, new_kv.shape[1] // 4
    part = lambda array, start, size: lax.dynamic_slice_in_dim(array, start, size, 1)
    return jnp.concatenate(
        [
            part(queries, core * width, width),
            part(new_kv, core * kv_width, kv_width),
            part(new_kv, 2 * kv_width + core * kv_width, kv_width),
        ],
        axis=1,
    )


def swap(piece, step, devices):
    return lax.ppermute(piece, "seq", [(i, i ^ step) for i in range(devices)])


def vision_rows(arrived, windows, w_qkv):
    vit = w_qkv.shape[0]
    qkv_rows = jnp.dot(arrived[:, :vit], w_qkv, preferred_element_type=jnp.float32).astype(jnp.bfloat16)
    return window_attention(qkv_rows, windows)


def shards(
    patches,
    row_owner,
    window_slot,
    w_patch,
    vit_gain,
    w_qkv,
    queries,
    new_kv,
    kv_cache,
    block_table,
):
    devices = lax.axis_size("seq")
    vit = w_patch.shape[1]
    capacity = 2 * patches.shape[0] // devices
    slots = devices * capacity
    entries = block_table.shape[1]
    per_owner = 2 * entries // devices
    blocks_dev = kv_cache.shape[0]
    lanes = kv_cache.shape[2] // LANES
    striped = devices == 2 * lanes and lanes == len(STEPS) and capacity == kv_cache.shape[1] and entries + 2 <= LANES
    if striped:
        steps = STEPS
        pieces = stripe(lanes, steps, kv_cache)
        pieces = [swap(piece, step, devices) if step else piece for step, piece in zip(steps, pieces)]
    payload, target, request, live = embed_and_route(
        patches, w_patch, vit_gain, row_owner, window_slot, block_table,
        capacity, slots, per_owner, blocks_dev, lanes if striped else None,
    )
    arrived = exchange(payload, devices)

    if not striped:
        notes = arrived[:, vit : vit + 2].astype(jnp.int32)
        asked = notes[:, 1].reshape(devices, capacity)[:, :per_owner].reshape(devices * per_owner)
        delivered = exchange(kv_cache[jnp.maximum(asked, 0)], devices)
        attended = vision_rows(arrived, notes[:, 0], w_qkv)
        delivered, attended = lax.optimization_barrier((delivered, attended))
        returned = exchange(attended, devices)
        attention_out = listed_prompt(request, live, queries, new_kv, delivered)
        return (pick_rows(target, returned), attention_out)

    rooms = [room for room in ROOMS if room < 2 * entries] + [2 * entries]
    attended, own_span, other_span, choice = vision_tiles(devices, entries, rooms[:-1], arrived, w_qkv)

    def finish(room):
        def run(arrived, attended, target, own_span, other_span, queries, new_kv, *pieces):
            outgoing = gather_stripes(lanes, steps, room, entries, arrived, attended, pieces)
            delivered = exchange(outgoing.reshape((-1,) + outgoing.shape[2:]), devices).reshape(outgoing.shape)
            extra = attended.shape[1]
            own_pack, other_pack = [head_half(queries, new_kv, core) for core in (core_index(), 1 - core_index())]
            other_pack = swap(other_pack, 1, devices)
            (other_out,) = striped_prompt(lanes, extra, other_span, other_pack, target, delivered, False)
            back = swap(other_out, 1, devices)
            own_out, vision_out = striped_prompt(lanes, extra, own_span, own_pack, target, delivered, True)
            return (vision_out, put_half(own_out, back))

        return run

    return lax.switch(
        choice[0, 0], [finish(room) for room in rooms],
        arrived, attended, target, own_span, other_span, queries, new_kv, *pieces,
    )


def solution(mesh):
    in_specs = (
        P(("groups", "seq"), None),
        P(("groups", "seq"), None),
        P(("groups", "seq")),
        P(),
        P(),
        P(),
        P(("groups", "seq"), None),
        P(("groups", "seq"), None),
        P(("groups", "seq"), None, None),
        P(("groups", "seq"), None),
    )
    out_specs = (P(("groups", "seq"), None), P(("groups", "seq"), None))
    return jax.shard_map(shards, mesh=mesh, in_specs=in_specs, out_specs=out_specs, check_vma=False)
```
